32 devices in a mesh: gx: 4 (over x, core), gy: 2 (over y), gz: 4 (over z).
Axes of the slice: x: 2, y: 2, z: 4, core: 2. Of those that a mesh axis runs over, the one named last changes fastest.
Arguments:
- positions: float32 [3, 4, 2, 8, 256], P(None, 'gx', 'gy', 'gz'), may hold values from 0 to 1
- velocities: float32 [3, 4, 2, 8, 256], P(None, 'gx', 'gy', 'gz'), may hold values from -2 to 2
- mass: float32 [4, 2, 8, 256], P('gx', 'gy', 'gz'), may hold values from 0.03 to 0.3
- counts: int32 [4, 2, 8], P('gx', 'gy', 'gz'), may hold values from 1 to 256, as said below
Outputs:
- new_positions: float32 [3, 4, 2, 8, 256], P(None, 'gx', 'gy', 'gz')
- new_velocities: float32 [3, 4, 2, 8, 256], P(None, 'gx', 'gy', 'gz')
The draws below stay inside these ranges and needn't reach their ends.
Inputs may be any that keep to these rules, and one draw needn't show every extreme that they name: `counts`: particles of a bin fill its first slots; every bin holds at least 128 particles, and some bin holds exactly 256 particles in every draw.
All inputs are finite; a program needn't handle non-finite values.
Results may differ from the reference program's by a relative error of at most 0.0001.
Values sent between devices are 32-bit elements; how exact they have to be, the bound alone decides.
No kernel may reach another device: no remote copies, remote signals or barrier semaphores. Data moves between devices by JAX's collectives and lax.ppermute only.
A program may use at most 64 MiB of HBM per device.

```python
import math
import jax
import jax.numpy as jnp
from jax import lax

CAP = 256
SUBCYCLES = 2
NBX = 4
NBY = 2
NBZ = 8


def draw_counts(key, part):
    first_key, second_key, third_key = jax.random.split(key, 3)
    shape = (NBX, NBY, NBZ)
    first = jax.random.randint(first_key, shape, 0, CAP)
    second = jax.random.randint(second_key, shape, 0, CAP)
    filled = CAP // 2 + first * second // (2 * CAP)
    chosen = jax.random.randint(third_key, (), 0, NBX * NBY * NBZ)
    flat_index = lax.broadcasted_iota(jnp.int32, (NBX * NBY * NBZ,), 0).reshape(shape)
    return jnp.where(flat_index == chosen, CAP, filled).astype(jnp.int32)


def shard_levels(rng, extent, pieces, smallest, top_value):
    def one(position, parts):
        steps = jax.random.uniform(jax.random.fold_in(jax.random.fold_in(rng, 6), position), (parts,), jnp.float32, smallest / len(pieces), top_value / len(pieces))
        return jnp.repeat(jnp.exp(steps), extent[position] // parts).reshape((-1,) + (1,) * (len(extent) - position - 1))

    factor_of = one(*pieces[0])
    for cut in pieces[1:]:
        factor_of = factor_of * one(*cut)
    return factor_of


def centred(rng, dims, scale, most, shards=(), kind=jnp.bfloat16):
    level = shard_levels(rng, dims, shards, -0.22, 0.18) if shards else 1.0
    entries = jax.random.normal(rng, dims, jnp.float32) * scale * level
    return jnp.minimum(jnp.maximum(entries, -most), most).astype(kind)


def setup_inputs(seed: int = 0) -> dict:
    seeds = jax.random.split(jax.random.key(seed), 5)
    positions = jnp.clip(1.0 * jax.random.uniform(seeds[0], (3, NBX, NBY, NBZ, CAP), jnp.float32) ** shard_levels(seeds[0], (3, NBX, NBY, NBZ, CAP), ((1, 4), (2, 2), (3, 4)), -0.2, 0.2), 0.0, 1.0)
    velocities = centred(seeds[1], (3, NBX, NBY, NBZ, CAP), 0.3, 2.0, ((1, 4), (2, 2), (3, 4)), jnp.float32)
    mass = jnp.clip(jnp.exp(math.log(0.3) - 2.3025852 * jax.random.uniform(seeds[2], (NBX, NBY, NBZ, CAP), jnp.float32) ** shard_levels(seeds[2], (NBX, NBY, NBZ, CAP), ((0, 4), (1, 2), (2, 4)), -0.2, 0.2)), 0.03, 0.3)
    counts = draw_counts(jax.random.fold_in(seeds[4], 71), 0)
    return dict(positions=positions, velocities=velocities, mass=mass, counts=counts)


time_step = 0.25


def pair_forces(target, source, source_mass, offset):
    target_rows = jnp.moveaxis(target.reshape(3, -1, NBZ, CAP), 1, 0)
    source_rows = jnp.moveaxis(source.reshape(3, -1, NBZ, CAP), 1, 0)
    mass_rows = source_mass.reshape(-1, NBZ, CAP)

    def one_row(items):
        target_row, source_row, mass_row = items
        delta = offset[:, None, None, None] + source_row[:, :, None, :] - target_row[:, :, :, None]
        squared = jnp.sum(delta * delta, axis=0)
        falloff = jnp.maximum(1.0 - squared, 0.0)
        weighted = falloff * falloff * falloff * mass_row[:, None, :]
        return jnp.sum(delta * weighted[None], axis=-1)

    result = lax.map(one_row, (target_rows, source_rows, mass_rows))
    return jnp.moveaxis(result, 0, 1).reshape(target.shape)


def reference(positions, velocities, mass, counts):
    occupied = lax.broadcasted_iota(jnp.int32, mass.shape, 3) < counts[..., None]
    weight = jnp.where(occupied, mass, jnp.zeros_like(mass))
    place = positions
    speed = velocities
    for subcycle in range(SUBCYCLES):
        accel = jnp.zeros_like(place)
        for shift_x in (-1, 0, 1):
            for shift_y in (-1, 0, 1):
                for shift_z in (-1, 0, 1):
                    source = jnp.roll(place, (-shift_x, -shift_y, -shift_z), (1, 2, 3))
                    source_mass = jnp.roll(weight, (-shift_x, -shift_y, -shift_z), (0, 1, 2))
                    offset = jnp.array([shift_x, shift_y, shift_z], jnp.float32)
                    accel = accel + pair_forces(place, source, source_mass, offset)
        speed = speed + time_step * accel
        place = jnp.clip(place + time_step * speed, 0.0, 1.0)
    new_positions = jnp.where(occupied[None], place, jnp.zeros_like(place))
    new_velocities = jnp.where(occupied[None], speed, jnp.zeros_like(speed))
    return new_positions, new_velocities
```

```python
import functools

import jax
import jax.numpy as jnp
from jax import lax
from jax.experimental import pallas as pl
from jax.experimental.pallas import tpu as pltpu
from jax.sharding import PartitionSpec as P

SUBCYCLES = 2

time_step = 0.25

CENTRE = (0.5, 0.5, 1.0)
F32, BF16 = jnp.float32, jnp.bfloat16


def parts(value):
    high = value.astype(BF16).astype(F32)
    rest = value - high
    mid = rest.astype(BF16).astype(F32)
    return high, mid, rest - mid


def row_index(rows, slots):
    return lax.broadcasted_iota(jnp.int32, (rows, slots), 0)


def shifted(packed, offset):
    row = row_index(*packed.shape)
    move = jnp.where(row == 0, offset[0], jnp.where(row == 1, offset[1], jnp.where(row == 2, offset[2], 0.0)))
    return packed + move.astype(F32)


def source_rows(packed, offset):
    slots = packed.shape[-1]
    moved = shifted(packed, offset)
    row = row_index(4, slots)
    square = jnp.sum(jnp.where(row < 3, moved * moved, 0.0), axis=0, keepdims=True)
    head = jnp.where(row < 3, moved, square)
    tail = jnp.where(row == 0, 1.0, 0.0).astype(F32)
    high, mid, low = parts(jnp.concatenate([head, tail], axis=0))
    distance = jnp.concatenate([high, high, high, mid, mid, low], axis=0).astype(BF16)
    mass = moved[3:4]
    carried = jnp.where(row < 3, moved * mass, mass)
    high, mid, low = parts(jnp.concatenate([carried, jnp.zeros_like(carried)], axis=0))
    summed = jnp.concatenate([high, mid, low, jnp.zeros_like(low)], axis=0).astype(BF16)
    return distance, summed


def target_rows(moved):
    slots = moved.shape[-1]
    row = row_index(4, slots)
    square = jnp.sum(jnp.where(row < 3, moved * moved, 0.0), axis=0, keepdims=True)
    head = jnp.where(row < 3, 2.0 * moved, -1.0)
    tail = jnp.where(row == 0, 1.0 - square, 0.0)
    high, mid, low = parts(jnp.concatenate([head, tail], axis=0))
    return jnp.concatenate([high, mid, low, high, mid, high], axis=0).T.astype(BF16)


def pair_weight(target, source):
    near = jnp.maximum(jnp.dot(target, source, preferred_element_type=F32), 0.0)
    weight = near * near * near
    high = weight.astype(BF16)
    return high, (weight - high.astype(F32)).astype(BF16)


def contract(weights, rows):
    return lax.dot_general(rows, weights, (((1,), (1,)), ((), ())), preferred_element_type=F32)


def occupied(counts_ref, z, shape):
    return lax.broadcasted_iota(jnp.int32, shape, 1) < counts_ref[0, 0, z]


def pack_kernel(counts_ref, place_ref, mass_ref, packed_ref):
    for z in range(2):
        mass = mass_ref[0, 0, z : z + 1, :]
        weight = jnp.where(occupied(counts_ref, z, mass.shape), mass, 0.0)
        rows = [place_ref[c, 0, 0, z : z + 1, :] for c in range(3)]
        packed_ref[z] = jnp.concatenate(rows + [weight], axis=0)


def step_kernel(layout, first, last, counts_ref, speed_ref, *refs):
    sources = refs[: len(layout)]
    if last:
        place_out, speed_out = refs[len(layout) : len(layout) + 2]
    else:
        packed_out, speed_out = refs[len(layout) : len(layout) + 2]
    near_ref, sum_ref = refs[len(layout) + 2 :]
    own = [sources[0][z] for z in range(2)]
    for ref, entries in zip(sources, layout):
        for index, column, level, offset in entries:
            distance, summed = source_rows(ref[index], offset)
            near_ref[column, level] = distance
            sum_ref[column, level] = summed
    moved = [shifted(own[z], (-CENTRE[0], -CENTRE[1], z - CENTRE[2])) for z in range(2)]
    targets = [target_rows(m) for m in moved]
    slots = own[0].shape[-1]

    def column_step(column, totals):
        out = []
        for z in range(2):
            total = totals[z]
            for level in range(z, z + 3):
                high, low = pair_weight(targets[z], near_ref[column, level])
                rows = sum_ref[column, level]
                total = total + contract(high, rows) + contract(low, rows)
            out.append(total)
        return tuple(out)

    zero = jnp.zeros((32, slots), F32)
    totals = lax.fori_loop(0, near_ref.shape[0], column_step, (zero, zero))
    for z in range(2):
        total = totals[z][0:8] + totals[z][8:16] + totals[z][16:24]
        total = total[0:4]
        accel = total - moved[z] * total[3:4]
        if first:
            speed = jnp.concatenate([speed_ref[c, 0, 0, z : z + 1, :] for c in range(3)] + [jnp.zeros((1, slots), F32)], axis=0)
        else:
            speed = speed_ref[z]
        speed = speed + time_step * accel
        place = jnp.clip(own[z] + time_step * speed, 0.0, 1.0)
        if last:
            keep = occupied(counts_ref, z, (1, slots))
            for c in range(3):
                place_out[c, 0, 0, z : z + 1, :] = jnp.where(keep, place[c : c + 1], 0.0)
                speed_out[c, 0, 0, z : z + 1, :] = jnp.where(keep, speed[c : c + 1], 0.0)
        else:
            row = row_index(4, slots)
            packed_out[z] = jnp.where(row < 3, place, own[z])
            speed_out[z] = speed


VMEM = pl.BlockSpec(memory_space=pltpu.VMEM)
SMEM = pl.BlockSpec(memory_space=pltpu.SMEM)


def ring(axis, step):
    size = lax.axis_size(axis)
    return [(i, (i + step) % size) for i in range(size)]


def neighbours(value, axis):
    before = lax.ppermute(value, axis, ring(axis, 1))
    if lax.axis_size(axis) == 2:
        return before, before
    return before, lax.ppermute(value, axis, ring(axis, -1))


def shell(packed):
    small = lax.axis_size("gy") == 2
    before, after = neighbours(packed, "gy")
    plane = jnp.concatenate([packed, before] if small else [packed, before, after], axis=0)
    y_shift = [[0], [-1, 1]] if small else [[0], [-1], [1]]
    left, right = neighbours(plane, "gx")
    slab = [(plane, 0), (left, -1), (right, 1)]
    pairs = plane.shape[0] // 2
    edges = []
    for z in range(2):
        edges.append(
            jnp.concatenate([part.reshape(pairs, 2, 4, -1)[:, z] for part, _ in slab], axis=0)
        )
    below = lax.ppermute(edges[1], "gz", ring("gz", 1))
    above = lax.ppermute(edges[0], "gz", ring("gz", -1))
    arrays, layout = [], []
    for part, x in slab:
        entries = []
        for pair in range(pairs):
            for y in y_shift[pair]:
                column = (x + 1) * 3 + y + 1
                for z in range(2):
                    entries.append((pair * 2 + z, column, z + 1, (x - CENTRE[0], y - CENTRE[1], z - CENTRE[2])))
        arrays.append(part)
        layout.append(entries)
    for part, z in ((below, -1), (above, 2)):
        entries = []
        for index, (_, x) in enumerate(slab):
            for pair in range(pairs):
                for y in y_shift[pair]:
                    column = (x + 1) * 3 + y + 1
                    entries.append((index * pairs + pair, column, z + 1, (x - CENTRE[0], y - CENTRE[1], z - CENTRE[2])))
        arrays.append(part)
        layout.append(entries)
    return arrays, layout


def on_device(positions, velocities, mass, counts):
    slots = positions.shape[-1]
    bins = jax.ShapeDtypeStruct((2, 4, slots), F32)
    packed = pl.pallas_call(
        pack_kernel,
        out_shape=bins,
        in_specs=[SMEM, VMEM, VMEM],
        out_specs=VMEM,
    )(counts, positions, mass)
    speed = velocities
    for subcycle in range(SUBCYCLES):
        arrays, layout = shell(packed)
        first, last = subcycle == 0, subcycle == SUBCYCLES - 1
        full = jax.ShapeDtypeStruct(positions.shape, F32)
        packed, speed = pl.pallas_call(
            functools.partial(step_kernel, layout, first, last),
            out_shape=(full, full) if last else (bins, bins),
            in_specs=[SMEM] + [VMEM] * (1 + len(arrays)),
            out_specs=(VMEM, VMEM),
            scratch_shapes=[pltpu.VMEM((9, 4, 48, slots), BF16), pltpu.VMEM((9, 4, 32, slots), BF16)],
            compiler_params=pltpu.CompilerParams(vmem_limit_bytes=32 * 1024 * 1024),
        )(counts, speed, *arrays)
    return packed, speed


def solution(mesh):
    placed = (
        P(None, "gx", "gy", "gz", None),
        P(None, "gx", "gy", "gz", None),
        P("gx", "gy", "gz", None),
        P("gx", "gy", "gz"),
    )
    return jax.shard_map(
        on_device,
        mesh=mesh,
        in_specs=placed,
        out_specs=(P(None, "gx", "gy", "gz", None), P(None, "gx", "gy", "gz", None)),
        check_vma=False,
    )
```

```python
import functools

import jax
import jax.numpy as jnp
from jax import lax
from jax.experimental import pallas as pl
from jax.experimental.pallas import tpu as pltpu
from jax.sharding import PartitionSpec as P

SUBCYCLES = 2

time_step = 0.25

CENTRE = (0.5, 0.5, 1.0)
F32, BF16 = jnp.float32, jnp.bfloat16


def parts(value):
    high = value.astype(BF16).astype(F32)
    rest = value - high
    mid = rest.astype(BF16).astype(F32)
    return high, mid, rest - mid


def row_index(rows, slots):
    return lax.broadcasted_iota(jnp.int32, (rows, slots), 0)


def shifted(packed, offset):
    row = row_index(*packed.shape)
    move = jnp.where(row == 0, offset[0], jnp.where(row == 1, offset[1], jnp.where(row == 2, offset[2], 0.0)))
    return packed + move.astype(F32)


def source_rows(packed, offset):
    slots = packed.shape[-1]
    moved = shifted(packed, offset)
    row = row_index(4, slots)
    square = jnp.sum(jnp.where(row < 3, moved * moved, 0.0), axis=0, keepdims=True)
    head = jnp.where(row < 3, moved, square)
    tail = jnp.where(row == 0, 1.0, 0.0).astype(F32)
    high, mid, low = parts(jnp.concatenate([head, tail], axis=0))
    distance = jnp.concatenate([high, high, high, mid, mid, low], axis=0).astype(BF16)
    mass = moved[3:4]
    carried = jnp.where(row < 3, moved * mass, mass)
    high, mid, low = parts(jnp.concatenate([carried, jnp.zeros_like(carried)], axis=0))
    summed = jnp.concatenate([high, mid, low, jnp.zeros_like(low)], axis=0).astype(BF16)
    return distance, summed


def target_rows(moved):
    slots = moved.shape[-1]
    row = row_index(4, slots)
    square = jnp.sum(jnp.where(row < 3, moved * moved, 0.0), axis=0, keepdims=True)
    head = jnp.where(row < 3, 2.0 * moved, -1.0)
    tail = jnp.where(row == 0, 1.0 - square, 0.0)
    high, mid, low = parts(jnp.concatenate([head, tail], axis=0))
    return jnp.concatenate([high, mid, low, high, mid, high], axis=0).T.astype(BF16)


def pair_weight(target, source):
    near = jnp.maximum(jnp.dot(target, source, preferred_element_type=F32), 0.0)
    weight = near * near * near
    high = weight.astype(BF16)
    return high, (weight - high.astype(F32)).astype(BF16)


def contract(weights, rows):
    return lax.dot_general(rows, weights, (((1,), (1,)), ((), ())), preferred_element_type=F32)


def occupied(counts_ref, z, shape):
    return lax.broadcasted_iota(jnp.int32, shape, 1) < counts_ref[0, 0, z]


def pack_kernel(counts_ref, place_ref, mass_ref, packed_ref):
    for z in range(2):
        mass = mass_ref[0, 0, z : z + 1, :]
        weight = jnp.where(occupied(counts_ref, z, mass.shape), mass, 0.0)
        rows = [place_ref[c, 0, 0, z : z + 1, :] for c in range(3)]
        packed_ref[z] = jnp.concatenate(rows + [weight], axis=0)


def gather_column(size_x, size_y):
    here_x, here_y = lax.axis_index("gx"), lax.axis_index("gy")
    places = []
    for x in (-1, 0, 1):
        for y in (-1, 0, 1):
            place = lax.rem(here_x + (x + size_x), size_x) * size_y + lax.rem(here_y + (y + size_y), size_y)
            places.append((place, x - CENTRE[0], y - CENTRE[1]))
    return places


def fill(refs, levels, sizes, near_ref, sum_ref):
    for column, (place, x, y) in enumerate(gather_column(*sizes)):
        for slot, (ref, level) in enumerate(zip(refs, levels)):
            distance, summed = source_rows(ref[place], (x, y, level - CENTRE[2]))
            near_ref[column, slot] = distance
            sum_ref[column, slot] = summed


def target_places(own_ref):
    own = [own_ref[z] for z in range(2)]
    return own, [shifted(own[z], (-CENTRE[0], -CENTRE[1], z - CENTRE[2])) for z in range(2)]


def totals_over(targets, wanted, near_ref, sum_ref, totals):
    def column_step(column, totals):
        out = []
        for z in range(2):
            total = totals[z]
            for slot in wanted[z]:
                high, low = pair_weight(targets[z], near_ref[column, slot])
                rows = sum_ref[column, slot]
                total = total + contract(high, rows) + contract(low, rows)
            out.append(total)
        return tuple(out)

    return lax.fori_loop(0, near_ref.shape[0], column_step, tuple(totals))


def inner_kernel(sizes, own_ref, low_ref, high_ref, total_ref, near_ref, sum_ref):
    _, moved = target_places(own_ref)
    targets = [target_rows(m) for m in moved]
    fill((low_ref, high_ref), (0, 1), sizes, near_ref, sum_ref)
    zero = jnp.zeros(total_ref.shape[1:], F32)
    totals = totals_over(targets, ((0, 1), (0, 1)), near_ref, sum_ref, (zero, zero))
    for z in range(2):
        total_ref[z] = totals[z]


def outer_kernel(sizes, first, last, counts_ref, speed_ref, own_ref, total_ref, below_ref, above_ref, *refs):
    if last:
        place_out, speed_out, near_ref, sum_ref = refs
    else:
        packed_out, speed_out, near_ref, sum_ref = refs
    own, moved = target_places(own_ref)
    targets = [target_rows(m) for m in moved]
    fill((below_ref, above_ref), (-1, 2), sizes, near_ref, sum_ref)
    totals = totals_over(targets, ((0,), (1,)), near_ref, sum_ref, (total_ref[0], total_ref[1]))
    slots = own[0].shape[-1]
    for z in range(2):
        total = totals[z][0:8] + totals[z][8:16] + totals[z][16:24]
        total = total[0:4]
        accel = total - moved[z] * total[3:4]
        if first:
            speed = jnp.concatenate([speed_ref[c, 0, 0, z : z + 1, :] for c in range(3)] + [jnp.zeros((1, slots), F32)], axis=0)
        else:
            speed = speed_ref[z]
        speed = speed + time_step * accel
        place = jnp.clip(own[z] + time_step * speed, 0.0, 1.0)
        if last:
            keep = occupied(counts_ref, z, (1, slots))
            for c in range(3):
                place_out[c, 0, 0, z : z + 1, :] = jnp.where(keep, place[c : c + 1], 0.0)
                speed_out[c, 0, 0, z : z + 1, :] = jnp.where(keep, speed[c : c + 1], 0.0)
        else:
            row = row_index(4, slots)
            packed_out[z] = jnp.where(row < 3, place, own[z])
            speed_out[z] = speed


VMEM = pl.BlockSpec(memory_space=pltpu.VMEM)
SMEM = pl.BlockSpec(memory_space=pltpu.SMEM)
PARAMS = pltpu.CompilerParams(vmem_limit_bytes=32 * 1024 * 1024)


def ring(axis, step):
    size = lax.axis_size(axis)
    return [(i, (i + step) % size) for i in range(size)]


def cost(pairs, slots):
    return pl.CostEstimate(flops=pairs * slots * slots * 200, bytes_accessed=1 << 18, transcendentals=0)


def on_device(positions, velocities, mass, counts):
    slots = positions.shape[-1]
    sizes = (lax.axis_size("gx"), lax.axis_size("gy"))
    columns = sizes[0] * sizes[1]
    bins = jax.ShapeDtypeStruct((2, 4, slots), F32)
    full = jax.ShapeDtypeStruct(positions.shape, F32)
    packed = pl.pallas_call(
        pack_kernel,
        out_shape=bins,
        in_specs=[SMEM, VMEM, VMEM],
        out_specs=VMEM,
    )(counts, positions, mass)
    speed = velocities
    for subcycle in range(SUBCYCLES):
        first, last = subcycle == 0, subcycle == SUBCYCLES - 1
        copies = jnp.broadcast_to(packed[:, None], (2, columns, 4, slots))
        planes = lax.all_to_all(copies, ("gx", "gy"), 1, 1, tiled=True)
        low, high = planes[0], planes[1]
        below = lax.ppermute(high, "gz", ring("gz", 1))
        above = lax.ppermute(low, "gz", ring("gz", -1))
        total = pl.pallas_call(
            functools.partial(inner_kernel, sizes),
            out_shape=jax.ShapeDtypeStruct((2, 32, slots), F32),
            in_specs=[VMEM] * 3,
            out_specs=VMEM,
            scratch_shapes=[pltpu.VMEM((9, 2, 48, slots), BF16), pltpu.VMEM((9, 2, 32, slots), BF16)],
            compiler_params=PARAMS,
            cost_estimate=cost(36, slots),
        )(packed, low, high)
        packed, speed = pl.pallas_call(
            functools.partial(outer_kernel, sizes, first, last),
            out_shape=(full, full) if last else (bins, bins),
            in_specs=[SMEM] + [VMEM] * 5,
            out_specs=(VMEM, VMEM),
            scratch_shapes=[pltpu.VMEM((9, 2, 48, slots), BF16), pltpu.VMEM((9, 2, 32, slots), BF16)],
            compiler_params=PARAMS,
            cost_estimate=cost(18, slots),
        )(counts, speed, packed, total, below, above)
    return packed, speed


def solution(mesh):
    placed = (
        P(None, "gx", "gy", "gz", None),
        P(None, "gx", "gy", "gz", None),
        P("gx", "gy", "gz", None),
        P("gx", "gy", "gz"),
    )
    return jax.shard_map(
        on_device,
        mesh=mesh,
        in_specs=placed,
        out_specs=(P(None, "gx", "gy", "gz", None), P(None, "gx", "gy", "gz", None)),
        check_vma=False,
    )
```

```python
import functools

import jax
import jax.numpy as jnp
from jax import lax
from jax.experimental import pallas as pl
from jax.experimental.pallas import tpu as pltpu
from jax.sharding import PartitionSpec as P

SUBCYCLES = 2

time_step = 0.25

CENTRE = (0.5, 0.5, 1.0)
F32, BF16 = jnp.float32, jnp.bfloat16


def parts(value):
    high = value.astype(BF16).astype(F32)
    rest = value - high
    mid = rest.astype(BF16).astype(F32)
    return high, mid, rest - mid


def row_index(rows, slots):
    return lax.broadcasted_iota(jnp.int32, (rows, slots), 0)


def shifted(packed, offset):
    row = row_index(*packed.shape)
    move = jnp.where(row == 0, offset[0], jnp.where(row == 1, offset[1], jnp.where(row == 2, offset[2], 0.0)))
    return packed + move.astype(F32)


def source_rows(packed, offset):
    slots = packed.shape[-1]
    moved = shifted(packed, offset)
    row = row_index(4, slots)
    square = jnp.sum(jnp.where(row < 3, moved * moved, 0.0), axis=0, keepdims=True)
    head = jnp.where(row < 3, moved, square)
    tail = jnp.where(row == 0, 1.0, 0.0).astype(F32)
    high, mid, low = parts(jnp.concatenate([head, tail], axis=0))
    distance = jnp.concatenate([high, high, high, mid, mid, low], axis=0).astype(BF16)
    mass = moved[3:4]
    carried = jnp.where(row < 3, moved * mass, mass)
    high, mid, low = parts(jnp.concatenate([carried, jnp.zeros_like(carried)], axis=0))
    summed = jnp.concatenate([high, mid, low, jnp.zeros_like(low)], axis=0).astype(BF16)
    return distance, summed


def target_rows(moved):
    slots = moved.shape[-1]
    row = row_index(4, slots)
    square = jnp.sum(jnp.where(row < 3, moved * moved, 0.0), axis=0, keepdims=True)
    head = jnp.where(row < 3, 2.0 * moved, -1.0)
    tail = jnp.where(row == 0, 1.0 - square, 0.0)
    high, mid, low = parts(jnp.concatenate([head, tail], axis=0))
    return jnp.concatenate([high, mid, low, high, mid, high], axis=0).T.astype(BF16)


def pair_weight(target, source):
    near = jnp.maximum(jnp.dot(target, source, preferred_element_type=F32), 0.0)
    weight = near * near * near
    high = weight.astype(BF16)
    return high, (weight - high.astype(F32)).astype(BF16)


def contract(weights, rows):
    return lax.dot_general(rows, weights, (((1,), (1,)), ((), ())), preferred_element_type=F32)


def occupied(counts_ref, z, shape):
    return lax.broadcasted_iota(jnp.int32, shape, 1) < counts_ref[0, 0, z]


def pack_kernel(counts_ref, place_ref, mass_ref, packed_ref):
    for z in range(2):
        mass = mass_ref[0, 0, z : z + 1, :]
        weight = jnp.where(occupied(counts_ref, z, mass.shape), mass, 0.0)
        rows = [place_ref[c, 0, 0, z : z + 1, :] for c in range(3)]
        packed_ref[z] = jnp.concatenate(rows + [weight], axis=0)


def gather_column(size_x, size_y):
    here_x, here_y = lax.axis_index("gx"), lax.axis_index("gy")
    places = []
    for x in (-1, 0, 1):
        for y in (-1, 0, 1):
            place = lax.rem(here_x + (x + size_x), size_x) * size_y + lax.rem(here_y + (y + size_y), size_y)
            places.append((place, x - CENTRE[0], y - CENTRE[1]))
    return places


def fill(gathered_ref, sizes, near_ref, sum_ref):
    here, size = lax.axis_index("gz"), sizes[2]
    levels = ((lax.rem(here + (size - 1), size), 1), (here, 0), (here, 1), (lax.rem(here + 1, size), 0))
    for column, (place, x, y) in enumerate(gather_column(sizes[0], sizes[1])):
        for slot, (device, z) in enumerate(levels):
            distance, summed = source_rows(gathered_ref[place * size + device, z], (x, y, slot - 1 - CENTRE[2]))
            near_ref[column, slot] = distance
            sum_ref[column, slot] = summed


def target_places(own_ref):
    own = [own_ref[z] for z in range(2)]
    return own, [shifted(own[z], (-CENTRE[0], -CENTRE[1], z - CENTRE[2])) for z in range(2)]


def totals_over(targets, wanted, near_ref, sum_ref, totals):
    def column_step(column, totals):
        out = []
        for z in range(2):
            total = totals[z]
            for slot in wanted[z]:
                high, low = pair_weight(targets[z], near_ref[column, slot])
                rows = sum_ref[column, slot]
                total = total + contract(high, rows) + contract(low, rows)
            out.append(total)
        return tuple(out)

    return lax.fori_loop(0, near_ref.shape[0], column_step, tuple(totals))


def step_kernel(sizes, first, last, counts_ref, speed_ref, own_ref, gathered_ref, *refs):
    if last:
        place_out, speed_out, near_ref, sum_ref = refs
    else:
        packed_out, speed_out, near_ref, sum_ref = refs
    own, moved = target_places(own_ref)
    targets = [target_rows(m) for m in moved]
    fill(gathered_ref, sizes, near_ref, sum_ref)
    slots = own[0].shape[-1]
    zero = jnp.zeros((32, slots), F32)
    totals = totals_over(targets, ((0, 1, 2), (1, 2, 3)), near_ref, sum_ref, (zero, zero))
    for z in range(2):
        total = totals[z][0:8] + totals[z][8:16] + totals[z][16:24]
        total = total[0:4]
        accel = total - moved[z] * total[3:4]
        if first:
            speed = jnp.concatenate([speed_ref[c, 0, 0, z : z + 1, :] for c in range(3)] + [jnp.zeros((1, slots), F32)], axis=0)
        else:
            speed = speed_ref[z]
        speed = speed + time_step * accel
        place = jnp.clip(own[z] + time_step * speed, 0.0, 1.0)
        if last:
            keep = occupied(counts_ref, z, (1, slots))
            for c in range(3):
                place_out[c, 0, 0, z : z + 1, :] = jnp.where(keep, place[c : c + 1], 0.0)
                speed_out[c, 0, 0, z : z + 1, :] = jnp.where(keep, speed[c : c + 1], 0.0)
        else:
            row = row_index(4, slots)
            packed_out[z] = jnp.where(row < 3, place, own[z])
            speed_out[z] = speed


VMEM = pl.BlockSpec(memory_space=pltpu.VMEM)
SMEM = pl.BlockSpec(memory_space=pltpu.SMEM)
PARAMS = pltpu.CompilerParams(vmem_limit_bytes=32 * 1024 * 1024)


def cost(pairs, slots):
    return pl.CostEstimate(flops=pairs * slots * slots * 200, bytes_accessed=1 << 18, transcendentals=0)


def on_device(positions, velocities, mass, counts):
    slots = positions.shape[-1]
    sizes = (lax.axis_size("gx"), lax.axis_size("gy"), lax.axis_size("gz"))
    bins = jax.ShapeDtypeStruct((2, 4, slots), F32)
    full = jax.ShapeDtypeStruct(positions.shape, F32)
    packed = pl.pallas_call(
        pack_kernel,
        out_shape=bins,
        in_specs=[SMEM, VMEM, VMEM],
        out_specs=VMEM,
    )(counts, positions, mass)
    speed = velocities
    for subcycle in range(SUBCYCLES):
        first, last = subcycle == 0, subcycle == SUBCYCLES - 1
        gathered = lax.all_gather(packed, ("gx", "gy", "gz"), tiled=False)
        packed, speed = pl.pallas_call(
            functools.partial(step_kernel, sizes, first, last),
            out_shape=(full, full) if last else (bins, bins),
            in_specs=[SMEM] + [VMEM] * 3,
            out_specs=(VMEM, VMEM),
            scratch_shapes=[pltpu.VMEM((9, 4, 48, slots), BF16), pltpu.VMEM((9, 4, 32, slots), BF16)],
            compiler_params=PARAMS,
            cost_estimate=cost(54, slots),
        )(counts, speed, packed, gathered)
    return packed, speed


def solution(mesh):
    placed = (
        P(None, "gx", "gy", "gz", None),
        P(None, "gx", "gy", "gz", None),
        P("gx", "gy", "gz", None),
        P("gx", "gy", "gz"),
    )
    return jax.shard_map(
        on_device,
        mesh=mesh,
        in_specs=placed,
        out_specs=(P(None, "gx", "gy", "gz", None), P(None, "gx", "gy", "gz", None)),
        check_vma=False,
    )
```

```python
import functools

import jax
import jax.numpy as jnp
from jax import lax
from jax.experimental import pallas as pl
from jax.experimental.pallas import tpu as pltpu
from jax.sharding import PartitionSpec as P

SUBCYCLES = 2

time_step = 0.25

CENTRE = (0.5, 0.5, 1.0)
F32, BF16 = jnp.float32, jnp.bfloat16


def parts(value):
    high = value.astype(BF16).astype(F32)
    rest = value - high
    mid = rest.astype(BF16).astype(F32)
    return high, mid, rest - mid


def row_index(rows, slots):
    return lax.broadcasted_iota(jnp.int32, (rows, slots), 0)


def shifted(packed, offset):
    row = row_index(*packed.shape)
    move = jnp.where(row == 0, offset[0], jnp.where(row == 1, offset[1], jnp.where(row == 2, offset[2], 0.0)))
    return packed + move.astype(F32)


def source_rows(packed, offset):
    slots = packed.shape[-1]
    moved = shifted(packed, offset)
    row = row_index(4, slots)
    square = jnp.sum(jnp.where(row < 3, moved * moved, 0.0), axis=0, keepdims=True)
    head = jnp.where(row < 3, moved, square)
    tail = jnp.where(row == 0, 1.0, 0.0).astype(F32)
    high, mid, low = parts(jnp.concatenate([head, tail], axis=0))
    distance = jnp.concatenate([high, high, high, mid, mid, low], axis=0).astype(BF16)
    mass = moved[3:4]
    carried = jnp.where(row < 3, moved * mass, mass)
    high, mid, low = parts(jnp.concatenate([carried, jnp.zeros_like(carried)], axis=0))
    summed = jnp.concatenate([high, mid, low, jnp.zeros_like(low)], axis=0).astype(BF16)
    return distance, summed


def target_rows(moved):
    slots = moved.shape[-1]
    row = row_index(4, slots)
    square = jnp.sum(jnp.where(row < 3, moved * moved, 0.0), axis=0, keepdims=True)
    head = jnp.where(row < 3, 2.0 * moved, -1.0)
    tail = jnp.where(row == 0, 1.0 - square, 0.0)
    high, mid, low = parts(jnp.concatenate([head, tail], axis=0))
    return jnp.concatenate([high, mid, low, high, mid, high], axis=0).T.astype(BF16)


def pair_weight(target, source):
    near = jnp.maximum(jnp.dot(target, source, preferred_element_type=F32), 0.0)
    weight = near * near * near
    high = weight.astype(BF16)
    return high, (weight - high.astype(F32)).astype(BF16)


def contract(weights, rows):
    return lax.dot_general(weights, rows, (((1,), (1,)), ((), ())), preferred_element_type=F32)


def occupied(counts_ref, z, shape):
    return lax.broadcasted_iota(jnp.int32, shape, 1) < counts_ref[0, 0, z]


def pack_kernel(counts_ref, place_ref, mass_ref, packed_ref):
    for z in range(2):
        mass = mass_ref[0, 0, z : z + 1, :]
        weight = jnp.where(occupied(counts_ref, z, mass.shape), mass, 0.0)
        rows = [place_ref[c, 0, 0, z : z + 1, :] for c in range(3)]
        packed_ref[z] = jnp.concatenate(rows + [weight], axis=0)


def step_kernel(layout, first, last, counts_ref, speed_ref, *refs):
    sources = refs[: len(layout)]
    if last:
        place_out, speed_out = refs[len(layout) : len(layout) + 2]
    else:
        packed_out, speed_out = refs[len(layout) : len(layout) + 2]
    near_ref, sum_ref = refs[len(layout) + 2 :]
    own = [sources[0][z] for z in range(2)]
    for ref, entries in zip(sources, layout):
        for index, column, level, offset in entries:
            distance, summed = source_rows(ref[index], offset)
            near_ref[column, level] = distance
            sum_ref[column, level] = summed
    moved = [shifted(own[z], (-CENTRE[0], -CENTRE[1], z - CENTRE[2])) for z in range(2)]
    targets = [target_rows(m) for m in moved]
    slots = own[0].shape[-1]

    def column_step(column, totals):
        out = []
        for z in range(2):
            highs, lows, rows = [], [], []
            for level in range(z, z + 3):
                high, low = pair_weight(targets[z], near_ref[column, level])
                highs.append(high)
                lows.append(low)
                rows.append(sum_ref[column, level])
            rows = jnp.concatenate(rows, axis=1)
            weights = jnp.concatenate(highs + lows, axis=1)
            out.append(totals[z] + contract(weights, jnp.concatenate([rows, rows], axis=1)))
        return tuple(out)

    zero = jnp.zeros((slots, 32), F32)
    totals = lax.fori_loop(0, near_ref.shape[0], column_step, (zero, zero))
    totals = [total.T for total in totals]
    for z in range(2):
        total = totals[z][0:8] + totals[z][8:16] + totals[z][16:24]
        total = total[0:4]
        accel = total - moved[z] * total[3:4]
        if first:
            speed = jnp.concatenate([speed_ref[c, 0, 0, z : z + 1, :] for c in range(3)] + [jnp.zeros((1, slots), F32)], axis=0)
        else:
            speed = speed_ref[z]
        speed = speed + time_step * accel
        place = jnp.clip(own[z] + time_step * speed, 0.0, 1.0)
        if last:
            keep = occupied(counts_ref, z, (1, slots))
            for c in range(3):
                place_out[c, 0, 0, z : z + 1, :] = jnp.where(keep, place[c : c + 1], 0.0)
                speed_out[c, 0, 0, z : z + 1, :] = jnp.where(keep, speed[c : c + 1], 0.0)
        else:
            row = row_index(4, slots)
            packed_out[z] = jnp.where(row < 3, place, own[z])
            speed_out[z] = speed


VMEM = pl.BlockSpec(memory_space=pltpu.VMEM)
SMEM = pl.BlockSpec(memory_space=pltpu.SMEM)


def ring(axis, step):
    size = lax.axis_size(axis)
    return [(i, (i + step) % size) for i in range(size)]


def neighbours(value, axis):
    before = lax.ppermute(value, axis, ring(axis, 1))
    if lax.axis_size(axis) == 2:
        return before, before
    return before, lax.ppermute(value, axis, ring(axis, -1))


def shell(packed):
    small = lax.axis_size("gy") == 2
    before, after = neighbours(packed, "gy")
    plane = jnp.concatenate([packed, before] if small else [packed, before, after], axis=0)
    y_shift = [[0], [-1, 1]] if small else [[0], [-1], [1]]
    left, right = neighbours(plane, "gx")
    slab = [(plane, 0), (left, -1), (right, 1)]
    pairs = plane.shape[0] // 2
    edges = []
    for z in range(2):
        edges.append(
            jnp.concatenate([part.reshape(pairs, 2, 4, -1)[:, z] for part, _ in slab], axis=0)
        )
    below = lax.ppermute(edges[1], "gz", ring("gz", 1))
    above = lax.ppermute(edges[0], "gz", ring("gz", -1))
    arrays, layout = [], []
    for part, x in slab:
        entries = []
        for pair in range(pairs):
            for y in y_shift[pair]:
                column = (x + 1) * 3 + y + 1
                for z in range(2):
                    entries.append((pair * 2 + z, column, z + 1, (x - CENTRE[0], y - CENTRE[1], z - CENTRE[2])))
        arrays.append(part)
        layout.append(entries)
    for part, z in ((below, -1), (above, 2)):
        entries = []
        for index, (_, x) in enumerate(slab):
            for pair in range(pairs):
                for y in y_shift[pair]:
                    column = (x + 1) * 3 + y + 1
                    entries.append((index * pairs + pair, column, z + 1, (x - CENTRE[0], y - CENTRE[1], z - CENTRE[2])))
        arrays.append(part)
        layout.append(entries)
    return arrays, layout


def on_device(positions, velocities, mass, counts):
    slots = positions.shape[-1]
    bins = jax.ShapeDtypeStruct((2, 4, slots), F32)
    packed = pl.pallas_call(
        pack_kernel,
        out_shape=bins,
        in_specs=[SMEM, VMEM, VMEM],
        out_specs=VMEM,
    )(counts, positions, mass)
    speed = velocities
    for subcycle in range(SUBCYCLES):
        arrays, layout = shell(packed)
        first, last = subcycle == 0, subcycle == SUBCYCLES - 1
        full = jax.ShapeDtypeStruct(positions.shape, F32)
        packed, speed = pl.pallas_call(
            functools.partial(step_kernel, layout, first, last),
            out_shape=(full, full) if last else (bins, bins),
            in_specs=[SMEM] + [VMEM] * (1 + len(arrays)),
            out_specs=(VMEM, VMEM),
            scratch_shapes=[pltpu.VMEM((9, 4, 48, slots), BF16), pltpu.VMEM((9, 4, 32, slots), BF16)],
            compiler_params=pltpu.CompilerParams(vmem_limit_bytes=32 * 1024 * 1024),
        )(counts, speed, *arrays)
    return packed, speed


def solution(mesh):
    placed = (
        P(None, "gx", "gy", "gz", None),
        P(None, "gx", "gy", "gz", None),
        P("gx", "gy", "gz", None),
        P("gx", "gy", "gz"),
    )
    return jax.shard_map(
        on_device,
        mesh=mesh,
        in_specs=placed,
        out_specs=(P(None, "gx", "gy", "gz", None), P(None, "gx", "gy", "gz", None)),
        check_vma=False,
    )
```

```python
import functools

import jax
import jax.numpy as jnp
from jax import lax
from jax.experimental import pallas as pl
from jax.experimental.pallas import tpu as pltpu
from jax.sharding import PartitionSpec as P

SUBCYCLES = 2

time_step = 0.25

CENTRE = (0.5, 0.5, 1.0)
F32, BF16 = jnp.float32, jnp.bfloat16


def parts(value):
    high = value.astype(BF16).astype(F32)
    rest = value - high
    mid = rest.astype(BF16).astype(F32)
    return high, mid, rest - mid


def row_index(rows, slots):
    return lax.broadcasted_iota(jnp.int32, (rows, slots), 0)


def shifted(packed, offset):
    row = row_index(*packed.shape)
    x, y, z = [jnp.asarray(o, F32) - c for o, c in zip(offset, CENTRE)]
    move = jnp.where(row == 0, x, jnp.where(row == 1, y, jnp.where(row == 2, z, 0.0)))
    return packed + move


def source_rows(packed, offset):
    slots = packed.shape[-1]
    moved = shifted(packed, offset)
    row = row_index(4, slots)
    square = jnp.sum(jnp.where(row < 3, moved * moved, 0.0), axis=0, keepdims=True)
    head = jnp.where(row < 3, moved, square)
    tail = jnp.where(row == 0, 1.0, 0.0).astype(F32)
    high, mid, low = parts(jnp.concatenate([head, tail], axis=0))
    distance = jnp.concatenate([high, high, high, mid, mid, low], axis=0).astype(BF16)
    mass = moved[3:4]
    carried = jnp.where(row < 3, moved * mass, mass)
    high, mid, low = parts(jnp.concatenate([carried, jnp.zeros_like(carried)], axis=0))
    summed = jnp.concatenate([high, mid, low, jnp.zeros_like(low)], axis=0).astype(BF16)
    return distance, summed


def target_rows(moved):
    slots = moved.shape[-1]
    row = row_index(4, slots)
    square = jnp.sum(jnp.where(row < 3, moved * moved, 0.0), axis=0, keepdims=True)
    head = jnp.where(row < 3, 2.0 * moved, -1.0)
    tail = jnp.where(row == 0, 1.0 - square, 0.0)
    high, mid, low = parts(jnp.concatenate([head, tail], axis=0))
    return jnp.concatenate([high, mid, low, high, mid, high], axis=0).T.astype(BF16)


def pair_weight(target, source):
    near = jnp.maximum(jnp.dot(target, source, preferred_element_type=F32), 0.0)
    weight = near * near * near
    high = weight.astype(BF16)
    return high, (weight - high.astype(F32)).astype(BF16)


def contract(weights, rows):
    return lax.dot_general(weights, rows, (((1,), (1,)), ((), ())), preferred_element_type=F32)


def occupied(counts_ref, z, shape):
    return lax.broadcasted_iota(jnp.int32, shape, 1) < counts_ref[0, 0, z]


def pack_kernel(counts_ref, place_ref, mass_ref, packed_ref):
    for z in range(2):
        mass = mass_ref[0, 0, z : z + 1, :]
        weight = jnp.where(occupied(counts_ref, z, mass.shape), mass, 0.0)
        rows = [place_ref[c, 0, 0, z : z + 1, :] for c in range(3)]
        packed_ref[z] = jnp.concatenate(rows + [weight], axis=0)


def ahead(axis):
    return 1 - 2 * lax.rem(lax.axis_index(axis), 2)


def y_shifts(size):
    if size == 2:
        return [[0], [-1, 1]]
    return [[0], [ahead("gy")], [-ahead("gy")]]


def fill(near_ref, sum_ref, entries):
    for number, (packed, offset) in enumerate(entries):
        group, member = divmod(number, 3)
        distance, summed = source_rows(packed, offset)
        near_ref[group, member] = distance
        sum_ref[group, member] = summed


def gathered(target, near_ref, sum_ref, group, members):
    highs, lows, rows = [], [], []
    for member in members:
        high, low = pair_weight(target, near_ref[group, member])
        highs.append(high)
        lows.append(low)
        rows.append(sum_ref[group, member])
    rows = jnp.concatenate(rows, axis=1)
    return contract(jnp.concatenate(highs + lows, axis=1), jnp.concatenate([rows, rows], axis=1))


def both_targets(target_ref, near_ref, sum_ref, totals):
    targets = [target_ref[z] for z in range(2)]

    def step(group, totals):
        return tuple(totals[z] + gathered(targets[z], near_ref, sum_ref, group, range(3)) for z in range(2))

    return lax.fori_loop(0, near_ref.shape[0], step, tuple(totals))


def plane_kernel(size_y, *refs):
    planes, (target_ref, total_ref, near_ref, sum_ref) = refs[:-4], refs[-4:]
    own_ref = planes[0]
    for z in range(2):
        target_ref[z] = target_rows(shifted(own_ref[z], (0, 0, z)))
    entries = []
    for ref, shifts in zip(planes, y_shifts(size_y)):
        for y in shifts:
            entries += [(ref[z], (0, y, z)) for z in range(2)]
    fill(near_ref, sum_ref, entries)
    zero = jnp.zeros(total_ref.shape[1:], F32)
    totals = both_targets(target_ref, near_ref, sum_ref, (zero, zero))
    for z in range(2):
        total_ref[z] = totals[z]


def slab_kernel(size_y, target_ref, before_ref, near_x_ref, far_x_ref, total_ref, near_ref, sum_ref):
    entries = []
    for ref, x in ((near_x_ref, ahead("gx")), (far_x_ref, -ahead("gx"))):
        for plane, shifts in enumerate(y_shifts(size_y)):
            for y in shifts:
                entries += [(ref[plane, z], (x, y, z)) for z in range(2)]
    fill(near_ref, sum_ref, entries)
    totals = both_targets(target_ref, near_ref, sum_ref, (before_ref[0], before_ref[1]))
    for z in range(2):
        total_ref[z] = totals[z]


def level_kernel(size_y, first, last, counts_ref, speed_ref, own_ref, target_ref, before_ref, near_z_ref, far_z_ref, *refs):
    if last:
        place_out, speed_out, near_ref, sum_ref = refs
    else:
        packed_out, speed_out, near_ref, sum_ref = refs
    turn = ahead("gz")
    near_z = (1 + turn) // 2
    sides = ((near_z_ref, near_z), (far_z_ref, 1 - near_z))
    lists = []
    for ref, z in sides:
        entries = []
        for column, x in enumerate((0, ahead("gx"), -ahead("gx"))):
            for plane, shifts in enumerate(y_shifts(size_y)):
                entries += [(ref[column, plane], (x, y, 3 * z - 1)) for y in shifts]
        lists.append(entries)
    entries = []
    for group in range(3):
        for side in range(2):
            entries += lists[side][3 * group : 3 * group + 3]
    for number, (packed, offset) in enumerate(entries):
        group, member = divmod(number, 6)
        distance, summed = source_rows(packed, offset)
        near_ref[group, member] = distance
        sum_ref[group, member] = summed
    targets = [target_ref[z] for _, z in sides]

    def step(group, totals):
        return tuple(
            totals[side] + gathered(targets[side], near_ref, sum_ref, group, range(3 * side, 3 * side + 3)) for side in range(2)
        )

    totals = lax.fori_loop(0, near_ref.shape[0], step, tuple(before_ref[z] for _, z in sides))
    slots = own_ref.shape[-1]
    swap = near_z == 1
    totals = [total.T for total in totals]
    totals = [jnp.where(swap, totals[1 - z], totals[z]) for z in range(2)]
    for z in range(2):
        total = totals[z][0:8] + totals[z][8:16] + totals[z][16:24]
        total = total[0:4]
        own = own_ref[z]
        accel = total - shifted(own, (0, 0, z)) * total[3:4]
        if first:
            speed = jnp.concatenate([speed_ref[c, 0, 0, z : z + 1, :] for c in range(3)] + [jnp.zeros((1, slots), F32)], axis=0)
        else:
            speed = speed_ref[z]
        speed = speed + time_step * accel
        place = jnp.clip(own + time_step * speed, 0.0, 1.0)
        if last:
            keep = occupied(counts_ref, z, (1, slots))
            for c in range(3):
                place_out[c, 0, 0, z : z + 1, :] = jnp.where(keep, place[c : c + 1], 0.0)
                speed_out[c, 0, 0, z : z + 1, :] = jnp.where(keep, speed[c : c + 1], 0.0)
        else:
            row = row_index(4, slots)
            packed_out[z] = jnp.where(row < 3, place, own)
            speed_out[z] = speed


VMEM = pl.BlockSpec(memory_space=pltpu.VMEM)
SMEM = pl.BlockSpec(memory_space=pltpu.SMEM)


def swaps(axis):
    size = lax.axis_size(axis)
    near = [(i, i ^ 1) for i in range(size)]
    far = [(i, (((i + 1) ^ 1) - 1) % size) for i in range(size)]
    return near, far


def scratch(groups, members, slots):
    return [pltpu.VMEM((groups, members, 48, slots), BF16), pltpu.VMEM((groups, members, 32, slots), BF16)]


def call(kernel, inputs, outputs, pairs, groups, members, slots):
    return pl.pallas_call(
        kernel,
        out_shape=outputs,
        in_specs=[spec for spec, _ in inputs],
        out_specs=tuple(VMEM for _ in outputs),
        scratch_shapes=scratch(groups, members, slots),
        compiler_params=pltpu.CompilerParams(vmem_limit_bytes=24 * 1024 * 1024),
        cost_estimate=pl.CostEstimate(flops=pairs * slots * slots * 1000, bytes_accessed=1 << 18, transcendentals=0),
    )(*[value for _, value in inputs])


def on_device(positions, velocities, mass, counts):
    slots = positions.shape[-1]
    size_y = lax.axis_size("gy")
    bins = jax.ShapeDtypeStruct((2, 4, slots), F32)
    full = jax.ShapeDtypeStruct(positions.shape, F32)
    running = jax.ShapeDtypeStruct((2, slots, 32), F32)
    packed = pl.pallas_call(
        pack_kernel,
        out_shape=bins,
        in_specs=[SMEM, VMEM, VMEM],
        out_specs=VMEM,
    )(counts, positions, mass)
    speed = velocities
    upper = lax.rem(lax.axis_index("gz"), 2)
    for subcycle in range(SUBCYCLES):
        first, last = subcycle == 0, subcycle == SUBCYCLES - 1
        near, far = swaps("gy")
        planes = [packed]
        if size_y > 2:
            other = lax.ppermute(packed, "gy", far)
            planes += [lax.ppermute(packed, "gy", near), other]
        else:
            planes.append(lax.ppermute(packed, "gy", near))
        plane = jnp.stack(planes)
        near, far = swaps("gx")
        far_x = lax.ppermute(plane, "gx", far)
        near_x = lax.ppermute(plane, "gx", near)
        targets, total = call(
            functools.partial(plane_kernel, size_y),
            [(VMEM, value) for value in planes],
            (jax.ShapeDtypeStruct((2, slots, 48), BF16), running),
            12, 2, 3, slots,
        )
        slab = jnp.stack([plane, near_x, far_x])
        near, far = swaps("gz")
        far_z = lax.ppermute(lax.dynamic_index_in_dim(slab, upper, 2, False), "gz", far)
        near_z = lax.ppermute(lax.dynamic_index_in_dim(slab, 1 - upper, 2, False), "gz", near)
        (total,) = call(
            functools.partial(slab_kernel, size_y),
            [(VMEM, value) for value in (targets, total, near_x, far_x)],
            (running,),
            24, 4, 3, slots,
        )
        packed, speed = call(
            functools.partial(level_kernel, size_y, first, last),
            [(SMEM, counts)] + [(VMEM, value) for value in (speed, packed, targets, total, near_z, far_z)],
            (full, full) if last else (bins, bins),
            18, 3, 6, slots,
        )
    return packed, speed


def solution(mesh):
    placed = (
        P(None, "gx", "gy", "gz", None),
        P(None, "gx", "gy", "gz", None),
        P("gx", "gy", "gz", None),
        P("gx", "gy", "gz"),
    )
    return jax.shard_map(
        on_device,
        mesh=mesh,
        in_specs=placed,
        out_specs=(P(None, "gx", "gy", "gz", None), P(None, "gx", "gy", "gz", None)),
        check_vma=False,
    )
```

```python
import functools

import jax
import jax.numpy as jnp
from jax import lax
from jax.experimental import pallas as pl
from jax.experimental.pallas import tpu as pltpu
from jax.sharding import PartitionSpec as P

SUBCYCLES = 2

time_step = 0.25

CENTRE = (0.5, 0.5, 1.0)
F32, BF16 = jnp.float32, jnp.bfloat16


def parts(value):
    high = value.astype(BF16).astype(F32)
    rest = value - high
    mid = rest.astype(BF16).astype(F32)
    return high, mid, rest - mid


def row_index(rows, slots):
    return lax.broadcasted_iota(jnp.int32, (rows, slots), 0)


def shifted(packed, offset):
    row = row_index(*packed.shape)
    x, y, z = [jnp.asarray(o, F32) - c for o, c in zip(offset, CENTRE)]
    move = jnp.where(row == 0, x, jnp.where(row == 1, y, jnp.where(row == 2, z, 0.0)))
    return packed + move


def source_rows(moved):
    row = row_index(*moved.shape)
    square = jnp.sum(jnp.where(row < 3, moved * moved, 0.0), axis=0, keepdims=True)
    head = jnp.where(row < 3, moved, square)
    tail = jnp.where(row == 0, 1.0, 0.0).astype(F32)
    high, mid, low = parts(jnp.concatenate([head, tail], axis=0))
    distance = jnp.concatenate([high, high, high, mid, mid, low], axis=0).astype(BF16)
    mass = moved[3:4]
    carried = jnp.where(row < 3, moved * mass, mass)
    high, mid, low = parts(jnp.concatenate([carried, jnp.zeros_like(carried)], axis=0))
    summed = jnp.concatenate([high, mid, low, jnp.zeros_like(low)], axis=0).astype(BF16)
    return distance, summed


def target_rows(moved):
    slots = moved.shape[-1]
    row = row_index(4, slots)
    square = jnp.sum(jnp.where(row < 3, moved * moved, 0.0), axis=0, keepdims=True)
    head = jnp.where(row < 3, 2.0 * moved, -1.0)
    tail = jnp.where(row == 0, 1.0 - square, 0.0)
    high, mid, low = parts(jnp.concatenate([head, tail], axis=0))
    return jnp.concatenate([high, mid, low, high, mid, high], axis=0).T.astype(BF16)


def pair_weight(target, source):
    near = jnp.maximum(jnp.dot(target, source, preferred_element_type=F32), 0.0)
    weight = near * near * near
    high = weight.astype(BF16)
    return high, (weight - high.astype(F32)).astype(BF16)


def contract(weights, rows):
    return lax.dot_general(weights, rows, (((1,), (1,)), ((), ())), preferred_element_type=F32)


def occupied(counts_ref, z, shape):
    return lax.broadcasted_iota(jnp.int32, shape, 1) < counts_ref[0, 0, z]


def pack_kernel(counts_ref, place_ref, mass_ref, packed_ref):
    for z in range(2):
        mass = mass_ref[0, 0, z : z + 1, :]
        weight = jnp.where(occupied(counts_ref, z, mass.shape), mass, 0.0)
        rows = [place_ref[c, 0, 0, z : z + 1, :] for c in range(3)]
        packed_ref[z] = jnp.concatenate(rows + [weight], axis=0)


def ahead(axis):
    return 1 - 2 * lax.rem(lax.axis_index(axis), 2)


def y_shifts(size):
    if size == 2:
        return [[0], [-1, 1]]
    return [[0], [ahead("gy")], [-ahead("gy")]]


def fill(near_ref, sum_ref, list_ref, entries):
    half = list_ref.shape[-1]
    lane = lax.broadcasted_iota(jnp.int32, (8, half), 1)
    list_ref[...] = jnp.zeros_like(list_ref)
    place = jnp.int32(0)
    held = {}
    for number, (ref, index, offset) in enumerate(entries):
        packed = ref[index]
        head, tail = shifted(packed[:, :half], offset), shifted(packed[:, half:], offset)
        if number == len(entries) - 1 and number % 2 == 0:
            list_ref[0] = jnp.concatenate([head, jnp.zeros_like(head)], axis=0)
        else:
            distance, summed = source_rows(head)
            near_ref[:, number * half : (number + 1) * half] = distance
            sum_ref[:, number * half : (number + 1) * half] = summed
        held[number] = tail
    if len(entries) % 2:
        place = place + half
    known = {}
    for number, (ref, index, offset) in enumerate(entries):
        tail = held[number]
        key = (id(ref),) + (index if isinstance(index, tuple) else (index,))
        if key not in known:
            present = jnp.where(tail[3:4] != 0.0, lane[0:1] + 1, 0).astype(F32)
            known[key] = jnp.max(present).astype(jnp.int32)
        length = known[key]
        tile, turn = lax.div(place, half), lax.rem(place, half)
        tail = jnp.where(lane < length, jnp.concatenate([tail, jnp.zeros_like(tail)], axis=0), 0.0)
        tail = pltpu.roll(tail, turn, 1)
        list_ref[tile] += jnp.where(lane >= turn, tail, 0.0)
        list_ref[tile + 1] += jnp.where(lane < turn, tail, 0.0)
        place = place + length
    return place


def gathered(target, nears, sums):
    highs, lows = [], []
    for near in nears:
        high, low = pair_weight(target, near)
        highs.append(high)
        lows.append(low)
    rows = jnp.concatenate(sums, axis=1)
    return contract(jnp.concatenate(highs + lows, axis=1), jnp.concatenate([rows, rows], axis=1))


def sums_over(targets, totals, near_ref, sum_ref, list_ref, length, chunk):
    half = list_ref.shape[-1]
    wide = 2 * half
    full = near_ref.shape[1] // (chunk * half)

    def first(number, totals):
        at = number * (chunk * half)
        nears, sums = [], []
        for tile in range(chunk // 2):
            lanes = pl.ds(pl.multiple_of(at + tile * wide, wide), wide)
            nears.append(near_ref[:, lanes])
            sums.append(sum_ref[:, lanes])
        return tuple(total + gathered(target, nears, sums) for target, total in zip(targets, totals))

    if full == 1:
        totals = first(0, totals)
    else:
        totals = lax.fori_loop(0, full, first, tuple(totals))

    def rest(number, totals):
        moved = jnp.concatenate([list_ref[2 * number], list_ref[2 * number + 1]], axis=1)
        near, summed = source_rows(moved[0:4])
        return tuple(total + gathered(target, [near], [summed]) for target, total in zip(targets, totals))

    return lax.fori_loop(0, lax.div(length + (wide - 1), wide), rest, tuple(totals))


def plane_kernel(size_y, *refs):
    planes, (target_ref, total_ref, near_ref, sum_ref, list_ref) = refs[:-5], refs[-5:]
    own_ref = planes[0]
    for z in range(2):
        target_ref[z] = target_rows(shifted(own_ref[z], (0, 0, z)))
    entries = []
    for ref, shifts in zip(planes, y_shifts(size_y)):
        for y in shifts:
            entries += [(ref, z, (0, y, z)) for z in range(2)]
    length = fill(near_ref, sum_ref, list_ref, entries)
    zero = jnp.zeros(total_ref.shape[1:], F32)
    targets = [target_ref[z] for z in range(2)]
    totals = sums_over(targets, (zero, zero), near_ref, sum_ref, list_ref, length, 6)
    for z in range(2):
        total_ref[z] = totals[z]


def slab_kernel(size_y, target_ref, before_ref, near_x_ref, far_x_ref, total_ref, near_ref, sum_ref, list_ref):
    entries = []
    for ref, x in ((near_x_ref, ahead("gx")), (far_x_ref, -ahead("gx"))):
        for plane, shifts in enumerate(y_shifts(size_y)):
            for y in shifts:
                entries += [(ref, (plane, z), (x, y, z)) for z in range(2)]
    length = fill(near_ref, sum_ref, list_ref, entries)
    targets = [target_ref[z] for z in range(2)]
    totals = sums_over(targets, (before_ref[0], before_ref[1]), near_ref, sum_ref, list_ref, length, 6)
    for z in range(2):
        total_ref[z] = totals[z]


def complete(size_y, first, z, speed_ref, own_ref, target_ref, before_ref, source_ref, near_ref, sum_ref, list_ref):
    entries = []
    for column, x in enumerate((0, ahead("gx"), -ahead("gx"))):
        for plane, shifts in enumerate(y_shifts(size_y)):
            entries += [(source_ref, (column, plane), (x, y, 3 * z - 1)) for y in shifts]
    length = fill(near_ref, sum_ref, list_ref, entries)
    (total,) = sums_over([target_ref[z]], (before_ref[z],), near_ref, sum_ref, list_ref, length, 8)
    total = total.T
    total = (total[0:8] + total[8:16] + total[16:24])[0:4]
    own = own_ref[z]
    accel = total - shifted(own, (0, 0, z)) * total[3:4]
    if first:
        rows = [jnp.where(z == 1, speed_ref[c, 0, 0, 1:2, :], speed_ref[c, 0, 0, 0:1, :]) for c in range(3)]
        speed = jnp.concatenate(rows + [jnp.zeros_like(rows[0])], axis=0)
    else:
        speed = speed_ref[z]
    speed = speed + time_step * accel
    place = jnp.clip(own + time_step * speed, 0.0, 1.0)
    return jnp.where(row_index(*own.shape) < 3, place, own), speed


def near_side():
    return (1 + ahead("gz")) // 2


def near_kernel(size_y, first, speed_ref, own_ref, target_ref, before_ref, source_ref, bin_ref, near_ref, sum_ref, list_ref):
    place, speed = complete(
        size_y, first, near_side(), speed_ref, own_ref, target_ref, before_ref, source_ref, near_ref, sum_ref, list_ref
    )
    bin_ref[0] = place
    bin_ref[1] = speed


def far_kernel(size_y, first, last, counts_ref, bin_ref, speed_ref, own_ref, target_ref, before_ref, source_ref, place_out, speed_out, near_ref, sum_ref, list_ref):
    other = near_side()
    z = 1 - other
    place, speed = complete(
        size_y, first, z, speed_ref, own_ref, target_ref, before_ref, source_ref, near_ref, sum_ref, list_ref
    )
    if not last:
        place_out[z] = place
        speed_out[z] = speed
        place_out[other] = bin_ref[0]
        speed_out[other] = bin_ref[1]
        return
    for side in range(2):
        keep = occupied(counts_ref, side, (1, place.shape[-1]))
        moved = jnp.where(z == side, place, bin_ref[0])
        kicked = jnp.where(z == side, speed, bin_ref[1])
        for c in range(3):
            place_out[c, 0, 0, side : side + 1, :] = jnp.where(keep, moved[c : c + 1], 0.0)
            speed_out[c, 0, 0, side : side + 1, :] = jnp.where(keep, kicked[c : c + 1], 0.0)


VMEM = pl.BlockSpec(memory_space=pltpu.VMEM)
SMEM = pl.BlockSpec(memory_space=pltpu.SMEM)


def swaps(axis):
    size = lax.axis_size(axis)
    near = [(i, i ^ 1) for i in range(size)]
    far = [(i, (((i + 1) ^ 1) - 1) % size) for i in range(size)]
    return near, far


def call(kernel, inputs, outputs, sources, targets, slots):
    half = slots // 2
    heads = sources // 2 * 2
    return pl.pallas_call(
        kernel,
        out_shape=outputs,
        in_specs=[spec for spec, _ in inputs],
        out_specs=tuple(VMEM for _ in outputs),
        scratch_shapes=[
            pltpu.VMEM((48, heads * half), BF16),
            pltpu.VMEM((32, heads * half), BF16),
            pltpu.VMEM((heads + 4, 8, half), F32),
        ],
        compiler_params=pltpu.CompilerParams(vmem_limit_bytes=24 * 1024 * 1024),
        cost_estimate=pl.CostEstimate(flops=sources * targets * slots * slots * 1000, bytes_accessed=1 << 18, transcendentals=0),
    )(*[value for _, value in inputs])


def on_device(positions, velocities, mass, counts):
    slots = positions.shape[-1]
    size_y = lax.axis_size("gy")
    bins = jax.ShapeDtypeStruct((2, 4, slots), F32)
    full = jax.ShapeDtypeStruct(positions.shape, F32)
    running = jax.ShapeDtypeStruct((2, slots, 32), F32)
    packed = pl.pallas_call(
        pack_kernel,
        out_shape=bins,
        in_specs=[SMEM, VMEM, VMEM],
        out_specs=VMEM,
    )(counts, positions, mass)
    speed = velocities
    upper = lax.rem(lax.axis_index("gz"), 2)
    for subcycle in range(SUBCYCLES):
        first, last = subcycle == 0, subcycle == SUBCYCLES - 1
        near, far = swaps("gy")
        planes = [packed]
        if size_y > 2:
            other = lax.ppermute(packed, "gy", far)
            planes += [lax.ppermute(packed, "gy", near), other]
        else:
            planes.append(lax.ppermute(packed, "gy", near))
        plane = jnp.stack(planes)
        near, far = swaps("gx")
        far_x = lax.ppermute(plane, "gx", far)
        near_x = lax.ppermute(plane, "gx", near)
        targets, total = call(
            functools.partial(plane_kernel, size_y),
            [(VMEM, value) for value in planes],
            (jax.ShapeDtypeStruct((2, slots, 48), BF16), running),
            6, 2, slots,
        )
        slab = jnp.stack([plane, near_x, far_x])
        near, far = swaps("gz")
        far_z = lax.ppermute(lax.dynamic_index_in_dim(slab, upper, 2, False), "gz", far)
        near_z = lax.ppermute(lax.dynamic_index_in_dim(slab, 1 - upper, 2, False), "gz", near)
        (total,) = call(
            functools.partial(slab_kernel, size_y),
            [(VMEM, value) for value in (targets, total, near_x, far_x)],
            (running,),
            12, 2, slots,
        )
        state = [(VMEM, value) for value in (speed, packed, targets, total)]
        (half_done,) = call(
            functools.partial(near_kernel, size_y, first),
            state + [(VMEM, near_z)],
            (bins,),
            9, 1, slots,
        )
        packed, speed = call(
            functools.partial(far_kernel, size_y, first, last),
            [(SMEM, counts), (VMEM, half_done)] + state + [(VMEM, far_z)],
            (full, full) if last else (bins, bins),
            9, 1, slots,
        )
    return packed, speed


def solution(mesh):
    placed = (
        P(None, "gx", "gy", "gz", None),
        P(None, "gx", "gy", "gz", None),
        P("gx", "gy", "gz", None),
        P("gx", "gy", "gz"),
    )
    return jax.shard_map(
        on_device,
        mesh=mesh,
        in_specs=placed,
        out_specs=(P(None, "gx", "gy", "gz", None), P(None, "gx", "gy", "gz", None)),
        check_vma=False,
    )
```

```python
import functools

import jax
import jax.numpy as jnp
from jax import lax
from jax.experimental import pallas as pl
from jax.experimental.pallas import tpu as pltpu
from jax.sharding import PartitionSpec as P

SUBCYCLES = 2

time_step = 0.25

CENTRE = (0.5, 0.5, 1.0)
F32, BF16 = jnp.float32, jnp.bfloat16


def parts(value):
    high = value.astype(BF16).astype(F32)
    rest = value - high
    mid = rest.astype(BF16).astype(F32)
    return high, mid, rest - mid


def row_index(rows, slots):
    return lax.broadcasted_iota(jnp.int32, (rows, slots), 0)


def shifted(packed, offset):
    row = row_index(*packed.shape)
    x, y, z = [jnp.asarray(o, F32) - c for o, c in zip(offset, CENTRE)]
    move = jnp.where(row == 0, x, jnp.where(row == 1, y, jnp.where(row == 2, z, 0.0)))
    return packed + move


def source_rows(moved):
    row = row_index(*moved.shape)
    square = jnp.sum(jnp.where(row < 3, moved * moved, 0.0), axis=0, keepdims=True)
    head = jnp.where(row < 3, moved, square)
    tail = jnp.where(row == 0, 1.0, 0.0).astype(F32)
    high, mid, low = parts(jnp.concatenate([head, tail], axis=0))
    distance = jnp.concatenate([high, high, high, mid, mid, low], axis=0).astype(BF16)
    mass = moved[3:4]
    carried = jnp.where(row < 3, moved * mass, mass)
    high, mid, low = parts(jnp.concatenate([carried, jnp.zeros_like(carried)], axis=0))
    summed = jnp.concatenate([high, mid, low, jnp.zeros_like(low)], axis=0).astype(BF16)
    return distance, summed


def target_rows(moved):
    slots = moved.shape[-1]
    row = row_index(4, slots)
    square = jnp.sum(jnp.where(row < 3, moved * moved, 0.0), axis=0, keepdims=True)
    head = jnp.where(row < 3, 2.0 * moved, -1.0)
    tail = jnp.where(row == 0, 1.0 - square, 0.0)
    high, mid, low = parts(jnp.concatenate([head, tail], axis=0))
    return jnp.concatenate([high, mid, low, high, mid, high], axis=0).T.astype(BF16)


def pair_weight(target, source):
    near = jnp.maximum(jnp.dot(target, source, preferred_element_type=F32), 0.0)
    weight = near * near * near
    high = weight.astype(BF16)
    return high, (weight - high.astype(F32)).astype(BF16)


def contract(weights, rows):
    return lax.dot_general(weights, rows, (((1,), (1,)), ((), ())), preferred_element_type=F32)


def pack_kernel(counts_ref, place_ref, mass_ref, packed_ref, keep_ref):
    for z in range(2):
        mass = mass_ref[0, 0, z : z + 1, :]
        keep = lax.broadcasted_iota(jnp.int32, mass.shape, 1) < counts_ref[0, :, z : z + 1]
        rows = [place_ref[c, 0, 0, z : z + 1, :] for c in range(3)]
        packed_ref[z] = jnp.concatenate(rows + [jnp.where(keep, mass, 0.0)], axis=0)
        keep_ref[z] = jnp.broadcast_to(jnp.where(keep, 1.0, 0.0), keep_ref.shape[1:])


def ahead(axis):
    return 1 - 2 * lax.rem(lax.axis_index(axis), 2)


def y_shifts(size):
    if size == 2:
        return [[0], [-1, 1]]
    return [[0], [ahead("gy")], [-ahead("gy")]]


def list_chunk(list_ref, chunk):
    return jnp.concatenate([list_ref[2 * chunk], list_ref[2 * chunk + 1]], axis=1)[0:4]


def fill(near_ref, sum_ref, list_ref, entries):
    half = list_ref.shape[-1]
    lane = lax.broadcasted_iota(jnp.int32, (8, half), 1)
    list_ref[...] = jnp.zeros_like(list_ref)
    place = jnp.int32(0)
    held = {}
    for number, (ref, index, offset) in enumerate(entries):
        packed = ref[index]
        head, tail = shifted(packed[:, :half], offset), shifted(packed[:, half:], offset)
        if number == len(entries) - 1 and number % 2 == 0:
            list_ref[0] = jnp.concatenate([head, jnp.zeros_like(head)], axis=0)
        else:
            distance, summed = source_rows(head)
            near_ref[:, number * half : (number + 1) * half] = distance
            sum_ref[:, number * half : (number + 1) * half] = summed
        held[number] = tail
    if len(entries) % 2:
        place = place + half
    known = {}
    for number, (ref, index, offset) in enumerate(entries):
        tail = held[number]
        key = (id(ref),) + (index if isinstance(index, tuple) else (index,))
        if key not in known:
            present = jnp.where(tail[3:4] != 0.0, lane[0:1] + 1, 0).astype(F32)
            known[key] = jnp.max(present).astype(jnp.int32)
        length = known[key]
        tile, turn = lax.div(place, half), lax.rem(place, half)
        tail = jnp.where(lane < length, jnp.concatenate([tail, jnp.zeros_like(tail)], axis=0), 0.0)
        tail = pltpu.roll(tail, turn, 1)
        list_ref[tile] += jnp.where(lane >= turn, tail, 0.0)
        list_ref[tile + 1] += jnp.where(lane < turn, tail, 0.0)
        place = place + length
    done = (len(entries) // 2) * 2 * half
    for chunk in range((near_ref.shape[1] - done) // (2 * half)):
        distance, summed = source_rows(list_chunk(list_ref, chunk))
        near_ref[:, done + chunk * 2 * half : done + (chunk + 1) * 2 * half] = distance
        sum_ref[:, done + chunk * 2 * half : done + (chunk + 1) * 2 * half] = summed
    return place


def gathered(target, nears, sums):
    highs, lows = [], []
    for near in nears:
        high, low = pair_weight(target, near)
        highs.append(high)
        lows.append(low)
    rows = jnp.concatenate(sums, axis=1)
    return contract(jnp.concatenate(highs + lows, axis=1), jnp.concatenate([rows, rows], axis=1))


def sums_over(targets, totals, near_ref, sum_ref, list_ref, length, sources, tiles):
    wide = 2 * list_ref.shape[-1]
    steps = near_ref.shape[1] // (tiles * wide)

    def step(number, totals):
        nears, sums = [], []
        for tile in range(tiles):
            lanes = pl.ds(pl.multiple_of((number * tiles + tile) * wide, wide), wide)
            nears.append(near_ref[:, lanes])
            sums.append(sum_ref[:, lanes])
        return tuple(total + gathered(target, nears, sums) for target, total in zip(targets, totals))

    totals = step(0, totals) if steps == 1 else lax.fori_loop(0, steps, step, tuple(totals))
    done = steps * tiles - sources // 2

    def rest(number, totals):
        near, summed = source_rows(list_chunk(list_ref, number))
        return tuple(total + gathered(target, [near], [summed]) for target, total in zip(targets, totals))

    return lax.fori_loop(done, jnp.maximum(lax.div(length + (wide - 1), wide), done), rest, tuple(totals))


def plane_kernel(size_y, *refs):
    planes, (target_ref, total_ref, near_ref, sum_ref, list_ref) = refs[:-5], refs[-5:]
    own_ref = planes[0]
    for z in range(2):
        target_ref[z] = target_rows(shifted(own_ref[z], (0, 0, z)))
    entries = []
    for ref, shifts in zip(planes, y_shifts(size_y)):
        for y in shifts:
            entries += [(ref, z, (0, y, z)) for z in range(2)]
    length = fill(near_ref, sum_ref, list_ref, entries)
    zero = jnp.zeros(total_ref.shape[1:], F32)
    targets = [target_ref[z] for z in range(2)]
    totals = sums_over(targets, (zero, zero), near_ref, sum_ref, list_ref, length, len(entries), 5)
    for z in range(2):
        total_ref[z] = totals[z]


def slab_kernel(size_y, target_ref, before_ref, near_x_ref, far_x_ref, total_ref, near_ref, sum_ref, list_ref):
    entries = []
    for ref, x in ((near_x_ref, ahead("gx")), (far_x_ref, -ahead("gx"))):
        for plane, shifts in enumerate(y_shifts(size_y)):
            for y in shifts:
                entries += [(ref, (plane, z), (x, y, z)) for z in range(2)]
    length = fill(near_ref, sum_ref, list_ref, entries)
    targets = [target_ref[z] for z in range(2)]
    totals = sums_over(targets, (before_ref[0], before_ref[1]), near_ref, sum_ref, list_ref, length, len(entries), 3)
    for z in range(2):
        total_ref[z] = totals[z]


def complete(size_y, first, z, speed_ref, own_ref, target_ref, before_ref, source_ref, near_ref, sum_ref, list_ref):
    entries = []
    for column, x in enumerate((0, ahead("gx"), -ahead("gx"))):
        for plane, shifts in enumerate(y_shifts(size_y)):
            entries += [(source_ref, (column, plane), (x, y, 3 * z - 1)) for y in shifts]
    length = fill(near_ref, sum_ref, list_ref, entries)
    (total,) = sums_over([target_ref[z]], (before_ref[z],), near_ref, sum_ref, list_ref, length, len(entries), 7)
    total = total.T
    total = (total[0:8] + total[8:16] + total[16:24])[0:4]
    own = own_ref[z]
    accel = total - shifted(own, (0, 0, z)) * total[3:4]
    if first:
        rows = [jnp.where(z == 1, speed_ref[c, 0, 0, 1:2, :], speed_ref[c, 0, 0, 0:1, :]) for c in range(3)]
        speed = jnp.concatenate(rows + [jnp.zeros_like(rows[0])], axis=0)
    else:
        speed = speed_ref[z]
    speed = speed + time_step * accel
    place = jnp.clip(own + time_step * speed, 0.0, 1.0)
    return jnp.where(row_index(*own.shape) < 3, place, own), speed


def near_side():
    return (1 + ahead("gz")) // 2


def near_kernel(size_y, first, speed_ref, own_ref, target_ref, before_ref, source_ref, bin_ref, near_ref, sum_ref, list_ref):
    place, speed = complete(
        size_y, first, near_side(), speed_ref, own_ref, target_ref, before_ref, source_ref, near_ref, sum_ref, list_ref
    )
    bin_ref[0] = place
    bin_ref[1] = speed


def far_kernel(size_y, first, last, keep_ref, bin_ref, speed_ref, own_ref, target_ref, before_ref, source_ref, place_out, speed_out, near_ref, sum_ref, list_ref):
    other = near_side()
    z = 1 - other
    place, speed = complete(
        size_y, first, z, speed_ref, own_ref, target_ref, before_ref, source_ref, near_ref, sum_ref, list_ref
    )
    if not last:
        place_out[z] = place
        speed_out[z] = speed
        place_out[other] = bin_ref[0]
        speed_out[other] = bin_ref[1]
        return
    for side in range(2):
        keep = keep_ref[side, 0:1] > 0.0
        moved = jnp.where(z == side, place, bin_ref[0])
        kicked = jnp.where(z == side, speed, bin_ref[1])
        for c in range(3):
            place_out[c, 0, 0, side : side + 1, :] = jnp.where(keep, moved[c : c + 1], 0.0)
            speed_out[c, 0, 0, side : side + 1, :] = jnp.where(keep, kicked[c : c + 1], 0.0)


VMEM = pl.BlockSpec(memory_space=pltpu.VMEM)


def swaps(axis):
    size = lax.axis_size(axis)
    near = [(i, i ^ 1) for i in range(size)]
    far = [(i, (((i + 1) ^ 1) - 1) % size) for i in range(size)]
    return near, far


def call(kernel, inputs, outputs, sources, targets, slots, chunks):
    half = slots // 2
    heads = sources // 2 * 2
    return pl.pallas_call(
        kernel,
        out_shape=outputs,
        in_specs=[VMEM] * len(inputs),
        out_specs=tuple(VMEM for _ in outputs),
        scratch_shapes=[
            pltpu.VMEM((48, heads * half + chunks * slots), BF16),
            pltpu.VMEM((32, heads * half + chunks * slots), BF16),
            pltpu.VMEM((heads + 4, 8, half), F32),
        ],
        compiler_params=pltpu.CompilerParams(vmem_limit_bytes=24 * 1024 * 1024),
        cost_estimate=pl.CostEstimate(flops=sources * targets * slots * slots * 1000, bytes_accessed=1 << 18, transcendentals=0),
    )(*inputs)


def on_device(positions, velocities, mass, counts):
    slots = positions.shape[-1]
    size_y = lax.axis_size("gy")
    bins = jax.ShapeDtypeStruct((2, 4, slots), F32)
    full = jax.ShapeDtypeStruct(positions.shape, F32)
    running = jax.ShapeDtypeStruct((2, slots, 32), F32)
    packed, keep = pl.pallas_call(
        pack_kernel,
        out_shape=(bins, bins),
        in_specs=[VMEM] * 3,
        out_specs=(VMEM, VMEM),
    )(counts, positions, mass)
    speed = velocities
    upper = lax.rem(lax.axis_index("gz"), 2)
    for subcycle in range(SUBCYCLES):
        first, last = subcycle == 0, subcycle == SUBCYCLES - 1
        near, far = swaps("gy")
        planes = [packed]
        if size_y > 2:
            other = lax.ppermute(packed, "gy", far)
            planes += [lax.ppermute(packed, "gy", near), other]
        else:
            planes.append(lax.ppermute(packed, "gy", near))
        plane = jnp.stack(planes)
        near, far = swaps("gx")
        far_x = lax.ppermute(plane, "gx", far)
        near_x = lax.ppermute(plane, "gx", near)
        targets, total = call(
            functools.partial(plane_kernel, size_y),
            planes,
            (jax.ShapeDtypeStruct((2, slots, 48), BF16), running),
            6, 2, slots, 2,
        )
        slab = jnp.stack([plane, near_x, far_x])
        near, far = swaps("gz")
        far_z = lax.ppermute(lax.dynamic_index_in_dim(slab, upper, 2, False), "gz", far)
        near_z = lax.ppermute(lax.dynamic_index_in_dim(slab, 1 - upper, 2, False), "gz", near)
        (total,) = call(
            functools.partial(slab_kernel, size_y),
            [targets, total, near_x, far_x],
            (running,),
            12, 2, slots, 3,
        )
        state = [speed, packed, targets, total]
        (half_done,) = call(
            functools.partial(near_kernel, size_y, first),
            state + [near_z],
            (bins,),
            9, 1, slots, 3,
        )
        packed, speed = call(
            functools.partial(far_kernel, size_y, first, last),
            [keep, half_done] + state + [far_z],
            (full, full) if last else (bins, bins),
            9, 1, slots, 3,
        )
    return packed, speed


def solution(mesh):
    placed = (
        P(None, "gx", "gy", "gz", None),
        P(None, "gx", "gy", "gz", None),
        P("gx", "gy", "gz", None),
        P("gx", "gy", "gz"),
    )
    return jax.shard_map(
        on_device,
        mesh=mesh,
        in_specs=placed,
        out_specs=(P(None, "gx", "gy", "gz", None), P(None, "gx", "gy", "gz", None)),
        check_vma=False,
    )
```

```python
import functools

import jax
import jax.numpy as jnp
from jax import lax
from jax.experimental import pallas as pl
from jax.experimental.pallas import tpu as pltpu
from jax.sharding import PartitionSpec as P

SUBCYCLES = 2

time_step = 0.25

CENTRE = (0.5, 0.5, 1.0)
F32, BF16 = jnp.float32, jnp.bfloat16


def parts(value):
    high = value.astype(BF16).astype(F32)
    rest = value - high
    mid = rest.astype(BF16).astype(F32)
    return high, mid, rest - mid


def row_index(rows, slots):
    return lax.broadcasted_iota(jnp.int32, (rows, slots), 0)


def shifted(packed, offset):
    row = row_index(*packed.shape)
    x, y, z = [jnp.asarray(o, F32) - c for o, c in zip(offset, CENTRE)]
    move = jnp.where(row == 0, x, jnp.where(row == 1, y, jnp.where(row == 2, z, 0.0)))
    return packed + move


def source_rows(moved):
    row = row_index(*moved.shape)
    square = jnp.sum(jnp.where(row < 3, moved * moved, 0.0), axis=0, keepdims=True)
    head = jnp.where(row < 3, moved, square)
    tail = jnp.where(row == 0, 1.0, 0.0).astype(F32)
    high, mid, low = parts(jnp.concatenate([head, tail], axis=0))
    distance = jnp.concatenate([high, high, high, mid, mid, low], axis=0).astype(BF16)
    mass = moved[3:4]
    carried = jnp.where(row < 3, moved * mass, mass)
    high, mid, low = parts(jnp.concatenate([carried, jnp.zeros_like(carried)], axis=0))
    summed = jnp.concatenate([high, mid, low, jnp.zeros_like(low)], axis=0).astype(BF16)
    return distance, summed


def target_rows(moved):
    slots = moved.shape[-1]
    row = row_index(4, slots)
    square = jnp.sum(jnp.where(row < 3, moved * moved, 0.0), axis=0, keepdims=True)
    head = jnp.where(row < 3, 2.0 * moved, -1.0)
    tail = jnp.where(row == 0, 1.0 - square, 0.0)
    high, mid, low = parts(jnp.concatenate([head, tail], axis=0))
    return jnp.concatenate([high, mid, low, high, mid, high], axis=0).T.astype(BF16)


def pair_weight(target, source):
    near = jnp.maximum(jnp.dot(target, source, preferred_element_type=F32), 0.0)
    weight = near * near * near
    high = weight.astype(BF16)
    return high, (weight - high.astype(F32)).astype(BF16)


def contract(weights, rows):
    return lax.dot_general(weights, rows, (((1,), (1,)), ((), ())), preferred_element_type=F32)


def pack_kernel(counts_ref, place_ref, mass_ref, packed_ref, keep_ref):
    for z in range(2):
        mass = mass_ref[0, 0, z : z + 1, :]
        keep = lax.broadcasted_iota(jnp.int32, mass.shape, 1) < counts_ref[0, :, z : z + 1]
        rows = [place_ref[c, 0, 0, z : z + 1, :] for c in range(3)]
        packed_ref[z] = jnp.concatenate(rows + [jnp.where(keep, mass, 0.0)], axis=0)
        keep_ref[z] = jnp.broadcast_to(jnp.where(keep, 1.0, 0.0), keep_ref.shape[1:])


def ahead(axis):
    return 1 - 2 * lax.rem(lax.axis_index(axis), 2)


def y_sources(size):
    if size == 2:
        here = lax.axis_index("gy")
        return [(here, 0, 0), (1 - here, -1, 1), (1 - here, 1, 1)]
    return [(0, 0, 0), (1, ahead("gy"), 1), (2, -ahead("gy"), 2)]


def list_chunk(list_ref, chunk):
    return jnp.concatenate([list_ref[2 * chunk], list_ref[2 * chunk + 1]], axis=1)[0:4]


def fill(near_ref, sum_ref, list_ref, entries):
    half = list_ref.shape[-1]
    lane = lax.broadcasted_iota(jnp.int32, (8, half), 1)
    list_ref[...] = jnp.zeros_like(list_ref)
    place = jnp.int32(0)
    held = {}
    for number, (ref, index, offset, _) in enumerate(entries):
        packed = ref[index]
        head, tail = shifted(packed[:, :half], offset), shifted(packed[:, half:], offset)
        if number == len(entries) - 1 and number % 2 == 0:
            list_ref[0] = jnp.concatenate([head, jnp.zeros_like(head)], axis=0)
        else:
            distance, summed = source_rows(head)
            near_ref[:, number * half : (number + 1) * half] = distance
            sum_ref[:, number * half : (number + 1) * half] = summed
        held[number] = tail
    if len(entries) % 2:
        place = place + half
    known = {}
    for number, (_, _, _, key) in enumerate(entries):
        tail = held[number]
        if key not in known:
            present = jnp.where(tail[3:4] != 0.0, lane[0:1] + 1, 0).astype(F32)
            known[key] = jnp.max(present).astype(jnp.int32)
        length = known[key]
        tile, turn = lax.div(place, half), lax.rem(place, half)
        tail = jnp.where(lane < length, jnp.concatenate([tail, jnp.zeros_like(tail)], axis=0), 0.0)
        tail = pltpu.roll(tail, turn, 1)
        list_ref[tile] += jnp.where(lane >= turn, tail, 0.0)
        list_ref[tile + 1] += jnp.where(lane < turn, tail, 0.0)
        place = place + length
    done = (len(entries) // 2) * 2 * half
    for chunk in range((near_ref.shape[1] - done) // (2 * half)):
        distance, summed = source_rows(list_chunk(list_ref, chunk))
        near_ref[:, done + chunk * 2 * half : done + (chunk + 1) * 2 * half] = distance
        sum_ref[:, done + chunk * 2 * half : done + (chunk + 1) * 2 * half] = summed
    return place


def gathered(target, nears, sums):
    highs, lows = [], []
    for near in nears:
        high, low = pair_weight(target, near)
        highs.append(high)
        lows.append(low)
    rows = jnp.concatenate(sums, axis=1)
    return contract(jnp.concatenate(highs + lows, axis=1), jnp.concatenate([rows, rows], axis=1))


def sums_over(targets, totals, near_ref, sum_ref, list_ref, length, sources, tiles):
    wide = 2 * list_ref.shape[-1]
    steps = near_ref.shape[1] // (tiles * wide)

    def step(number, totals):
        nears, sums = [], []
        for tile in range(tiles):
            lanes = pl.ds(pl.multiple_of((number * tiles + tile) * wide, wide), wide)
            nears.append(near_ref[:, lanes])
            sums.append(sum_ref[:, lanes])
        return tuple(total + gathered(target, nears, sums) for target, total in zip(targets, totals))

    totals = step(0, totals) if steps == 1 else lax.fori_loop(0, steps, step, tuple(totals))
    done = steps * tiles - sources // 2

    def rest(number, totals):
        near, summed = source_rows(list_chunk(list_ref, number))
        return tuple(total + gathered(target, [near], [summed]) for target, total in zip(targets, totals))

    return lax.fori_loop(done, jnp.maximum(lax.div(length + (wide - 1), wide), done), rest, tuple(totals))


def plane_kernel(size_y, own_ref, plane_ref, target_ref, total_ref, near_ref, sum_ref, list_ref):
    for z in range(2):
        target_ref[z] = target_rows(shifted(own_ref[z], (0, 0, z)))
    entries = []
    for plane, y, number in y_sources(size_y):
        entries += [(plane_ref, (plane, z), (0, y, z), (number, z)) for z in range(2)]
    length = fill(near_ref, sum_ref, list_ref, entries)
    zero = jnp.zeros(total_ref.shape[1:], F32)
    targets = [target_ref[z] for z in range(2)]
    totals = sums_over(targets, (zero, zero), near_ref, sum_ref, list_ref, length, len(entries), 5)
    for z in range(2):
        total_ref[z] = totals[z]


def slab_kernel(size_y, target_ref, before_ref, near_x_ref, far_x_ref, total_ref, near_ref, sum_ref, list_ref):
    entries = []
    for side, (ref, x) in enumerate(((near_x_ref, ahead("gx")), (far_x_ref, -ahead("gx")))):
        for plane, y, number in y_sources(size_y):
            entries += [(ref, (plane, z), (x, y, z), (side, number, z)) for z in range(2)]
    length = fill(near_ref, sum_ref, list_ref, entries)
    targets = [target_ref[z] for z in range(2)]
    totals = sums_over(targets, (before_ref[0], before_ref[1]), near_ref, sum_ref, list_ref, length, len(entries), 3)
    for z in range(2):
        total_ref[z] = totals[z]


def complete(size_y, first, z, speed_ref, own_ref, target_ref, before_ref, source_ref, near_ref, sum_ref, list_ref):
    entries = []
    for column, x in enumerate((0, ahead("gx"), -ahead("gx"))):
        for plane, y, number in y_sources(size_y):
            entries.append((source_ref, (column, plane), (x, y, 3 * z - 1), (column, number)))
    length = fill(near_ref, sum_ref, list_ref, entries)
    (total,) = sums_over([target_ref[z]], (before_ref[z],), near_ref, sum_ref, list_ref, length, len(entries), 7)
    total = total.T
    total = (total[0:8] + total[8:16] + total[16:24])[0:4]
    own = own_ref[z]
    accel = total - shifted(own, (0, 0, z)) * total[3:4]
    if first:
        rows = [jnp.where(z == 1, speed_ref[c, 0, 0, 1:2, :], speed_ref[c, 0, 0, 0:1, :]) for c in range(3)]
        speed = jnp.concatenate(rows + [jnp.zeros_like(rows[0])], axis=0)
    else:
        speed = speed_ref[z]
    speed = speed + time_step * accel
    place = jnp.clip(own + time_step * speed, 0.0, 1.0)
    return jnp.where(row_index(*own.shape) < 3, place, own), speed


def near_side():
    return (1 + ahead("gz")) // 2


def near_kernel(size_y, first, speed_ref, own_ref, target_ref, before_ref, source_ref, bin_ref, near_ref, sum_ref, list_ref):
    place, speed = complete(
        size_y, first, near_side(), speed_ref, own_ref, target_ref, before_ref, source_ref, near_ref, sum_ref, list_ref
    )
    bin_ref[0] = place
    bin_ref[1] = speed


def far_kernel(size_y, first, last, keep_ref, bin_ref, speed_ref, own_ref, target_ref, before_ref, source_ref, place_out, speed_out, near_ref, sum_ref, list_ref):
    other = near_side()
    z = 1 - other
    place, speed = complete(
        size_y, first, z, speed_ref, own_ref, target_ref, before_ref, source_ref, near_ref, sum_ref, list_ref
    )
    if not last:
        place_out[z] = place
        speed_out[z] = speed
        place_out[other] = bin_ref[0]
        speed_out[other] = bin_ref[1]
        return
    for side in range(2):
        keep = keep_ref[side, 0:1] > 0.0
        moved = jnp.where(z == side, place, bin_ref[0])
        kicked = jnp.where(z == side, speed, bin_ref[1])
        for c in range(3):
            place_out[c, 0, 0, side : side + 1, :] = jnp.where(keep, moved[c : c + 1], 0.0)
            speed_out[c, 0, 0, side : side + 1, :] = jnp.where(keep, kicked[c : c + 1], 0.0)


VMEM = pl.BlockSpec(memory_space=pltpu.VMEM)


def swaps(axis):
    size = lax.axis_size(axis)
    near = [(i, i ^ 1) for i in range(size)]
    far = [(i, (((i + 1) ^ 1) - 1) % size) for i in range(size)]
    return near, far


def call(kernel, inputs, outputs, sources, targets, slots, chunks):
    half = slots // 2
    heads = sources // 2 * 2
    return pl.pallas_call(
        kernel,
        out_shape=outputs,
        in_specs=[VMEM] * len(inputs),
        out_specs=tuple(VMEM for _ in outputs),
        scratch_shapes=[
            pltpu.VMEM((48, heads * half + chunks * slots), BF16),
            pltpu.VMEM((32, heads * half + chunks * slots), BF16),
            pltpu.VMEM((heads + 4, 8, half), F32),
        ],
        compiler_params=pltpu.CompilerParams(vmem_limit_bytes=24 * 1024 * 1024),
        cost_estimate=pl.CostEstimate(flops=sources * targets * slots * slots * 1000, bytes_accessed=1 << 18, transcendentals=0),
    )(*inputs)


def on_device(positions, velocities, mass, counts):
    slots = positions.shape[-1]
    size_y = lax.axis_size("gy")
    bins = jax.ShapeDtypeStruct((2, 4, slots), F32)
    full = jax.ShapeDtypeStruct(positions.shape, F32)
    running = jax.ShapeDtypeStruct((2, slots, 32), F32)
    packed, keep = pl.pallas_call(
        pack_kernel,
        out_shape=(bins, bins),
        in_specs=[VMEM] * 3,
        out_specs=(VMEM, VMEM),
    )(counts, positions, mass)
    speed = velocities
    upper = lax.rem(lax.axis_index("gz"), 2)
    for subcycle in range(SUBCYCLES):
        first, last = subcycle == 0, subcycle == SUBCYCLES - 1
        if size_y > 2:
            near, far = swaps("gy")
            other = lax.ppermute(packed, "gy", far)
            plane = jnp.stack([packed, lax.ppermute(packed, "gy", near), other])
        elif first:
            plane = lax.all_gather(packed, "gy")
        else:
            plane = lax.all_to_all(jnp.broadcast_to(packed[None], (2,) + packed.shape), "gy", 0, 0)
        near, far = swaps("gx")
        far_x = lax.ppermute(plane, "gx", far)
        near_x = lax.ppermute(plane, "gx", near)
        targets, total = call(
            functools.partial(plane_kernel, size_y),
            [packed, plane],
            (jax.ShapeDtypeStruct((2, slots, 48), BF16), running),
            6, 2, slots, 2,
        )
        slab = jnp.stack([plane, near_x, far_x])
        near, far = swaps("gz")
        far_z = lax.ppermute(lax.dynamic_index_in_dim(slab, upper, 2, False), "gz", far)
        near_z = lax.ppermute(lax.dynamic_index_in_dim(slab, 1 - upper, 2, False), "gz", near)
        (total,) = call(
            functools.partial(slab_kernel, size_y),
            [targets, total, near_x, far_x],
            (running,),
            12, 2, slots, 3,
        )
        state = [speed, packed, targets, total]
        (half_done,) = call(
            functools.partial(near_kernel, size_y, first),
            state + [near_z],
            (bins,),
            9, 1, slots, 3,
        )
        packed, speed = call(
            functools.partial(far_kernel, size_y, first, last),
            [keep, half_done] + state + [far_z],
            (full, full) if last else (bins, bins),
            9, 1, slots, 3,
        )
    return packed, speed


def solution(mesh):
    placed = (
        P(None, "gx", "gy", "gz", None),
        P(None, "gx", "gy", "gz", None),
        P("gx", "gy", "gz", None),
        P("gx", "gy", "gz"),
    )
    return jax.shard_map(
        on_device,
        mesh=mesh,
        in_specs=placed,
        out_specs=(P(None, "gx", "gy", "gz", None), P(None, "gx", "gy", "gz", None)),
        check_vma=False,
    )
```

```python
import functools

import jax
import jax.numpy as jnp
from jax import lax
from jax.experimental import pallas as pl
from jax.experimental.pallas import tpu as pltpu
from jax.sharding import PartitionSpec as P

SUBCYCLES = 2

time_step = 0.25

CENTRE = (0.5, 0.5, 1.0)
F32, BF16 = jnp.float32, jnp.bfloat16


def parts(value):
    high = value.astype(BF16).astype(F32)
    rest = value - high
    mid = rest.astype(BF16).astype(F32)
    return high, mid, rest - mid


def row_index(rows, slots):
    return lax.broadcasted_iota(jnp.int32, (rows, slots), 0)


def shifted(packed, offset):
    row = row_index(*packed.shape)
    x, y, z = [jnp.asarray(o, F32) - c for o, c in zip(offset, CENTRE)]
    move = jnp.where(row == 0, x, jnp.where(row == 1, y, jnp.where(row == 2, z, 0.0)))
    return packed + move


def source_rows(moved):
    row = row_index(*moved.shape)
    square = jnp.sum(jnp.where(row < 3, moved * moved, 0.0), axis=0, keepdims=True)
    head = jnp.where(row < 3, moved, square)
    tail = jnp.where(row == 0, 1.0, 0.0).astype(F32)
    high, mid, low = parts(jnp.concatenate([head, tail], axis=0))
    distance = jnp.concatenate([high, high, high, mid, mid, low], axis=0).astype(BF16)
    mass = moved[3:4]
    carried = jnp.where(row < 3, moved * mass, mass)
    high, mid, low = parts(jnp.concatenate([carried, jnp.zeros_like(carried)], axis=0))
    summed = jnp.concatenate([high, mid, low, jnp.zeros_like(low)], axis=0).astype(BF16)
    return distance, summed


def target_rows(moved):
    slots = moved.shape[-1]
    row = row_index(4, slots)
    square = jnp.sum(jnp.where(row < 3, moved * moved, 0.0), axis=0, keepdims=True)
    head = jnp.where(row < 3, 2.0 * moved, -1.0)
    tail = jnp.where(row == 0, 1.0 - square, 0.0)
    high, mid, low = parts(jnp.concatenate([head, tail], axis=0))
    return jnp.concatenate([high, mid, low, high, mid, high], axis=0).T.astype(BF16)


def pair_weight(target, source):
    near = jnp.maximum(jnp.dot(target, source, preferred_element_type=F32), 0.0)
    weight = near * near * near
    high = weight.astype(BF16)
    return high, (weight - high.astype(F32)).astype(BF16)


def contract(weights, rows):
    return lax.dot_general(weights, rows, (((1,), (1,)), ((), ())), preferred_element_type=F32)


def pack_kernel(counts_ref, place_ref, mass_ref, packed_ref, keep_ref):
    for z in range(2):
        mass = mass_ref[0, 0, z : z + 1, :]
        keep = lax.broadcasted_iota(jnp.int32, mass.shape, 1) < counts_ref[0, :, z : z + 1]
        rows = [place_ref[c, 0, 0, z : z + 1, :] for c in range(3)]
        packed_ref[z] = jnp.concatenate(rows + [jnp.where(keep, mass, 0.0)], axis=0)
        keep_ref[z] = jnp.broadcast_to(jnp.where(keep, 1.0, 0.0), keep_ref.shape[1:])


def y_shifts(size):
    return [[0], [-1, 1]] if size == 2 else [[0], [-1], [1]]


def list_chunk(list_ref, chunk):
    return jnp.concatenate([list_ref[2 * chunk], list_ref[2 * chunk + 1]], axis=1)[0:4]


def fill(near_ref, sum_ref, list_ref, entries):
    half = list_ref.shape[-1]
    lane = lax.broadcasted_iota(jnp.int32, (8, half), 1)
    list_ref[...] = jnp.zeros_like(list_ref)
    place = jnp.int32(0)
    held = {}
    for number, (ref, index, offset) in enumerate(entries):
        packed = ref[index]
        head, tail = shifted(packed[:, :half], offset), shifted(packed[:, half:], offset)
        if number == len(entries) - 1 and number % 2 == 0:
            list_ref[0] = jnp.concatenate([head, jnp.zeros_like(head)], axis=0)
        else:
            distance, summed = source_rows(head)
            near_ref[:, number * half : (number + 1) * half] = distance
            sum_ref[:, number * half : (number + 1) * half] = summed
        held[number] = tail
    if len(entries) % 2:
        place = place + half
    known = {}
    for number, (ref, index, offset) in enumerate(entries):
        tail = held[number]
        key = (id(ref),) + (index if isinstance(index, tuple) else (index,))
        if key not in known:
            present = jnp.where(tail[3:4] != 0.0, lane[0:1] + 1, 0).astype(F32)
            known[key] = jnp.max(present).astype(jnp.int32)
        length = known[key]
        tile, turn = lax.div(place, half), lax.rem(place, half)
        tail = jnp.where(lane < length, jnp.concatenate([tail, jnp.zeros_like(tail)], axis=0), 0.0)
        tail = pltpu.roll(tail, turn, 1)
        list_ref[tile] += jnp.where(lane >= turn, tail, 0.0)
        list_ref[tile + 1] += jnp.where(lane < turn, tail, 0.0)
        place = place + length
    done = (len(entries) // 2) * 2 * half
    for chunk in range((near_ref.shape[1] - done) // (2 * half)):
        distance, summed = source_rows(list_chunk(list_ref, chunk))
        near_ref[:, done + chunk * 2 * half : done + (chunk + 1) * 2 * half] = distance
        sum_ref[:, done + chunk * 2 * half : done + (chunk + 1) * 2 * half] = summed
    return place


def gathered(target, nears, sums):
    highs, lows = [], []
    for near in nears:
        high, low = pair_weight(target, near)
        highs.append(high)
        lows.append(low)
    rows = jnp.concatenate(sums, axis=1)
    return contract(jnp.concatenate(highs + lows, axis=1), jnp.concatenate([rows, rows], axis=1))


def sums_over(targets, totals, near_ref, sum_ref, list_ref, length, sources, tiles):
    wide = 2 * list_ref.shape[-1]
    steps = near_ref.shape[1] // (tiles * wide)

    def step(number, totals):
        nears, sums = [], []
        for tile in range(tiles):
            lanes = pl.ds(pl.multiple_of((number * tiles + tile) * wide, wide), wide)
            nears.append(near_ref[:, lanes])
            sums.append(sum_ref[:, lanes])
        return tuple(total + gathered(target, nears, sums) for target, total in zip(targets, totals))

    totals = step(0, totals) if steps == 1 else lax.fori_loop(0, steps, step, tuple(totals))
    done = steps * tiles - sources // 2

    def rest(number, totals):
        near, summed = source_rows(list_chunk(list_ref, number))
        return tuple(total + gathered(target, [near], [summed]) for target, total in zip(targets, totals))

    return lax.fori_loop(done, jnp.maximum(lax.div(length + (wide - 1), wide), done), rest, tuple(totals))


def plane_kernel(size_y, *refs):
    planes, (target_ref, total_ref, near_ref, sum_ref, list_ref) = refs[:-5], refs[-5:]
    own_ref = planes[0]
    for z in range(2):
        target_ref[z] = target_rows(shifted(own_ref[z], (0, 0, z)))
    entries = []
    for ref, shifts in zip(planes, y_shifts(size_y)):
        for y in shifts:
            entries += [(ref, z, (0, y, z)) for z in range(2)]
    length = fill(near_ref, sum_ref, list_ref, entries)
    zero = jnp.zeros(total_ref.shape[1:], F32)
    targets = [target_ref[z] for z in range(2)]
    totals = sums_over(targets, (zero, zero), near_ref, sum_ref, list_ref, length, len(entries), 5)
    for z in range(2):
        total_ref[z] = totals[z]


def slab_kernel(size_y, target_ref, before_ref, left_ref, right_ref, total_ref, near_ref, sum_ref, list_ref):
    entries = []
    for ref, x in ((left_ref, -1), (right_ref, 1)):
        for plane, shifts in enumerate(y_shifts(size_y)):
            for y in shifts:
                entries += [(ref, (plane, z), (x, y, z)) for z in range(2)]
    length = fill(near_ref, sum_ref, list_ref, entries)
    targets = [target_ref[z] for z in range(2)]
    totals = sums_over(targets, (before_ref[0], before_ref[1]), near_ref, sum_ref, list_ref, length, len(entries), 3)
    for z in range(2):
        total_ref[z] = totals[z]


def complete(size_y, first, z, speed_ref, own_ref, target_ref, before_ref, source_ref, near_ref, sum_ref, list_ref):
    entries = []
    for column, x in enumerate((0, -1, 1)):
        for plane, shifts in enumerate(y_shifts(size_y)):
            entries += [(source_ref, (column, plane), (x, y, 3 * z - 1)) for y in shifts]
    length = fill(near_ref, sum_ref, list_ref, entries)
    (total,) = sums_over([target_ref[z]], (before_ref[z],), near_ref, sum_ref, list_ref, length, len(entries), 7)
    total = total.T
    total = (total[0:8] + total[8:16] + total[16:24])[0:4]
    own = own_ref[z]
    accel = total - shifted(own, (0, 0, z)) * total[3:4]
    if first:
        rows = [speed_ref[c, 0, 0, z : z + 1, :] for c in range(3)]
        speed = jnp.concatenate(rows + [jnp.zeros_like(rows[0])], axis=0)
    else:
        speed = speed_ref[z]
    speed = speed + time_step * accel
    place = jnp.clip(own + time_step * speed, 0.0, 1.0)
    return jnp.where(row_index(*own.shape) < 3, place, own), speed


def below_kernel(size_y, first, speed_ref, own_ref, target_ref, before_ref, source_ref, bin_ref, near_ref, sum_ref, list_ref):
    place, speed = complete(size_y, first, 0, speed_ref, own_ref, target_ref, before_ref, source_ref, near_ref, sum_ref, list_ref)
    bin_ref[0] = place
    bin_ref[1] = speed


def above_kernel(size_y, first, last, keep_ref, bin_ref, speed_ref, own_ref, target_ref, before_ref, source_ref, place_out, speed_out, near_ref, sum_ref, list_ref):
    place, speed = complete(size_y, first, 1, speed_ref, own_ref, target_ref, before_ref, source_ref, near_ref, sum_ref, list_ref)
    for z, (moved, kicked) in enumerate(((bin_ref[0], bin_ref[1]), (place, speed))):
        if not last:
            place_out[z] = moved
            speed_out[z] = kicked
            continue
        keep = keep_ref[z, 0:1] > 0.0
        for c in range(3):
            place_out[c, 0, 0, z : z + 1, :] = jnp.where(keep, moved[c : c + 1], 0.0)
            speed_out[c, 0, 0, z : z + 1, :] = jnp.where(keep, kicked[c : c + 1], 0.0)


VMEM = pl.BlockSpec(memory_space=pltpu.VMEM)


def from_before(value, axis):
    size = lax.axis_size(axis)
    return lax.ppermute(value, axis, [(i, (i + 1) % size) for i in range(size)])


def from_after(value, axis):
    size = lax.axis_size(axis)
    return lax.ppermute(value, axis, [((i + 1) % size, i) for i in range(size)])


def call(kernel, inputs, outputs, sources, targets, slots, chunks):
    half = slots // 2
    heads = sources // 2 * 2
    return pl.pallas_call(
        kernel,
        out_shape=outputs,
        in_specs=[VMEM] * len(inputs),
        out_specs=tuple(VMEM for _ in outputs),
        scratch_shapes=[
            pltpu.VMEM((48, heads * half + chunks * slots), BF16),
            pltpu.VMEM((32, heads * half + chunks * slots), BF16),
            pltpu.VMEM((heads + 4, 8, half), F32),
        ],
        compiler_params=pltpu.CompilerParams(vmem_limit_bytes=24 * 1024 * 1024),
        cost_estimate=pl.CostEstimate(flops=sources * targets * slots * slots * 1000, bytes_accessed=1 << 18, transcendentals=0),
    )(*inputs)


def on_device(positions, velocities, mass, counts):
    slots = positions.shape[-1]
    size_y = lax.axis_size("gy")
    bins = jax.ShapeDtypeStruct((2, 4, slots), F32)
    full = jax.ShapeDtypeStruct(positions.shape, F32)
    running = jax.ShapeDtypeStruct((2, slots, 32), F32)
    packed, keep = pl.pallas_call(
        pack_kernel,
        out_shape=(bins, bins),
        in_specs=[VMEM] * 3,
        out_specs=(VMEM, VMEM),
    )(counts, positions, mass)
    speed = velocities
    for subcycle in range(SUBCYCLES):
        first, last = subcycle == 0, subcycle == SUBCYCLES - 1
        planes = [packed, from_before(packed, "gy")]
        if size_y > 2:
            planes.append(from_after(packed, "gy"))
        plane = jnp.stack(planes)
        right = from_after(plane, "gx")
        left = from_before(plane, "gx")
        targets, total = call(
            functools.partial(plane_kernel, size_y),
            planes,
            (jax.ShapeDtypeStruct((2, slots, 48), BF16), running),
            6, 2, slots, 2,
        )
        slab = jnp.stack([plane, left, right])
        below = from_before(slab[:, :, 1], "gz")
        above = from_after(slab[:, :, 0], "gz")
        (total,) = call(
            functools.partial(slab_kernel, size_y),
            [targets, total, left, right],
            (running,),
            12, 2, slots, 3,
        )
        state = [speed, packed, targets, total]
        (half_done,) = call(
            functools.partial(below_kernel, size_y, first),
            state + [below],
            (bins,),
            9, 1, slots, 3,
        )
        packed, speed = call(
            functools.partial(above_kernel, size_y, first, last),
            [keep, half_done] + state + [above],
            (full, full) if last else (bins, bins),
            9, 1, slots, 3,
        )
    return packed, speed


def solution(mesh):
    placed = (
        P(None, "gx", "gy", "gz", None),
        P(None, "gx", "gy", "gz", None),
        P("gx", "gy", "gz", None),
        P("gx", "gy", "gz"),
    )
    return jax.shard_map(
        on_device,
        mesh=mesh,
        in_specs=placed,
        out_specs=(P(None, "gx", "gy", "gz", None), P(None, "gx", "gy", "gz", None)),
        check_vma=False,
    )
```

```python
import functools

import jax
import jax.numpy as jnp
from jax import lax
from jax.experimental import pallas as pl
from jax.experimental.pallas import tpu as pltpu
from jax.sharding import PartitionSpec as P

SUBCYCLES = 2

time_step = 0.25

CENTRE = (0.5, 0.5, 1.0)
F32, BF16 = jnp.float32, jnp.bfloat16


def parts(value):
    high = value.astype(BF16).astype(F32)
    rest = value - high
    mid = rest.astype(BF16).astype(F32)
    return high, mid, rest - mid


def row_index(rows, slots):
    return lax.broadcasted_iota(jnp.int32, (rows, slots), 0)


def shifted(packed, offset):
    row = row_index(*packed.shape)
    x, y, z = [jnp.asarray(o, F32) - c for o, c in zip(offset, CENTRE)]
    move = jnp.where(row == 0, x, jnp.where(row == 1, y, jnp.where(row == 2, z, 0.0)))
    return packed + move


def source_rows(moved):
    row = row_index(*moved.shape)
    square = jnp.sum(jnp.where(row < 3, moved * moved, 0.0), axis=0, keepdims=True)
    head = jnp.where(row < 3, moved, square)
    tail = jnp.where(row == 0, 1.0, 0.0).astype(F32)
    high, mid, low = parts(jnp.concatenate([head, tail], axis=0))
    distance = jnp.concatenate([high, high, high, mid, mid, low], axis=0).astype(BF16)
    mass = moved[3:4]
    carried = jnp.where(row < 3, moved * mass, mass)
    high, mid, low = parts(jnp.concatenate([carried, jnp.zeros_like(carried)], axis=0))
    summed = jnp.concatenate([high, mid, low, jnp.zeros_like(low)], axis=0).astype(BF16)
    return distance, summed


def target_rows(moved):
    slots = moved.shape[-1]
    row = row_index(4, slots)
    square = jnp.sum(jnp.where(row < 3, moved * moved, 0.0), axis=0, keepdims=True)
    head = jnp.where(row < 3, 2.0 * moved, -1.0)
    tail = jnp.where(row == 0, 1.0 - square, 0.0)
    high, mid, low = parts(jnp.concatenate([head, tail], axis=0))
    return jnp.concatenate([high, mid, low, high, mid, high], axis=0).T.astype(BF16)


def pair_weight(target, source):
    near = jnp.maximum(jnp.dot(target, source, preferred_element_type=F32), 0.0)
    weight = near * near * near
    high = weight.astype(BF16)
    return high, (weight - high.astype(F32)).astype(BF16)


def contract(weights, rows):
    return lax.dot_general(weights, rows, (((1,), (1,)), ((), ())), preferred_element_type=F32)


def pack_kernel(counts_ref, place_ref, mass_ref, packed_ref, keep_ref):
    for z in range(2):
        mass = mass_ref[0, 0, z : z + 1, :]
        keep = lax.broadcasted_iota(jnp.int32, mass.shape, 1) < counts_ref[0, :, z : z + 1]
        rows = [place_ref[c, 0, 0, z : z + 1, :] for c in range(3)]
        packed_ref[z] = jnp.concatenate(rows + [jnp.where(keep, mass, 0.0)], axis=0)
        keep_ref[z] = jnp.broadcast_to(jnp.where(keep, 1.0, 0.0), keep_ref.shape[1:])


def ahead(axis):
    return 1 - 2 * lax.rem(lax.axis_index(axis), 2)


def y_shifts(size):
    if size == 2:
        return [[0], [-1, 1]]
    return [[0], [ahead("gy")], [-ahead("gy")]]


def list_chunk(list_ref, chunk):
    return jnp.concatenate([list_ref[2 * chunk], list_ref[2 * chunk + 1]], axis=1)[0:4]


def fill(near_ref, sum_ref, list_ref, entries):
    half = list_ref.shape[-1]
    lane = lax.broadcasted_iota(jnp.int32, (8, half), 1)
    list_ref[...] = jnp.zeros_like(list_ref)
    place = jnp.int32(0)
    held = {}
    for number, (ref, index, offset) in enumerate(entries):
        packed = ref[index]
        head, tail = shifted(packed[:, :half], offset), shifted(packed[:, half:], offset)
        if number == len(entries) - 1 and number % 2 == 0:
            list_ref[0] = jnp.concatenate([head, jnp.zeros_like(head)], axis=0)
        else:
            distance, summed = source_rows(head)
            near_ref[:, number * half : (number + 1) * half] = distance
            sum_ref[:, number * half : (number + 1) * half] = summed
        held[number] = tail
    if len(entries) % 2:
        place = place + half
    known = {}
    for number, (ref, index, offset) in enumerate(entries):
        tail = held[number]
        key = (id(ref),) + (index if isinstance(index, tuple) else (index,))
        if key not in known:
            present = jnp.where(tail[3:4] != 0.0, lane[0:1] + 1, 0).astype(F32)
            known[key] = jnp.max(present).astype(jnp.int32)
        length = known[key]
        tile, turn = lax.div(place, half), lax.rem(place, half)
        tail = jnp.where(lane < length, jnp.concatenate([tail, jnp.zeros_like(tail)], axis=0), 0.0)
        tail = pltpu.roll(tail, turn, 1)
        list_ref[tile] += jnp.where(lane >= turn, tail, 0.0)
        list_ref[tile + 1] += jnp.where(lane < turn, tail, 0.0)
        place = place + length
    done = (len(entries) // 2) * 2 * half
    for chunk in range((near_ref.shape[1] - done) // (2 * half)):
        distance, summed = source_rows(list_chunk(list_ref, chunk))
        near_ref[:, done + chunk * 2 * half : done + (chunk + 1) * 2 * half] = distance
        sum_ref[:, done + chunk * 2 * half : done + (chunk + 1) * 2 * half] = summed
    return place


def gathered(target, nears, sums):
    highs, lows = [], []
    for near in nears:
        high, low = pair_weight(target, near)
        highs.append(high)
        lows.append(low)
    rows = jnp.concatenate(sums, axis=1)
    return contract(jnp.concatenate(highs + lows, axis=1), jnp.concatenate([rows, rows], axis=1))


def sums_over(targets, totals, near_ref, sum_ref, list_ref, length, sources, tiles):
    wide = 2 * list_ref.shape[-1]
    steps = near_ref.shape[1] // (tiles * wide)

    def step(number, totals):
        nears, sums = [], []
        for tile in range(tiles):
            lanes = pl.ds(pl.multiple_of((number * tiles + tile) * wide, wide), wide)
            nears.append(near_ref[:, lanes])
            sums.append(sum_ref[:, lanes])
        return tuple(total + gathered(target, nears, sums) for target, total in zip(targets, totals))

    totals = step(0, totals) if steps == 1 else lax.fori_loop(0, steps, step, tuple(totals))
    done = steps * tiles - sources // 2

    def rest(number, totals):
        near, summed = source_rows(list_chunk(list_ref, number))
        return tuple(total + gathered(target, [near], [summed]) for target, total in zip(targets, totals))

    return lax.fori_loop(done, jnp.maximum(lax.div(length + (wide - 1), wide), done), rest, tuple(totals))


def plane_kernel(size_y, *refs):
    planes, (target_ref, total_ref, near_ref, sum_ref, list_ref) = refs[:-5], refs[-5:]
    own_ref = planes[0]
    for z in range(2):
        target_ref[z] = target_rows(shifted(own_ref[z], (0, 0, z)))
    entries = []
    for ref, shifts in zip(planes, y_shifts(size_y)):
        for y in shifts:
            entries += [(ref, z, (0, y, z)) for z in range(2)]
    length = fill(near_ref, sum_ref, list_ref, entries)
    zero = jnp.zeros(total_ref.shape[1:], F32)
    targets = [target_ref[z] for z in range(2)]
    totals = sums_over(targets, (zero, zero), near_ref, sum_ref, list_ref, length, len(entries), 5)
    for z in range(2):
        total_ref[z] = totals[z]


def slab_kernel(size_y, target_ref, before_ref, left_ref, right_ref, total_ref, near_ref, sum_ref, list_ref):
    entries = []
    for ref, x in ((left_ref, -1), (right_ref, 1)):
        for plane, shifts in enumerate(y_shifts(size_y)):
            for y in shifts:
                entries += [(ref, (plane, z), (x, y, z)) for z in range(2)]
    length = fill(near_ref, sum_ref, list_ref, entries)
    targets = [target_ref[z] for z in range(2)]
    totals = sums_over(targets, (before_ref[0], before_ref[1]), near_ref, sum_ref, list_ref, length, len(entries), 3)
    for z in range(2):
        total_ref[z] = totals[z]


def complete(size_y, first, z, speed_ref, own_ref, target_ref, before_ref, source_ref, near_ref, sum_ref, list_ref):
    entries = []
    for column, x in enumerate((0, -1, 1)):
        for plane, shifts in enumerate(y_shifts(size_y)):
            entries += [(source_ref, (column, plane), (x, y, 3 * z - 1)) for y in shifts]
    length = fill(near_ref, sum_ref, list_ref, entries)
    (total,) = sums_over([target_ref[z]], (before_ref[z],), near_ref, sum_ref, list_ref, length, len(entries), 7)
    total = total.T
    total = (total[0:8] + total[8:16] + total[16:24])[0:4]
    own = own_ref[z]
    accel = total - shifted(own, (0, 0, z)) * total[3:4]
    if first:
        rows = [jnp.where(z == 1, speed_ref[c, 0, 0, 1:2, :], speed_ref[c, 0, 0, 0:1, :]) for c in range(3)]
        speed = jnp.concatenate(rows + [jnp.zeros_like(rows[0])], axis=0)
    else:
        speed = speed_ref[z]
    speed = speed + time_step * accel
    place = jnp.clip(own + time_step * speed, 0.0, 1.0)
    return jnp.where(row_index(*own.shape) < 3, place, own), speed


def near_side():
    return (1 + ahead("gz")) // 2


def near_kernel(size_y, first, speed_ref, own_ref, target_ref, before_ref, source_ref, bin_ref, near_ref, sum_ref, list_ref):
    place, speed = complete(
        size_y, first, near_side(), speed_ref, own_ref, target_ref, before_ref, source_ref, near_ref, sum_ref, list_ref
    )
    bin_ref[0] = place
    bin_ref[1] = speed


def far_kernel(size_y, first, last, keep_ref, bin_ref, speed_ref, own_ref, target_ref, before_ref, source_ref, place_out, speed_out, near_ref, sum_ref, list_ref):
    other = near_side()
    z = 1 - other
    place, speed = complete(
        size_y, first, z, speed_ref, own_ref, target_ref, before_ref, source_ref, near_ref, sum_ref, list_ref
    )
    if not last:
        place_out[z] = place
        speed_out[z] = speed
        place_out[other] = bin_ref[0]
        speed_out[other] = bin_ref[1]
        return
    for side in range(2):
        keep = keep_ref[side, 0:1] > 0.0
        moved = jnp.where(z == side, place, bin_ref[0])
        kicked = jnp.where(z == side, speed, bin_ref[1])
        for c in range(3):
            place_out[c, 0, 0, side : side + 1, :] = jnp.where(keep, moved[c : c + 1], 0.0)
            speed_out[c, 0, 0, side : side + 1, :] = jnp.where(keep, kicked[c : c + 1], 0.0)


VMEM = pl.BlockSpec(memory_space=pltpu.VMEM)


def swaps(axis):
    size = lax.axis_size(axis)
    near = [(i, i ^ 1) for i in range(size)]
    far = [(i, (((i + 1) ^ 1) - 1) % size) for i in range(size)]
    return near, far


def shift(axis, step):
    size = lax.axis_size(axis)
    return [(i, (i + step) % size) for i in range(size)]


def call(kernel, inputs, outputs, sources, targets, slots, chunks):
    half = slots // 2
    heads = sources // 2 * 2
    return pl.pallas_call(
        kernel,
        out_shape=outputs,
        in_specs=[VMEM] * len(inputs),
        out_specs=tuple(VMEM for _ in outputs),
        scratch_shapes=[
            pltpu.VMEM((48, heads * half + chunks * slots), BF16),
            pltpu.VMEM((32, heads * half + chunks * slots), BF16),
            pltpu.VMEM((heads + 4, 8, half), F32),
        ],
        compiler_params=pltpu.CompilerParams(vmem_limit_bytes=24 * 1024 * 1024),
        cost_estimate=pl.CostEstimate(flops=sources * targets * slots * slots * 1000, bytes_accessed=1 << 18, transcendentals=0),
    )(*inputs)


def on_device(positions, velocities, mass, counts):
    slots = positions.shape[-1]
    size_y = lax.axis_size("gy")
    bins = jax.ShapeDtypeStruct((2, 4, slots), F32)
    full = jax.ShapeDtypeStruct(positions.shape, F32)
    running = jax.ShapeDtypeStruct((2, slots, 32), F32)
    packed, keep = pl.pallas_call(
        pack_kernel,
        out_shape=(bins, bins),
        in_specs=[VMEM] * 3,
        out_specs=(VMEM, VMEM),
    )(counts, positions, mass)
    speed = velocities
    upper = lax.rem(lax.axis_index("gz"), 2)
    for subcycle in range(SUBCYCLES):
        first, last = subcycle == 0, subcycle == SUBCYCLES - 1
        near, far = swaps("gy")
        planes = [packed]
        if size_y > 2:
            other = lax.ppermute(packed, "gy", far)
            planes += [lax.ppermute(packed, "gy", near), other]
        else:
            planes.append(lax.ppermute(packed, "gy", near))
        plane = jnp.stack(planes)
        right = lax.ppermute(plane, "gx", shift("gx", -1))
        left = lax.ppermute(plane, "gx", shift("gx", 1))
        targets, total = call(
            functools.partial(plane_kernel, size_y),
            planes,
            (jax.ShapeDtypeStruct((2, slots, 48), BF16), running),
            6, 2, slots, 2,
        )
        slab = jnp.stack([plane, left, right])
        near, far = swaps("gz")
        far_z = lax.ppermute(lax.dynamic_index_in_dim(slab, upper, 2, False), "gz", far)
        near_z = lax.ppermute(lax.dynamic_index_in_dim(slab, 1 - upper, 2, False), "gz", near)
        (total,) = call(
            functools.partial(slab_kernel, size_y),
            [targets, total, left, right],
            (running,),
            12, 2, slots, 3,
        )
        state = [speed, packed, targets, total]
        (half_done,) = call(
            functools.partial(near_kernel, size_y, first),
            state + [near_z],
            (bins,),
            9, 1, slots, 3,
        )
        packed, speed = call(
            functools.partial(far_kernel, size_y, first, last),
            [keep, half_done] + state + [far_z],
            (full, full) if last else (bins, bins),
            9, 1, slots, 3,
        )
    return packed, speed


def solution(mesh):
    placed = (
        P(None, "gx", "gy", "gz", None),
        P(None, "gx", "gy", "gz", None),
        P("gx", "gy", "gz", None),
        P("gx", "gy", "gz"),
    )
    return jax.shard_map(
        on_device,
        mesh=mesh,
        in_specs=placed,
        out_specs=(P(None, "gx", "gy", "gz", None), P(None, "gx", "gy", "gz", None)),
        check_vma=False,
    )
```

```python
import functools

import jax
import jax.numpy as jnp
from jax import lax
from jax.experimental import pallas as pl
from jax.experimental.pallas import tpu as pltpu
from jax.sharding import PartitionSpec as P

SUBCYCLES = 2

time_step = 0.25

CENTRE = (0.5, 0.5, 1.0)
F32, BF16 = jnp.float32, jnp.bfloat16


def parts(value):
    high = value.astype(BF16).astype(F32)
    rest = value - high
    mid = rest.astype(BF16).astype(F32)
    return high, mid, rest - mid


def row_index(rows, slots):
    return lax.broadcasted_iota(jnp.int32, (rows, slots), 0)


def shifted(packed, offset):
    row = row_index(*packed.shape)
    x, y, z = [jnp.asarray(o, F32) - c for o, c in zip(offset, CENTRE)]
    move = jnp.where(row == 0, x, jnp.where(row == 1, y, jnp.where(row == 2, z, 0.0)))
    return packed + move


def source_rows(moved):
    row = row_index(*moved.shape)
    square = jnp.sum(jnp.where(row < 3, moved * moved, 0.0), axis=0, keepdims=True)
    head = jnp.where(row < 3, moved, square)
    tail = jnp.where(row == 0, 1.0, 0.0).astype(F32)
    high, mid, low = parts(jnp.concatenate([head, tail], axis=0))
    distance = jnp.concatenate([high, high, high, mid, mid, low], axis=0).astype(BF16)
    mass = moved[3:4]
    carried = jnp.where(row < 3, moved * mass, mass)
    high, mid, low = parts(jnp.concatenate([carried, jnp.zeros_like(carried)], axis=0))
    summed = jnp.concatenate([high, mid, low, jnp.zeros_like(low)], axis=0).astype(BF16)
    return distance, summed


def target_rows(moved):
    slots = moved.shape[-1]
    row = row_index(4, slots)
    square = jnp.sum(jnp.where(row < 3, moved * moved, 0.0), axis=0, keepdims=True)
    head = jnp.where(row < 3, 2.0 * moved, -1.0)
    tail = jnp.where(row == 0, 1.0 - square, 0.0)
    high, mid, low = parts(jnp.concatenate([head, tail], axis=0))
    return jnp.concatenate([high, mid, low, high, mid, high], axis=0).T.astype(BF16)


def pair_weight(target, source):
    near = jnp.maximum(jnp.dot(target, source, preferred_element_type=F32), 0.0)
    weight = near * near * near
    high = weight.astype(BF16)
    return high, (weight - high.astype(F32)).astype(BF16)


def contract(weights, rows):
    return lax.dot_general(weights, rows, (((1,), (1,)), ((), ())), preferred_element_type=F32)


def pack_kernel(counts_ref, place_ref, mass_ref, packed_ref, keep_ref):
    for z in range(2):
        mass = mass_ref[0, 0, z : z + 1, :]
        keep = lax.broadcasted_iota(jnp.int32, mass.shape, 1) < counts_ref[0, :, z : z + 1]
        rows = [place_ref[c, 0, 0, z : z + 1, :] for c in range(3)]
        packed_ref[z] = jnp.concatenate(rows + [jnp.where(keep, mass, 0.0)], axis=0)
        keep_ref[z] = jnp.broadcast_to(jnp.where(keep, 1.0, 0.0), keep_ref.shape[1:])


def ahead(axis):
    return 1 - 2 * lax.rem(lax.axis_index(axis), 2)


def y_shifts(size):
    if size == 2:
        return [[0], [-1, 1]]
    return [[0], [ahead("gy")], [-ahead("gy")]]


def list_chunk(list_ref, chunk):
    return jnp.concatenate([list_ref[2 * chunk], list_ref[2 * chunk + 1]], axis=1)[0:4]


def fill(near_ref, sum_ref, list_ref, entries):
    half = list_ref.shape[-1]
    lane = lax.broadcasted_iota(jnp.int32, (8, half), 1)
    list_ref[...] = jnp.zeros_like(list_ref)
    place = jnp.int32(0)
    held = {}
    for number, (ref, index, offset) in enumerate(entries):
        packed = ref[index]
        head, tail = shifted(packed[:, :half], offset), shifted(packed[:, half:], offset)
        if number == len(entries) - 1 and number % 2 == 0:
            list_ref[0] = jnp.concatenate([head, jnp.zeros_like(head)], axis=0)
        else:
            distance, summed = source_rows(head)
            near_ref[:, number * half : (number + 1) * half] = distance
            sum_ref[:, number * half : (number + 1) * half] = summed
        held[number] = tail
    if len(entries) % 2:
        place = place + half
    known = {}
    for number, (ref, index, offset) in enumerate(entries):
        tail = held[number]
        key = (id(ref),) + (index if isinstance(index, tuple) else (index,))
        if key not in known:
            present = jnp.where(tail[3:4] != 0.0, lane[0:1] + 1, 0).astype(F32)
            known[key] = jnp.max(present).astype(jnp.int32)
        length = known[key]
        tile, turn = lax.div(place, half), lax.rem(place, half)
        tail = jnp.where(lane < length, jnp.concatenate([tail, jnp.zeros_like(tail)], axis=0), 0.0)
        tail = pltpu.roll(tail, turn, 1)
        list_ref[tile] += jnp.where(lane >= turn, tail, 0.0)
        list_ref[tile + 1] += jnp.where(lane < turn, tail, 0.0)
        place = place + length
    done = (len(entries) // 2) * 2 * half
    for chunk in range((near_ref.shape[1] - done) // (2 * half)):
        distance, summed = source_rows(list_chunk(list_ref, chunk))
        near_ref[:, done + chunk * 2 * half : done + (chunk + 1) * 2 * half] = distance
        sum_ref[:, done + chunk * 2 * half : done + (chunk + 1) * 2 * half] = summed
    return place


def gathered(target, nears, sums):
    highs, lows = [], []
    for near in nears:
        high, low = pair_weight(target, near)
        highs.append(high)
        lows.append(low)
    rows = jnp.concatenate(sums, axis=1)
    return contract(jnp.concatenate(highs + lows, axis=1), jnp.concatenate([rows, rows], axis=1))


def sums_over(targets, totals, near_ref, sum_ref, list_ref, length, sources, tiles):
    wide = 2 * list_ref.shape[-1]
    steps = near_ref.shape[1] // (tiles * wide)

    def step(number, totals):
        nears, sums = [], []
        for tile in range(tiles):
            lanes = pl.ds(pl.multiple_of((number * tiles + tile) * wide, wide), wide)
            nears.append(near_ref[:, lanes])
            sums.append(sum_ref[:, lanes])
        return tuple(total + gathered(target, nears, sums) for target, total in zip(targets, totals))

    totals = step(0, totals) if steps == 1 else lax.fori_loop(0, steps, step, tuple(totals))
    done = steps * tiles - sources // 2

    def rest(number, totals):
        near, summed = source_rows(list_chunk(list_ref, number))
        return tuple(total + gathered(target, [near], [summed]) for target, total in zip(targets, totals))

    return lax.fori_loop(done, jnp.maximum(lax.div(length + (wide - 1), wide), done), rest, tuple(totals))


def plane_kernel(size_y, *refs):
    planes, (target_ref, total_ref, near_ref, sum_ref, list_ref) = refs[:-5], refs[-5:]
    own_ref = planes[0]
    for z in range(2):
        target_ref[z] = target_rows(shifted(own_ref[z], (0, 0, z)))
    entries = []
    for ref, shifts in zip(planes, y_shifts(size_y)):
        for y in shifts:
            entries += [(ref, z, (0, y, z)) for z in range(2)]
    length = fill(near_ref, sum_ref, list_ref, entries)
    zero = jnp.zeros(total_ref.shape[1:], F32)
    targets = [target_ref[z] for z in range(2)]
    totals = sums_over(targets, (zero, zero), near_ref, sum_ref, list_ref, length, len(entries), 5)
    for z in range(2):
        total_ref[z] = totals[z]


def slab_kernel(size_y, target_ref, before_ref, near_x_ref, far_x_ref, total_ref, near_ref, sum_ref, list_ref):
    entries = []
    for ref, x in ((near_x_ref, ahead("gx")), (far_x_ref, -ahead("gx"))):
        for plane, shifts in enumerate(y_shifts(size_y)):
            for y in shifts:
                entries += [(ref, (plane, z), (x, y, z)) for z in range(2)]
    length = fill(near_ref, sum_ref, list_ref, entries)
    targets = [target_ref[z] for z in range(2)]
    totals = sums_over(targets, (before_ref[0], before_ref[1]), near_ref, sum_ref, list_ref, length, len(entries), 9)
    for z in range(2):
        total_ref[z] = totals[z]


def complete(size_y, first, z, speed_ref, own_ref, target_ref, before_ref, source_ref, near_ref, sum_ref, list_ref):
    entries = []
    for column, x in enumerate((0, ahead("gx"), -ahead("gx"))):
        for plane, shifts in enumerate(y_shifts(size_y)):
            entries += [(source_ref, (column, plane), (x, y, 3 * z - 1)) for y in shifts]
    length = fill(near_ref, sum_ref, list_ref, entries)
    (total,) = sums_over([target_ref[z]], (before_ref[z],), near_ref, sum_ref, list_ref, length, len(entries), 7)
    total = total.T
    total = (total[0:8] + total[8:16] + total[16:24])[0:4]
    own = own_ref[z]
    accel = total - shifted(own, (0, 0, z)) * total[3:4]
    if first:
        rows = [jnp.where(z == 1, speed_ref[c, 0, 0, 1:2, :], speed_ref[c, 0, 0, 0:1, :]) for c in range(3)]
        speed = jnp.concatenate(rows + [jnp.zeros_like(rows[0])], axis=0)
    else:
        speed = speed_ref[z]
    speed = speed + time_step * accel
    place = jnp.clip(own + time_step * speed, 0.0, 1.0)
    return jnp.where(row_index(*own.shape) < 3, place, own), speed


def near_side():
    return (1 + ahead("gz")) // 2


def near_kernel(size_y, first, speed_ref, own_ref, target_ref, before_ref, source_ref, bin_ref, near_ref, sum_ref, list_ref):
    place, speed = complete(
        size_y, first, near_side(), speed_ref, own_ref, target_ref, before_ref, source_ref, near_ref, sum_ref, list_ref
    )
    bin_ref[0] = place
    bin_ref[1] = speed


def far_kernel(size_y, first, last, keep_ref, bin_ref, speed_ref, own_ref, target_ref, before_ref, source_ref, place_out, speed_out, near_ref, sum_ref, list_ref):
    other = near_side()
    z = 1 - other
    place, speed = complete(
        size_y, first, z, speed_ref, own_ref, target_ref, before_ref, source_ref, near_ref, sum_ref, list_ref
    )
    if not last:
        place_out[z] = place
        speed_out[z] = speed
        place_out[other] = bin_ref[0]
        speed_out[other] = bin_ref[1]
        return
    for side in range(2):
        keep = keep_ref[side, 0:1] > 0.0
        moved = jnp.where(z == side, place, bin_ref[0])
        kicked = jnp.where(z == side, speed, bin_ref[1])
        for c in range(3):
            place_out[c, 0, 0, side : side + 1, :] = jnp.where(keep, moved[c : c + 1], 0.0)
            speed_out[c, 0, 0, side : side + 1, :] = jnp.where(keep, kicked[c : c + 1], 0.0)


VMEM = pl.BlockSpec(memory_space=pltpu.VMEM)


def swaps(axis):
    size = lax.axis_size(axis)
    near = [(i, i ^ 1) for i in range(size)]
    far = [(i, (((i + 1) ^ 1) - 1) % size) for i in range(size)]
    return near, far


def call(kernel, inputs, outputs, sources, targets, slots, chunks):
    half = slots // 2
    heads = sources // 2 * 2
    return pl.pallas_call(
        kernel,
        out_shape=outputs,
        in_specs=[VMEM] * len(inputs),
        out_specs=tuple(VMEM for _ in outputs),
        scratch_shapes=[
            pltpu.VMEM((48, heads * half + chunks * slots), BF16),
            pltpu.VMEM((32, heads * half + chunks * slots), BF16),
            pltpu.VMEM((heads + 4, 8, half), F32),
        ],
        compiler_params=pltpu.CompilerParams(vmem_limit_bytes=24 * 1024 * 1024),
        cost_estimate=pl.CostEstimate(flops=sources * targets * slots * slots * 1000, bytes_accessed=1 << 18, transcendentals=0),
    )(*inputs)


def on_device(positions, velocities, mass, counts):
    slots = positions.shape[-1]
    size_y = lax.axis_size("gy")
    bins = jax.ShapeDtypeStruct((2, 4, slots), F32)
    full = jax.ShapeDtypeStruct(positions.shape, F32)
    running = jax.ShapeDtypeStruct((2, slots, 32), F32)
    packed, keep = pl.pallas_call(
        pack_kernel,
        out_shape=(bins, bins),
        in_specs=[VMEM] * 3,
        out_specs=(VMEM, VMEM),
    )(counts, positions, mass)
    speed = velocities
    upper = lax.rem(lax.axis_index("gz"), 2)
    for subcycle in range(SUBCYCLES):
        first, last = subcycle == 0, subcycle == SUBCYCLES - 1
        near, far = swaps("gy")
        planes = [packed]
        if size_y > 2:
            other = lax.ppermute(packed, "gy", far)
            planes += [lax.ppermute(packed, "gy", near), other]
        else:
            planes.append(lax.ppermute(packed, "gy", near))
        plane = jnp.stack(planes)
        near, far = swaps("gx")
        near_x = lax.ppermute(plane, "gx", near)
        far_x = lax.ppermute(plane, "gx", far)
        targets, total = call(
            functools.partial(plane_kernel, size_y),
            planes,
            (jax.ShapeDtypeStruct((2, slots, 48), BF16), running),
            6, 2, slots, 2,
        )
        slab = jnp.stack([plane, near_x, far_x])
        near, far = swaps("gz")
        far_z = lax.ppermute(lax.dynamic_index_in_dim(slab, upper, 2, False), "gz", far)
        near_z = lax.ppermute(lax.dynamic_index_in_dim(slab, 1 - upper, 2, False), "gz", near)
        (total,) = call(
            functools.partial(slab_kernel, size_y),
            [targets, total, near_x, far_x],
            (running,),
            12, 2, slots, 3,
        )
        state = [speed, packed, targets, total]
        (half_done,) = call(
            functools.partial(near_kernel, size_y, first),
            state + [near_z],
            (bins,),
            9, 1, slots, 3,
        )
        packed, speed = call(
            functools.partial(far_kernel, size_y, first, last),
            [keep, half_done] + state + [far_z],
            (full, full) if last else (bins, bins),
            9, 1, slots, 3,
        )
    return packed, speed


def solution(mesh):
    placed = (
        P(None, "gx", "gy", "gz", None),
        P(None, "gx", "gy", "gz", None),
        P("gx", "gy", "gz", None),
        P("gx", "gy", "gz"),
    )
    return jax.shard_map(
        on_device,
        mesh=mesh,
        in_specs=placed,
        out_specs=(P(None, "gx", "gy", "gz", None), P(None, "gx", "gy", "gz", None)),
        check_vma=False,
    )
```

```python
import functools

import jax
import jax.numpy as jnp
from jax import lax
from jax.experimental import pallas as pl
from jax.experimental.pallas import tpu as pltpu
from jax.sharding import PartitionSpec as P

SUBCYCLES = 2

time_step = 0.25

CENTRE = (0.5, 0.5, 1.0)
F32, BF16 = jnp.float32, jnp.bfloat16


def parts(value):
    high = value.astype(BF16).astype(F32)
    rest = value - high
    mid = rest.astype(BF16).astype(F32)
    return high, mid, rest - mid


def row_index(rows, slots):
    return lax.broadcasted_iota(jnp.int32, (rows, slots), 0)


def shifted(packed, offset):
    row = row_index(*packed.shape)
    x, y, z = [jnp.asarray(o, F32) - c for o, c in zip(offset, CENTRE)]
    move = jnp.where(row == 0, x, jnp.where(row == 1, y, jnp.where(row == 2, z, 0.0)))
    return packed + move


def source_rows(moved):
    row = row_index(*moved.shape)
    square = jnp.sum(jnp.where(row < 3, moved * moved, 0.0), axis=0, keepdims=True)
    head = jnp.where(row < 3, moved, square)
    tail = jnp.where(row == 0, 1.0, 0.0).astype(F32)
    high, mid, low = parts(jnp.concatenate([head, tail], axis=0))
    distance = jnp.concatenate([high, high, high, mid, mid, low], axis=0).astype(BF16)
    mass = moved[3:4]
    carried = jnp.where(row < 3, moved * mass, mass)
    high, mid, low = parts(jnp.concatenate([carried, jnp.zeros_like(carried)], axis=0))
    summed = jnp.concatenate([high, mid, low, jnp.zeros_like(low)], axis=0).astype(BF16)
    return distance, summed


def target_rows(moved):
    slots = moved.shape[-1]
    row = row_index(4, slots)
    square = jnp.sum(jnp.where(row < 3, moved * moved, 0.0), axis=0, keepdims=True)
    head = jnp.where(row < 3, 2.0 * moved, -1.0)
    tail = jnp.where(row == 0, 1.0 - square, 0.0)
    high, mid, low = parts(jnp.concatenate([head, tail], axis=0))
    return jnp.concatenate([high, mid, low, high, mid, high], axis=0).T.astype(BF16)


def pair_weight(target, source):
    near = jnp.maximum(jnp.dot(target, source, preferred_element_type=F32), 0.0)
    weight = near * near * near
    high = weight.astype(BF16)
    return high, (weight - high.astype(F32)).astype(BF16)


def contract(weights, rows):
    return lax.dot_general(weights, rows, (((1,), (1,)), ((), ())), preferred_element_type=F32)


def pack_kernel(counts_ref, place_ref, mass_ref, packed_ref, keep_ref):
    for z in range(2):
        mass = mass_ref[0, 0, z : z + 1, :]
        keep = lax.broadcasted_iota(jnp.int32, mass.shape, 1) < counts_ref[0, :, z : z + 1]
        rows = [place_ref[c, 0, 0, z : z + 1, :] for c in range(3)]
        packed_ref[z] = jnp.concatenate(rows + [jnp.where(keep, mass, 0.0)], axis=0)
        keep_ref[z] = jnp.broadcast_to(jnp.where(keep, 1.0, 0.0), keep_ref.shape[1:])


def ahead(axis):
    return 1 - 2 * lax.rem(lax.axis_index(axis), 2)


def y_shifts(size):
    if size == 2:
        return [[0], [-1, 1]]
    return [[0], [ahead("gy")], [-ahead("gy")]]


def list_chunk(list_ref, chunk):
    return jnp.concatenate([list_ref[2 * chunk], list_ref[2 * chunk + 1]], axis=1)[0:4]


def fill(near_ref, sum_ref, list_ref, entries):
    half = list_ref.shape[-1]
    lane = lax.broadcasted_iota(jnp.int32, (8, half), 1)
    list_ref[...] = jnp.zeros_like(list_ref)
    place = jnp.int32(0)
    held = {}
    for number, (ref, index, offset) in enumerate(entries):
        packed = ref[index]
        head, tail = shifted(packed[:, :half], offset), shifted(packed[:, half:], offset)
        if number == len(entries) - 1 and number % 2 == 0:
            list_ref[0] = jnp.concatenate([head, jnp.zeros_like(head)], axis=0)
        else:
            distance, summed = source_rows(head)
            near_ref[:, number * half : (number + 1) * half] = distance
            sum_ref[:, number * half : (number + 1) * half] = summed
        held[number] = tail
    if len(entries) % 2:
        place = place + half
    known = {}
    for number, (ref, index, offset) in enumerate(entries):
        tail = held[number]
        key = (id(ref),) + (index if isinstance(index, tuple) else (index,))
        if key not in known:
            present = jnp.where(tail[3:4] != 0.0, lane[0:1] + 1, 0).astype(F32)
            known[key] = jnp.max(present).astype(jnp.int32)
        length = known[key]
        tile, turn = lax.div(place, half), lax.rem(place, half)
        tail = jnp.where(lane < length, jnp.concatenate([tail, jnp.zeros_like(tail)], axis=0), 0.0)
        tail = pltpu.roll(tail, turn, 1)
        list_ref[tile] += jnp.where(lane >= turn, tail, 0.0)
        list_ref[tile + 1] += jnp.where(lane < turn, tail, 0.0)
        place = place + length
    done = (len(entries) // 2) * 2 * half
    for chunk in range((near_ref.shape[1] - done) // (2 * half)):
        distance, summed = source_rows(list_chunk(list_ref, chunk))
        near_ref[:, done + chunk * 2 * half : done + (chunk + 1) * 2 * half] = distance
        sum_ref[:, done + chunk * 2 * half : done + (chunk + 1) * 2 * half] = summed
    return place


def gathered(target, nears, sums):
    highs, lows = [], []
    for near in nears:
        high, low = pair_weight(target, near)
        highs.append(high)
        lows.append(low)
    rows = jnp.concatenate(sums, axis=1)
    return contract(jnp.concatenate(highs + lows, axis=1), jnp.concatenate([rows, rows], axis=1))


def sums_over(targets, totals, near_ref, sum_ref, list_ref, length, sources, tiles):
    wide = 2 * list_ref.shape[-1]
    steps = near_ref.shape[1] // (tiles * wide)

    def step(number, totals):
        nears, sums = [], []
        for tile in range(tiles):
            lanes = pl.ds(pl.multiple_of((number * tiles + tile) * wide, wide), wide)
            nears.append(near_ref[:, lanes])
            sums.append(sum_ref[:, lanes])
        return tuple(total + gathered(target, nears, sums) for target, total in zip(targets, totals))

    totals = step(0, totals) if steps == 1 else lax.fori_loop(0, steps, step, tuple(totals))
    done = steps * tiles - sources // 2

    def rest(number, totals):
        near, summed = source_rows(list_chunk(list_ref, number))
        return tuple(total + gathered(target, [near], [summed]) for target, total in zip(targets, totals))

    return lax.fori_loop(done, jnp.maximum(lax.div(length + (wide - 1), wide), done), rest, tuple(totals))


def plane_kernel(size_y, *refs):
    planes, (target_ref, total_ref, near_ref, sum_ref, list_ref) = refs[:-5], refs[-5:]
    own_ref = planes[0]
    for z in range(2):
        target_ref[z] = target_rows(shifted(own_ref[z], (0, 0, z)))
    entries = []
    for ref, shifts in zip(planes, y_shifts(size_y)):
        for y in shifts:
            entries += [(ref, z, (0, y, z)) for z in range(2)]
    length = fill(near_ref, sum_ref, list_ref, entries)
    zero = jnp.zeros(total_ref.shape[1:], F32)
    targets = [target_ref[z] for z in range(2)]
    totals = sums_over(targets, (zero, zero), near_ref, sum_ref, list_ref, length, len(entries), 5)
    for z in range(2):
        total_ref[z] = totals[z]


def slab_kernel(size_y, target_ref, before_ref, near_x_ref, *refs):
    far_refs, (total_ref, near_ref, sum_ref, list_ref) = refs[:-4], refs[-4:]
    entries = []
    for plane, shifts in enumerate(y_shifts(size_y)):
        for y in shifts:
            entries += [(near_x_ref, (plane, z), (ahead("gx"), y, z)) for z in range(2)]
            entries += [(far_refs[plane], z, (-ahead("gx"), y, z)) for z in range(2)]
    length = fill(near_ref, sum_ref, list_ref, entries)
    targets = [target_ref[z] for z in range(2)]
    totals = sums_over(targets, (before_ref[0], before_ref[1]), near_ref, sum_ref, list_ref, length, len(entries), 9)
    for z in range(2):
        total_ref[z] = totals[z]


def complete(size_y, first, z, speed_ref, own_ref, target_ref, before_ref, source_ref, near_ref, sum_ref, list_ref):
    entries = []
    for column, x in enumerate((0, ahead("gx"), -ahead("gx"))):
        for plane, shifts in enumerate(y_shifts(size_y)):
            index = column * len(y_shifts(size_y)) + plane
            entries += [(source_ref, index, (x, y, 3 * z - 1)) for y in shifts]
    length = fill(near_ref, sum_ref, list_ref, entries)
    (total,) = sums_over([target_ref[z]], (before_ref[z],), near_ref, sum_ref, list_ref, length, len(entries), 7)
    total = total.T
    total = (total[0:8] + total[8:16] + total[16:24])[0:4]
    own = own_ref[z]
    accel = total - shifted(own, (0, 0, z)) * total[3:4]
    if first:
        rows = [jnp.where(z == 1, speed_ref[c, 0, 0, 1:2, :], speed_ref[c, 0, 0, 0:1, :]) for c in range(3)]
        speed = jnp.concatenate(rows + [jnp.zeros_like(rows[0])], axis=0)
    else:
        speed = speed_ref[z]
    speed = speed + time_step * accel
    place = jnp.clip(own + time_step * speed, 0.0, 1.0)
    return jnp.where(row_index(*own.shape) < 3, place, own), speed


def near_side():
    return (1 + ahead("gz")) // 2


def near_kernel(size_y, first, speed_ref, own_ref, target_ref, before_ref, source_ref, bin_ref, near_ref, sum_ref, list_ref):
    place, speed = complete(
        size_y, first, near_side(), speed_ref, own_ref, target_ref, before_ref, source_ref, near_ref, sum_ref, list_ref
    )
    bin_ref[0] = place
    bin_ref[1] = speed


def far_kernel(size_y, first, last, keep_ref, bin_ref, speed_ref, own_ref, target_ref, before_ref, source_ref, place_out, speed_out, near_ref, sum_ref, list_ref):
    other = near_side()
    z = 1 - other
    place, speed = complete(
        size_y, first, z, speed_ref, own_ref, target_ref, before_ref, source_ref, near_ref, sum_ref, list_ref
    )
    if not last:
        place_out[z] = place
        speed_out[z] = speed
        place_out[other] = bin_ref[0]
        speed_out[other] = bin_ref[1]
        return
    for side in range(2):
        keep = keep_ref[side, 0:1] > 0.0
        moved = jnp.where(z == side, place, bin_ref[0])
        kicked = jnp.where(z == side, speed, bin_ref[1])
        for c in range(3):
            place_out[c, 0, 0, side : side + 1, :] = jnp.where(keep, moved[c : c + 1], 0.0)
            speed_out[c, 0, 0, side : side + 1, :] = jnp.where(keep, kicked[c : c + 1], 0.0)


VMEM = pl.BlockSpec(memory_space=pltpu.VMEM)


def swaps(axis):
    size = lax.axis_size(axis)
    near = [(i, i ^ 1) for i in range(size)]
    far = [(i, (((i + 1) ^ 1) - 1) % size) for i in range(size)]
    return near, far


def across(value, path_x, path_y):
    size_y = lax.axis_size("gy")
    pairs = [(x * size_y + y, to_x * size_y + to_y) for x, to_x in path_x for y, to_y in path_y]
    return lax.ppermute(value, ("gx", "gy"), pairs)


def call(kernel, inputs, outputs, sources, targets, slots, chunks):
    half = slots // 2
    heads = sources // 2 * 2
    return pl.pallas_call(
        kernel,
        out_shape=outputs,
        in_specs=[VMEM] * len(inputs),
        out_specs=tuple(VMEM for _ in outputs),
        scratch_shapes=[
            pltpu.VMEM((48, heads * half + chunks * slots), BF16),
            pltpu.VMEM((32, heads * half + chunks * slots), BF16),
            pltpu.VMEM((heads + 4, 8, half), F32),
        ],
        compiler_params=pltpu.CompilerParams(vmem_limit_bytes=24 * 1024 * 1024),
        cost_estimate=pl.CostEstimate(flops=sources * targets * slots * slots * 1000, bytes_accessed=1 << 18, transcendentals=0),
    )(*inputs)


def on_device(positions, velocities, mass, counts):
    slots = positions.shape[-1]
    size_y = lax.axis_size("gy")
    bins = jax.ShapeDtypeStruct((2, 4, slots), F32)
    full = jax.ShapeDtypeStruct(positions.shape, F32)
    running = jax.ShapeDtypeStruct((2, slots, 32), F32)
    packed, keep = pl.pallas_call(
        pack_kernel,
        out_shape=(bins, bins),
        in_specs=[VMEM] * 3,
        out_specs=(VMEM, VMEM),
    )(counts, positions, mass)
    speed = velocities
    upper = lax.rem(lax.axis_index("gz"), 2)
    for subcycle in range(SUBCYCLES):
        first, last = subcycle == 0, subcycle == SUBCYCLES - 1
        paths = swaps("gy")[: min(size_y, 3) - 1]
        planes = [packed] + [lax.ppermute(packed, "gy", path) for path in paths]
        near, far = swaps("gx")
        far_planes = [lax.ppermute(packed, "gx", far)] + [across(packed, far, path) for path in paths]
        plane = jnp.stack(planes)
        near_x = lax.ppermute(plane, "gx", near)
        targets, total = call(
            functools.partial(plane_kernel, size_y),
            planes,
            (jax.ShapeDtypeStruct((2, slots, 48), BF16), running),
            6, 2, slots, 2,
        )
        slab = jnp.concatenate([plane, near_x] + [value[None] for value in far_planes], axis=0)
        near, far = swaps("gz")
        far_z = lax.ppermute(lax.dynamic_index_in_dim(slab, upper, 1, False), "gz", far)
        near_z = lax.ppermute(lax.dynamic_index_in_dim(slab, 1 - upper, 1, False), "gz", near)
        (total,) = call(
            functools.partial(slab_kernel, size_y),
            [targets, total, near_x] + far_planes,
            (running,),
            12, 2, slots, 3,
        )
        state = [speed, packed, targets, total]
        (half_done,) = call(
            functools.partial(near_kernel, size_y, first),
            state + [near_z],
            (bins,),
            9, 1, slots, 3,
        )
        packed, speed = call(
            functools.partial(far_kernel, size_y, first, last),
            [keep, half_done] + state + [far_z],
            (full, full) if last else (bins, bins),
            9, 1, slots, 3,
        )
    return packed, speed


def solution(mesh):
    placed = (
        P(None, "gx", "gy", "gz", None),
        P(None, "gx", "gy", "gz", None),
        P("gx", "gy", "gz", None),
        P("gx", "gy", "gz"),
    )
    return jax.shard_map(
        on_device,
        mesh=mesh,
        in_specs=placed,
        out_specs=(P(None, "gx", "gy", "gz", None), P(None, "gx", "gy", "gz", None)),
        check_vma=False,
    )
```

```python
import functools

import jax
import jax.numpy as jnp
from jax import lax
from jax.experimental import pallas as pl
from jax.experimental.pallas import tpu as pltpu
from jax.sharding import PartitionSpec as P

SUBCYCLES = 2

time_step = 0.25

CENTRE = (0.5, 0.5, 1.0)
F32, BF16 = jnp.float32, jnp.bfloat16


def parts(value):
    high = value.astype(BF16).astype(F32)
    rest = value - high
    mid = rest.astype(BF16).astype(F32)
    return high, mid, rest - mid


def row_index(rows, slots):
    return lax.broadcasted_iota(jnp.int32, (rows, slots), 0)


def shifted(packed, offset):
    row = row_index(*packed.shape)
    x, y, z = [jnp.asarray(o, F32) - c for o, c in zip(offset, CENTRE)]
    move = jnp.where(row == 0, x, jnp.where(row == 1, y, jnp.where(row == 2, z, 0.0)))
    return packed + move


def source_rows(moved):
    row = row_index(*moved.shape)
    square = jnp.sum(jnp.where(row < 3, moved * moved, 0.0), axis=0, keepdims=True)
    head = jnp.where(row < 3, moved, square)
    tail = jnp.where(row == 0, 1.0, 0.0).astype(F32)
    high, mid, low = parts(jnp.concatenate([head, tail], axis=0))
    distance = jnp.concatenate([high, high, high, mid, mid, low], axis=0).astype(BF16)
    mass = moved[3:4]
    carried = jnp.where(row < 3, moved * mass, mass)
    high, mid, low = parts(jnp.concatenate([carried, jnp.zeros_like(carried)], axis=0))
    summed = jnp.concatenate([high, mid, low, jnp.zeros_like(low)], axis=0).astype(BF16)
    return distance, summed


def target_rows(moved):
    slots = moved.shape[-1]
    row = row_index(4, slots)
    square = jnp.sum(jnp.where(row < 3, moved * moved, 0.0), axis=0, keepdims=True)
    head = jnp.where(row < 3, 2.0 * moved, -1.0)
    tail = jnp.where(row == 0, 1.0 - square, 0.0)
    high, mid, low = parts(jnp.concatenate([head, tail], axis=0))
    return jnp.concatenate([high, mid, low, high, mid, high], axis=0).T.astype(BF16)


def pair_weight(target, source):
    near = jnp.maximum(jnp.dot(target, source, preferred_element_type=F32), 0.0)
    weight = near * near * near
    high = weight.astype(BF16)
    return high, (weight - high.astype(F32)).astype(BF16)


def contract(weights, rows):
    return lax.dot_general(weights, rows, (((1,), (1,)), ((), ())), preferred_element_type=F32)


def pack_kernel(counts_ref, place_ref, mass_ref, packed_ref, keep_ref):
    for z in range(2):
        mass = mass_ref[0, 0, z : z + 1, :]
        keep = lax.broadcasted_iota(jnp.int32, mass.shape, 1) < counts_ref[0, :, z : z + 1]
        rows = [place_ref[c, 0, 0, z : z + 1, :] for c in range(3)]
        packed_ref[z] = jnp.concatenate(rows + [jnp.where(keep, mass, 0.0)], axis=0)
        keep_ref[z] = jnp.broadcast_to(jnp.where(keep, 1.0, 0.0), keep_ref.shape[1:])


def ahead(axis):
    return 1 - 2 * lax.rem(lax.axis_index(axis), 2)


def y_shifts(size):
    if size == 2:
        return [[0], [-1, 1]]
    return [[0], [ahead("gy")], [-ahead("gy")]]


def list_chunk(list_ref, chunk):
    return jnp.concatenate([list_ref[2 * chunk], list_ref[2 * chunk + 1]], axis=1)[0:4]


def fill(near_ref, sum_ref, list_ref, entries):
    half = list_ref.shape[-1]
    lane = lax.broadcasted_iota(jnp.int32, (8, half), 1)
    list_ref[...] = jnp.zeros_like(list_ref)
    place = jnp.int32(0)
    held = {}
    for number, (ref, index, offset) in enumerate(entries):
        packed = ref[index]
        head, tail = shifted(packed[:, :half], offset), shifted(packed[:, half:], offset)
        if number == len(entries) - 1 and number % 2 == 0:
            list_ref[0] = jnp.concatenate([head, jnp.zeros_like(head)], axis=0)
        else:
            distance, summed = source_rows(head)
            near_ref[:, number * half : (number + 1) * half] = distance
            sum_ref[:, number * half : (number + 1) * half] = summed
        held[number] = tail
    if len(entries) % 2:
        place = place + half
    known = {}
    for number, (ref, index, offset) in enumerate(entries):
        tail = held[number]
        key = (id(ref),) + (index if isinstance(index, tuple) else (index,))
        if key not in known:
            present = jnp.where(tail[3:4] != 0.0, lane[0:1] + 1, 0).astype(F32)
            known[key] = jnp.max(present).astype(jnp.int32)
        length = known[key]
        tile, turn = lax.div(place, half), lax.rem(place, half)
        tail = jnp.where(lane < length, jnp.concatenate([tail, jnp.zeros_like(tail)], axis=0), 0.0)
        tail = pltpu.roll(tail, turn, 1)
        list_ref[tile] += jnp.where(lane >= turn, tail, 0.0)
        list_ref[tile + 1] += jnp.where(lane < turn, tail, 0.0)
        place = place + length
    done = (len(entries) // 2) * 2 * half
    for chunk in range((near_ref.shape[1] - done) // (2 * half)):
        distance, summed = source_rows(list_chunk(list_ref, chunk))
        near_ref[:, done + chunk * 2 * half : done + (chunk + 1) * 2 * half] = distance
        sum_ref[:, done + chunk * 2 * half : done + (chunk + 1) * 2 * half] = summed
    return place


def gathered(target, nears, sums):
    highs, lows = [], []
    for near in nears:
        high, low = pair_weight(target, near)
        highs.append(high)
        lows.append(low)
    rows = jnp.concatenate(sums, axis=1)
    return contract(jnp.concatenate(highs + lows, axis=1), jnp.concatenate([rows, rows], axis=1))


def sums_over(targets, totals, near_ref, sum_ref, list_ref, length, sources, tiles):
    wide = 2 * list_ref.shape[-1]
    steps = near_ref.shape[1] // (tiles * wide)

    def step(number, totals):
        nears, sums = [], []
        for tile in range(tiles):
            lanes = pl.ds(pl.multiple_of((number * tiles + tile) * wide, wide), wide)
            nears.append(near_ref[:, lanes])
            sums.append(sum_ref[:, lanes])
        return tuple(total + gathered(target, nears, sums) for target, total in zip(targets, totals))

    totals = step(0, totals) if steps == 1 else lax.fori_loop(0, steps, step, tuple(totals))
    done = steps * tiles - sources // 2

    def rest(number, totals):
        near, summed = source_rows(list_chunk(list_ref, number))
        return tuple(total + gathered(target, [near], [summed]) for target, total in zip(targets, totals))

    return lax.fori_loop(done, jnp.maximum(lax.div(length + (wide - 1), wide), done), rest, tuple(totals))


def plane_kernel(size_y, *refs):
    planes, (target_ref, total_ref, near_ref, sum_ref, list_ref) = refs[:-5], refs[-5:]
    own_ref = planes[0]
    for z in range(2):
        target_ref[z] = target_rows(shifted(own_ref[z], (0, 0, z)))
    entries = []
    for ref, shifts in zip(planes, y_shifts(size_y)):
        for y in shifts:
            entries += [(ref, z, (0, y, z)) for z in range(2)]
    length = fill(near_ref, sum_ref, list_ref, entries)
    zero = jnp.zeros(total_ref.shape[1:], F32)
    targets = [target_ref[z] for z in range(2)]
    totals = sums_over(targets, (zero, zero), near_ref, sum_ref, list_ref, length, len(entries), 5)
    for z in range(2):
        total_ref[z] = totals[z]


def slab_kernel(size_y, target_ref, before_ref, near_x_ref, *refs):
    far_refs, (total_ref, near_ref, sum_ref, list_ref) = refs[:-4], refs[-4:]
    entries = []
    for plane, shifts in enumerate(y_shifts(size_y)):
        for y in shifts:
            entries += [(near_x_ref, (plane, z), (ahead("gx"), y, z)) for z in range(2)]
            entries += [(far_refs[plane - 1], z, (-ahead("gx"), y, z)) for z in range(2)]
    length = fill(near_ref, sum_ref, list_ref, entries)
    targets = [target_ref[z] for z in range(2)]
    totals = sums_over(targets, (before_ref[0], before_ref[1]), near_ref, sum_ref, list_ref, length, len(entries), 9)
    for z in range(2):
        total_ref[z] = totals[z]


def complete(size_y, first, z, speed_ref, own_ref, target_ref, before_ref, source_ref, near_ref, sum_ref, list_ref):
    entries = []
    for column, x in enumerate((0, ahead("gx"), -ahead("gx"))):
        for plane, shifts in enumerate(y_shifts(size_y)):
            planes = len(y_shifts(size_y))
            index = column * planes + (plane if column < 2 else (plane - 1) % planes)
            entries += [(source_ref, index, (x, y, 3 * z - 1)) for y in shifts]
    length = fill(near_ref, sum_ref, list_ref, entries)
    (total,) = sums_over([target_ref[z]], (before_ref[z],), near_ref, sum_ref, list_ref, length, len(entries), 7)
    total = total.T
    total = (total[0:8] + total[8:16] + total[16:24])[0:4]
    own = own_ref[z]
    accel = total - shifted(own, (0, 0, z)) * total[3:4]
    if first:
        rows = [jnp.where(z == 1, speed_ref[c, 0, 0, 1:2, :], speed_ref[c, 0, 0, 0:1, :]) for c in range(3)]
        speed = jnp.concatenate(rows + [jnp.zeros_like(rows[0])], axis=0)
    else:
        speed = speed_ref[z]
    speed = speed + time_step * accel
    place = jnp.clip(own + time_step * speed, 0.0, 1.0)
    return jnp.where(row_index(*own.shape) < 3, place, own), speed


def near_side():
    return (1 + ahead("gz")) // 2


def near_kernel(size_y, first, speed_ref, own_ref, target_ref, before_ref, source_ref, bin_ref, near_ref, sum_ref, list_ref):
    place, speed = complete(
        size_y, first, near_side(), speed_ref, own_ref, target_ref, before_ref, source_ref, near_ref, sum_ref, list_ref
    )
    bin_ref[0] = place
    bin_ref[1] = speed


def far_kernel(size_y, first, last, keep_ref, bin_ref, speed_ref, own_ref, target_ref, before_ref, source_ref, place_out, speed_out, near_ref, sum_ref, list_ref):
    other = near_side()
    z = 1 - other
    place, speed = complete(
        size_y, first, z, speed_ref, own_ref, target_ref, before_ref, source_ref, near_ref, sum_ref, list_ref
    )
    if not last:
        place_out[z] = place
        speed_out[z] = speed
        place_out[other] = bin_ref[0]
        speed_out[other] = bin_ref[1]
        return
    for side in range(2):
        keep = keep_ref[side, 0:1] > 0.0
        moved = jnp.where(z == side, place, bin_ref[0])
        kicked = jnp.where(z == side, speed, bin_ref[1])
        for c in range(3):
            place_out[c, 0, 0, side : side + 1, :] = jnp.where(keep, moved[c : c + 1], 0.0)
            speed_out[c, 0, 0, side : side + 1, :] = jnp.where(keep, kicked[c : c + 1], 0.0)


VMEM = pl.BlockSpec(memory_space=pltpu.VMEM)


def swaps(axis):
    size = lax.axis_size(axis)
    near = [(i, i ^ 1) for i in range(size)]
    far = [(i, (((i + 1) ^ 1) - 1) % size) for i in range(size)]
    return near, far


def across(value, path_x, path_y):
    size_y = lax.axis_size("gy")
    pairs = [(x * size_y + y, to_x * size_y + to_y) for x, to_x in path_x for y, to_y in path_y]
    return lax.ppermute(value, ("gx", "gy"), pairs)


def call(kernel, inputs, outputs, sources, targets, slots, chunks):
    half = slots // 2
    heads = sources // 2 * 2
    return pl.pallas_call(
        kernel,
        out_shape=outputs,
        in_specs=[VMEM] * len(inputs),
        out_specs=tuple(VMEM for _ in outputs),
        scratch_shapes=[
            pltpu.VMEM((48, heads * half + chunks * slots), BF16),
            pltpu.VMEM((32, heads * half + chunks * slots), BF16),
            pltpu.VMEM((heads + 4, 8, half), F32),
        ],
        compiler_params=pltpu.CompilerParams(vmem_limit_bytes=24 * 1024 * 1024),
        cost_estimate=pl.CostEstimate(flops=sources * targets * slots * slots * 1000, bytes_accessed=1 << 18, transcendentals=0),
    )(*inputs)


def on_device(positions, velocities, mass, counts):
    slots = positions.shape[-1]
    size_y = lax.axis_size("gy")
    bins = jax.ShapeDtypeStruct((2, 4, slots), F32)
    full = jax.ShapeDtypeStruct(positions.shape, F32)
    running = jax.ShapeDtypeStruct((2, slots, 32), F32)
    packed, keep = pl.pallas_call(
        pack_kernel,
        out_shape=(bins, bins),
        in_specs=[VMEM] * 3,
        out_specs=(VMEM, VMEM),
    )(counts, positions, mass)
    speed = velocities
    upper = lax.rem(lax.axis_index("gz"), 2)
    for subcycle in range(SUBCYCLES):
        first, last = subcycle == 0, subcycle == SUBCYCLES - 1
        paths = swaps("gy")[: min(size_y, 3) - 1]
        planes = [packed] + [lax.ppermute(packed, "gy", path) for path in paths]
        near, far = swaps("gx")
        far_planes = [across(packed, far, path) for path in paths] + [lax.ppermute(packed, "gx", far)]
        plane = jnp.stack(planes)
        near_x = lax.ppermute(plane, "gx", near)
        targets, total = call(
            functools.partial(plane_kernel, size_y),
            planes,
            (jax.ShapeDtypeStruct((2, slots, 48), BF16), running),
            6, 2, slots, 2,
        )
        slab = jnp.concatenate([plane, near_x] + [value[None] for value in far_planes], axis=0)
        near, far = swaps("gz")
        far_z = lax.ppermute(lax.dynamic_index_in_dim(slab, upper, 1, False), "gz", far)
        near_z = lax.ppermute(lax.dynamic_index_in_dim(slab, 1 - upper, 1, False), "gz", near)
        (total,) = call(
            functools.partial(slab_kernel, size_y),
            [targets, total, near_x] + far_planes,
            (running,),
            12, 2, slots, 3,
        )
        state = [speed, packed, targets, total]
        (half_done,) = call(
            functools.partial(near_kernel, size_y, first),
            state + [near_z],
            (bins,),
            9, 1, slots, 3,
        )
        packed, speed = call(
            functools.partial(far_kernel, size_y, first, last),
            [keep, half_done] + state + [far_z],
            (full, full) if last else (bins, bins),
            9, 1, slots, 3,
        )
    return packed, speed


def solution(mesh):
    placed = (
        P(None, "gx", "gy", "gz", None),
        P(None, "gx", "gy", "gz", None),
        P("gx", "gy", "gz", None),
        P("gx", "gy", "gz"),
    )
    return jax.shard_map(
        on_device,
        mesh=mesh,
        in_specs=placed,
        out_specs=(P(None, "gx", "gy", "gz", None), P(None, "gx", "gy", "gz", None)),
        check_vma=False,
    )
```

```python
import functools

import jax
import jax.numpy as jnp
from jax import lax
from jax.experimental import pallas as pl
from jax.experimental.pallas import tpu as pltpu
from jax.sharding import PartitionSpec as P

SUBCYCLES = 2

time_step = 0.25

CENTRE = (0.5, 0.5, 1.0)
F32, BF16 = jnp.float32, jnp.bfloat16


def parts(value):
    high = value.astype(BF16).astype(F32)
    rest = value - high
    mid = rest.astype(BF16).astype(F32)
    return high, mid, rest - mid


def row_index(rows, slots):
    return lax.broadcasted_iota(jnp.int32, (rows, slots), 0)


def shifted(packed, offset):
    row = row_index(*packed.shape)
    x, y, z = [jnp.asarray(o, F32) - c for o, c in zip(offset, CENTRE)]
    move = jnp.where(row == 0, x, jnp.where(row == 1, y, jnp.where(row == 2, z, 0.0)))
    return packed + move


def source_rows(moved):
    row = row_index(*moved.shape)
    square = jnp.sum(jnp.where(row < 3, moved * moved, 0.0), axis=0, keepdims=True)
    head = jnp.where(row < 3, moved, square)
    tail = jnp.where(row == 0, 1.0, 0.0).astype(F32)
    high, mid, low = parts(jnp.concatenate([head, tail], axis=0))
    distance = jnp.concatenate([high, high, high, mid, mid, low], axis=0).astype(BF16)
    mass = moved[3:4]
    carried = jnp.where(row < 3, moved * mass, mass)
    high, mid, low = parts(jnp.concatenate([carried, jnp.zeros_like(carried)], axis=0))
    summed = jnp.concatenate([high, mid, low, jnp.zeros_like(low)], axis=0).astype(BF16)
    return distance, summed


def target_rows(moved):
    slots = moved.shape[-1]
    row = row_index(4, slots)
    square = jnp.sum(jnp.where(row < 3, moved * moved, 0.0), axis=0, keepdims=True)
    head = jnp.where(row < 3, 2.0 * moved, -1.0)
    tail = jnp.where(row == 0, 1.0 - square, 0.0)
    high, mid, low = parts(jnp.concatenate([head, tail], axis=0))
    return jnp.concatenate([high, mid, low, high, mid, high], axis=0).T.astype(BF16)


def pair_weight(target, source):
    near = jnp.maximum(jnp.dot(target, source, preferred_element_type=F32), 0.0)
    weight = near * near * near
    high = weight.astype(BF16)
    return high, (weight - high.astype(F32)).astype(BF16)


def contract(weights, rows):
    return lax.dot_general(weights, rows, (((1,), (1,)), ((), ())), preferred_element_type=F32)


def pack_kernel(counts_ref, place_ref, mass_ref, packed_ref, keep_ref):
    for z in range(2):
        mass = mass_ref[0, 0, z : z + 1, :]
        keep = lax.broadcasted_iota(jnp.int32, mass.shape, 1) < counts_ref[0, :, z : z + 1]
        rows = [place_ref[c, 0, 0, z : z + 1, :] for c in range(3)]
        packed_ref[z] = jnp.concatenate(rows + [jnp.where(keep, mass, 0.0)], axis=0)
        keep_ref[z] = jnp.broadcast_to(jnp.where(keep, 1.0, 0.0), keep_ref.shape[1:])


def ahead(axis):
    return 1 - 2 * lax.rem(lax.axis_index(axis), 2)


def y_shifts(size):
    if size == 2:
        return [[0], [-1, 1]]
    return [[0], [ahead("gy")], [-ahead("gy")]]


def list_chunk(list_ref, chunk):
    return jnp.concatenate([list_ref[2 * chunk], list_ref[2 * chunk + 1]], axis=1)[0:4]


def fill(near_ref, sum_ref, list_ref, entries):
    half = list_ref.shape[-1]
    lane = lax.broadcasted_iota(jnp.int32, (8, half), 1)
    list_ref[...] = jnp.zeros_like(list_ref)
    place = jnp.int32(0)
    held = {}
    for number, (ref, index, offset) in enumerate(entries):
        packed = ref[index]
        head, tail = shifted(packed[:, :half], offset), shifted(packed[:, half:], offset)
        if number == len(entries) - 1 and number % 2 == 0:
            list_ref[0] = jnp.concatenate([head, jnp.zeros_like(head)], axis=0)
        else:
            distance, summed = source_rows(head)
            near_ref[:, number * half : (number + 1) * half] = distance
            sum_ref[:, number * half : (number + 1) * half] = summed
        held[number] = tail
    if len(entries) % 2:
        place = place + half
    known = {}
    for number, (ref, index, offset) in enumerate(entries):
        tail = held[number]
        key = (id(ref),) + (index if isinstance(index, tuple) else (index,))
        if key not in known:
            present = jnp.where(tail[3:4] != 0.0, lane[0:1] + 1, 0).astype(F32)
            known[key] = jnp.max(present).astype(jnp.int32)
        length = known[key]
        tile, turn = lax.div(place, half), lax.rem(place, half)
        tail = jnp.where(lane < length, jnp.concatenate([tail, jnp.zeros_like(tail)], axis=0), 0.0)
        tail = pltpu.roll(tail, turn, 1)
        list_ref[tile] += jnp.where(lane >= turn, tail, 0.0)
        list_ref[tile + 1] += jnp.where(lane < turn, tail, 0.0)
        place = place + length
    done = (len(entries) // 2) * 2 * half
    for chunk in range((near_ref.shape[1] - done) // (2 * half)):
        distance, summed = source_rows(list_chunk(list_ref, chunk))
        near_ref[:, done + chunk * 2 * half : done + (chunk + 1) * 2 * half] = distance
        sum_ref[:, done + chunk * 2 * half : done + (chunk + 1) * 2 * half] = summed
    return place


def gathered(target, nears, sums):
    highs, lows = [], []
    for near in nears:
        high, low = pair_weight(target, near)
        highs.append(high)
        lows.append(low)
    rows = jnp.concatenate(sums, axis=1)
    return contract(jnp.concatenate(highs + lows, axis=1), jnp.concatenate([rows, rows], axis=1))


def sums_over(targets, totals, near_ref, sum_ref, list_ref, length, sources, tiles):
    wide = 2 * list_ref.shape[-1]
    steps = near_ref.shape[1] // (tiles * wide)

    def step(number, totals):
        nears, sums = [], []
        for tile in range(tiles):
            lanes = pl.ds(pl.multiple_of((number * tiles + tile) * wide, wide), wide)
            nears.append(near_ref[:, lanes])
            sums.append(sum_ref[:, lanes])
        return tuple(total + gathered(target, nears, sums) for target, total in zip(targets, totals))

    totals = step(0, totals) if steps == 1 else lax.fori_loop(0, steps, step, tuple(totals))
    done = steps * tiles - sources // 2

    def rest(number, totals):
        near, summed = source_rows(list_chunk(list_ref, number))
        return tuple(total + gathered(target, [near], [summed]) for target, total in zip(targets, totals))

    return lax.fori_loop(done, jnp.maximum(lax.div(length + (wide - 1), wide), done), rest, tuple(totals))


def plane_kernel(size_y, *refs):
    planes, (target_ref, total_ref, near_ref, sum_ref, list_ref) = refs[:-5], refs[-5:]
    own_ref = planes[0]
    for z in range(2):
        target_ref[z] = target_rows(shifted(own_ref[z], (0, 0, z)))
    entries = []
    for ref, shifts in zip(planes, y_shifts(size_y)):
        for y in shifts:
            entries += [(ref, z, (0, y, z)) for z in range(2)]
    length = fill(near_ref, sum_ref, list_ref, entries)
    zero = jnp.zeros(total_ref.shape[1:], F32)
    targets = [target_ref[z] for z in range(2)]
    totals = sums_over(targets, (zero, zero), near_ref, sum_ref, list_ref, length, len(entries), 5)
    for z in range(2):
        total_ref[z] = totals[z]


def slab_kernel(size_y, target_ref, before_ref, near_x_ref, *refs):
    far_refs, (total_ref, near_ref, sum_ref, list_ref) = refs[:-4], refs[-4:]
    entries = []
    for plane, shifts in enumerate(y_shifts(size_y)):
        for y in shifts:
            entries += [(near_x_ref, (plane, z), (ahead("gx"), y, z)) for z in range(2)]
            entries += [(far_refs[plane - 1], z, (-ahead("gx"), y, z)) for z in range(2)]
    length = fill(near_ref, sum_ref, list_ref, entries)
    targets = [target_ref[z] for z in range(2)]
    totals = sums_over(targets, (before_ref[0], before_ref[1]), near_ref, sum_ref, list_ref, length, len(entries), 9)
    for z in range(2):
        total_ref[z] = totals[z]


def complete(size_y, first, z, speed_ref, own_ref, target_ref, before_ref, source_ref, near_ref, sum_ref, list_ref):
    entries = []
    for column, x in enumerate((0, ahead("gx"), -ahead("gx"))):
        for plane, shifts in enumerate(y_shifts(size_y)):
            planes = len(y_shifts(size_y))
            index = column * planes + (plane if column < 2 else (plane - 1) % planes)
            entries += [(source_ref, index, (x, y, 3 * z - 1)) for y in shifts]
    length = fill(near_ref, sum_ref, list_ref, entries)
    (total,) = sums_over([target_ref[z]], (before_ref[z],), near_ref, sum_ref, list_ref, length, len(entries), 7)
    total = total.T
    total = (total[0:8] + total[8:16] + total[16:24])[0:4]
    own = own_ref[z]
    accel = total - shifted(own, (0, 0, z)) * total[3:4]
    if first:
        rows = [jnp.where(z == 1, speed_ref[c, 0, 0, 1:2, :], speed_ref[c, 0, 0, 0:1, :]) for c in range(3)]
        speed = jnp.concatenate(rows + [jnp.zeros_like(rows[0])], axis=0)
    else:
        speed = speed_ref[z]
    speed = speed + time_step * accel
    place = jnp.clip(own + time_step * speed, 0.0, 1.0)
    return jnp.where(row_index(*own.shape) < 3, place, own), speed


def near_side():
    return (1 + ahead("gz")) // 2


def near_kernel(size_y, first, speed_ref, own_ref, target_ref, before_ref, source_ref, bin_ref, near_ref, sum_ref, list_ref):
    place, speed = complete(
        size_y, first, near_side(), speed_ref, own_ref, target_ref, before_ref, source_ref, near_ref, sum_ref, list_ref
    )
    bin_ref[0] = place
    bin_ref[1] = speed


def far_kernel(size_y, first, last, keep_ref, bin_ref, speed_ref, own_ref, target_ref, before_ref, source_ref, place_out, speed_out, near_ref, sum_ref, list_ref):
    other = near_side()
    z = 1 - other
    place, speed = complete(
        size_y, first, z, speed_ref, own_ref, target_ref, before_ref, source_ref, near_ref, sum_ref, list_ref
    )
    if not last:
        place_out[z] = place
        speed_out[z] = speed
        place_out[other] = bin_ref[0]
        speed_out[other] = bin_ref[1]
        return
    for side in range(2):
        keep = keep_ref[side, 0:1] > 0.0
        moved = jnp.where(z == side, place, bin_ref[0])
        kicked = jnp.where(z == side, speed, bin_ref[1])
        for c in range(3):
            place_out[c, 0, 0, side : side + 1, :] = jnp.where(keep, moved[c : c + 1], 0.0)
            speed_out[c, 0, 0, side : side + 1, :] = jnp.where(keep, kicked[c : c + 1], 0.0)


VMEM = pl.BlockSpec(memory_space=pltpu.VMEM)


def swaps(axis):
    size = lax.axis_size(axis)
    near = [(i, i ^ 1) for i in range(size)]
    far = [(i, (((i + 1) ^ 1) - 1) % size) for i in range(size)]
    return near, far


def across(value, path_x, path_y):
    size_y = lax.axis_size("gy")
    pairs = [(x * size_y + y, to_x * size_y + to_y) for x, to_x in path_x for y, to_y in path_y]
    return lax.ppermute(value, ("gx", "gy"), pairs)


def call(kernel, inputs, outputs, sources, targets, slots, chunks):
    half = slots // 2
    heads = sources // 2 * 2
    return pl.pallas_call(
        kernel,
        out_shape=outputs,
        in_specs=[VMEM] * len(inputs),
        out_specs=tuple(VMEM for _ in outputs),
        scratch_shapes=[
            pltpu.VMEM((48, heads * half + chunks * slots), BF16),
            pltpu.VMEM((32, heads * half + chunks * slots), BF16),
            pltpu.VMEM((heads + 4, 8, half), F32),
        ],
        compiler_params=pltpu.CompilerParams(vmem_limit_bytes=24 * 1024 * 1024),
        cost_estimate=pl.CostEstimate(flops=sources * targets * slots * slots * 1000, bytes_accessed=1 << 18, transcendentals=0),
    )(*inputs)


def on_device(positions, velocities, mass, counts):
    slots = positions.shape[-1]
    size_y = lax.axis_size("gy")
    bins = jax.ShapeDtypeStruct((2, 4, slots), F32)
    full = jax.ShapeDtypeStruct(positions.shape, F32)
    running = jax.ShapeDtypeStruct((2, slots, 32), F32)
    packed, keep = pl.pallas_call(
        pack_kernel,
        out_shape=(bins, bins),
        in_specs=[VMEM] * 3,
        out_specs=(VMEM, VMEM),
        compiler_params=pltpu.CompilerParams(vmem_limit_bytes=8 * 1024 * 1024),
    )(counts, positions, mass)
    speed = velocities
    upper = lax.rem(lax.axis_index("gz"), 2)
    for subcycle in range(SUBCYCLES):
        first, last = subcycle == 0, subcycle == SUBCYCLES - 1
        paths = swaps("gy")[: min(size_y, 3) - 1]
        planes = [packed] + [lax.ppermute(packed, "gy", path) for path in paths]
        near, far = swaps("gx")
        far_planes = [across(packed, far, path) for path in paths] + [lax.ppermute(packed, "gx", far)]
        plane = jnp.stack(planes)
        near_x = lax.ppermute(plane, "gx", near)
        targets, total = call(
            functools.partial(plane_kernel, size_y),
            planes,
            (jax.ShapeDtypeStruct((2, slots, 48), BF16), running),
            6, 2, slots, 2,
        )
        slab = jnp.concatenate([plane, near_x] + [value[None] for value in far_planes], axis=0)
        near, far = swaps("gz")
        far_z = lax.ppermute(lax.dynamic_index_in_dim(slab, upper, 1, False), "gz", far)
        near_z = lax.ppermute(lax.dynamic_index_in_dim(slab, 1 - upper, 1, False), "gz", near)
        (total,) = call(
            functools.partial(slab_kernel, size_y),
            [targets, total, near_x] + far_planes,
            (running,),
            12, 2, slots, 3,
        )
        state = [speed, packed, targets, total]
        (half_done,) = call(
            functools.partial(near_kernel, size_y, first),
            state + [near_z],
            (bins,),
            9, 1, slots, 3,
        )
        packed, speed = call(
            functools.partial(far_kernel, size_y, first, last),
            [keep, half_done] + state + [far_z],
            (full, full) if last else (bins, bins),
            9, 1, slots, 3,
        )
    return packed, speed


def solution(mesh):
    placed = (
        P(None, "gx", "gy", "gz", None),
        P(None, "gx", "gy", "gz", None),
        P("gx", "gy", "gz", None),
        P("gx", "gy", "gz"),
    )
    return jax.shard_map(
        on_device,
        mesh=mesh,
        in_specs=placed,
        out_specs=(P(None, "gx", "gy", "gz", None), P(None, "gx", "gy", "gz", None)),
        check_vma=False,
    )
```

```python
import functools

import jax
import jax.numpy as jnp
from jax import lax
from jax.experimental import pallas as pl
from jax.experimental.pallas import tpu as pltpu
from jax.sharding import PartitionSpec as P

SUBCYCLES = 2

time_step = 0.25

CENTRE = (0.5, 0.5, 1.0)
F32, BF16 = jnp.float32, jnp.bfloat16


def parts(value):
    high = value.astype(BF16).astype(F32)
    rest = value - high
    mid = rest.astype(BF16).astype(F32)
    return high, mid, rest - mid


def row_index(rows, slots):
    return lax.broadcasted_iota(jnp.int32, (rows, slots), 0)


def shifted(packed, offset):
    row = row_index(*packed.shape)
    x, y, z = [jnp.asarray(o, F32) - c for o, c in zip(offset, CENTRE)]
    move = jnp.where(row == 0, x, jnp.where(row == 1, y, jnp.where(row == 2, z, 0.0)))
    return packed + move


def source_rows(moved):
    row = row_index(*moved.shape)
    square = jnp.sum(jnp.where(row < 3, moved * moved, 0.0), axis=0, keepdims=True)
    head = jnp.where(row < 3, moved, square)
    tail = jnp.where(row == 0, 1.0, 0.0).astype(F32)
    high, mid, low = parts(jnp.concatenate([head, tail], axis=0))
    distance = jnp.concatenate([high, high, high, mid, mid, low], axis=0).astype(BF16)
    mass = moved[3:4]
    carried = jnp.where(row < 3, moved * mass, mass)
    high, mid, low = parts(jnp.concatenate([carried, jnp.zeros_like(carried)], axis=0))
    summed = jnp.concatenate([high, mid, low, jnp.zeros_like(low)], axis=0).astype(BF16)
    return distance, summed


def target_rows(moved):
    slots = moved.shape[-1]
    row = row_index(4, slots)
    square = jnp.sum(jnp.where(row < 3, moved * moved, 0.0), axis=0, keepdims=True)
    head = jnp.where(row < 3, 2.0 * moved, -1.0)
    tail = jnp.where(row == 0, 1.0 - square, 0.0)
    high, mid, low = parts(jnp.concatenate([head, tail], axis=0))
    return jnp.concatenate([high, mid, low, high, mid, high], axis=0).T.astype(BF16)


def pair_weight(target, source):
    near = jnp.maximum(jnp.dot(target, source, preferred_element_type=F32), 0.0)
    weight = near * near * near
    high = weight.astype(BF16)
    return high, (weight - high.astype(F32)).astype(BF16)


def contract(weights, rows):
    return lax.dot_general(weights, rows, (((1,), (1,)), ((), ())), preferred_element_type=F32)


def pack_kernel(rows_ref, packed_ref, keep_ref):
    for z in range(2):
        packed_ref[z] = jnp.concatenate([rows_ref[c, z : z + 1, :] for c in range(4)], axis=0)
        keep_ref[z] = jnp.broadcast_to(rows_ref[4, z : z + 1, :], keep_ref.shape[1:])


def ahead(axis):
    return 1 - 2 * lax.rem(lax.axis_index(axis), 2)


def y_shifts(size):
    if size == 2:
        return [[0], [-1, 1]]
    return [[0], [ahead("gy")], [-ahead("gy")]]


def list_chunk(list_ref, chunk):
    return jnp.concatenate([list_ref[2 * chunk], list_ref[2 * chunk + 1]], axis=1)[0:4]


def fill(near_ref, sum_ref, list_ref, entries):
    half = list_ref.shape[-1]
    lane = lax.broadcasted_iota(jnp.int32, (8, half), 1)
    list_ref[...] = jnp.zeros_like(list_ref)
    place = jnp.int32(0)
    held = {}
    for number, (ref, index, offset) in enumerate(entries):
        packed = ref[index]
        head, tail = shifted(packed[:, :half], offset), shifted(packed[:, half:], offset)
        if number == len(entries) - 1 and number % 2 == 0:
            list_ref[0] = jnp.concatenate([head, jnp.zeros_like(head)], axis=0)
        else:
            distance, summed = source_rows(head)
            near_ref[:, number * half : (number + 1) * half] = distance
            sum_ref[:, number * half : (number + 1) * half] = summed
        held[number] = tail
    if len(entries) % 2:
        place = place + half
    known = {}
    for number, (ref, index, offset) in enumerate(entries):
        tail = held[number]
        key = (id(ref),) + (index if isinstance(index, tuple) else (index,))
        if key not in known:
            present = jnp.where(tail[3:4] != 0.0, lane[0:1] + 1, 0).astype(F32)
            known[key] = jnp.max(present).astype(jnp.int32)
        length = known[key]
        tile, turn = lax.div(place, half), lax.rem(place, half)
        tail = jnp.where(lane < length, jnp.concatenate([tail, jnp.zeros_like(tail)], axis=0), 0.0)
        tail = pltpu.roll(tail, turn, 1)
        list_ref[tile] += jnp.where(lane >= turn, tail, 0.0)
        list_ref[tile + 1] += jnp.where(lane < turn, tail, 0.0)
        place = place + length
    done = (len(entries) // 2) * 2 * half
    for chunk in range((near_ref.shape[1] - done) // (2 * half)):
        distance, summed = source_rows(list_chunk(list_ref, chunk))
        near_ref[:, done + chunk * 2 * half : done + (chunk + 1) * 2 * half] = distance
        sum_ref[:, done + chunk * 2 * half : done + (chunk + 1) * 2 * half] = summed
    return place


def gathered(target, nears, sums):
    highs, lows = [], []
    for near in nears:
        high, low = pair_weight(target, near)
        highs.append(high)
        lows.append(low)
    rows = jnp.concatenate(sums, axis=1)
    return contract(jnp.concatenate(highs + lows, axis=1), jnp.concatenate([rows, rows], axis=1))


def sums_over(targets, totals, near_ref, sum_ref, list_ref, length, sources, tiles):
    wide = 2 * list_ref.shape[-1]
    steps = near_ref.shape[1] // (tiles * wide)

    def step(number, totals):
        nears, sums = [], []
        for tile in range(tiles):
            lanes = pl.ds(pl.multiple_of((number * tiles + tile) * wide, wide), wide)
            nears.append(near_ref[:, lanes])
            sums.append(sum_ref[:, lanes])
        return tuple(total + gathered(target, nears, sums) for target, total in zip(targets, totals))

    totals = step(0, totals) if steps == 1 else lax.fori_loop(0, steps, step, tuple(totals))
    done = steps * tiles - sources // 2

    def rest(number, totals):
        near, summed = source_rows(list_chunk(list_ref, number))
        return tuple(total + gathered(target, [near], [summed]) for target, total in zip(targets, totals))

    return lax.fori_loop(done, jnp.maximum(lax.div(length + (wide - 1), wide), done), rest, tuple(totals))


def plane_kernel(size_y, *refs):
    planes, (target_ref, total_ref, near_ref, sum_ref, list_ref) = refs[:-5], refs[-5:]
    own_ref = planes[0]
    for z in range(2):
        target_ref[z] = target_rows(shifted(own_ref[z], (0, 0, z)))
    entries = []
    for ref, shifts in zip(planes, y_shifts(size_y)):
        for y in shifts:
            entries += [(ref, z, (0, y, z)) for z in range(2)]
    length = fill(near_ref, sum_ref, list_ref, entries)
    zero = jnp.zeros(total_ref.shape[1:], F32)
    targets = [target_ref[z] for z in range(2)]
    totals = sums_over(targets, (zero, zero), near_ref, sum_ref, list_ref, length, len(entries), 5)
    for z in range(2):
        total_ref[z] = totals[z]


def slab_kernel(size_y, target_ref, before_ref, near_x_ref, *refs):
    far_refs, (total_ref, near_ref, sum_ref, list_ref) = refs[:-4], refs[-4:]
    entries = []
    for plane, shifts in enumerate(y_shifts(size_y)):
        for y in shifts:
            entries += [(near_x_ref, (plane, z), (ahead("gx"), y, z)) for z in range(2)]
            entries += [(far_refs[plane - 1], z, (-ahead("gx"), y, z)) for z in range(2)]
    length = fill(near_ref, sum_ref, list_ref, entries)
    targets = [target_ref[z] for z in range(2)]
    totals = sums_over(targets, (before_ref[0], before_ref[1]), near_ref, sum_ref, list_ref, length, len(entries), 9)
    for z in range(2):
        total_ref[z] = totals[z]


def complete(size_y, first, z, speed_ref, own_ref, target_ref, before_ref, source_ref, near_ref, sum_ref, list_ref):
    entries = []
    for column, x in enumerate((0, ahead("gx"), -ahead("gx"))):
        for plane, shifts in enumerate(y_shifts(size_y)):
            planes = len(y_shifts(size_y))
            index = column * planes + (plane if column < 2 else (plane - 1) % planes)
            entries += [(source_ref, index, (x, y, 3 * z - 1)) for y in shifts]
    length = fill(near_ref, sum_ref, list_ref, entries)
    (total,) = sums_over([target_ref[z]], (before_ref[z],), near_ref, sum_ref, list_ref, length, len(entries), 7)
    total = total.T
    total = (total[0:8] + total[8:16] + total[16:24])[0:4]
    own = own_ref[z]
    accel = total - shifted(own, (0, 0, z)) * total[3:4]
    if first:
        rows = [jnp.where(z == 1, speed_ref[c, 0, 0, 1:2, :], speed_ref[c, 0, 0, 0:1, :]) for c in range(3)]
        speed = jnp.concatenate(rows + [jnp.zeros_like(rows[0])], axis=0)
    else:
        speed = speed_ref[z]
    speed = speed + time_step * accel
    place = jnp.clip(own + time_step * speed, 0.0, 1.0)
    return jnp.where(row_index(*own.shape) < 3, place, own), speed


def near_side():
    return (1 + ahead("gz")) // 2


def near_kernel(size_y, first, speed_ref, own_ref, target_ref, before_ref, source_ref, bin_ref, near_ref, sum_ref, list_ref):
    place, speed = complete(
        size_y, first, near_side(), speed_ref, own_ref, target_ref, before_ref, source_ref, near_ref, sum_ref, list_ref
    )
    bin_ref[0] = place
    bin_ref[1] = speed


def far_kernel(size_y, first, last, keep_ref, bin_ref, speed_ref, own_ref, target_ref, before_ref, source_ref, place_out, speed_out, near_ref, sum_ref, list_ref):
    other = near_side()
    z = 1 - other
    place, speed = complete(
        size_y, first, z, speed_ref, own_ref, target_ref, before_ref, source_ref, near_ref, sum_ref, list_ref
    )
    if not last:
        place_out[z] = place
        speed_out[z] = speed
        place_out[other] = bin_ref[0]
        speed_out[other] = bin_ref[1]
        return
    for side in range(2):
        keep = keep_ref[side, 0:1] > 0.0
        moved = jnp.where(z == side, place, bin_ref[0])
        kicked = jnp.where(z == side, speed, bin_ref[1])
        for c in range(3):
            place_out[c, 0, 0, side : side + 1, :] = jnp.where(keep, moved[c : c + 1], 0.0)
            speed_out[c, 0, 0, side : side + 1, :] = jnp.where(keep, kicked[c : c + 1], 0.0)


VMEM = pl.BlockSpec(memory_space=pltpu.VMEM)


def swaps(axis):
    size = lax.axis_size(axis)
    near = [(i, i ^ 1) for i in range(size)]
    far = [(i, (((i + 1) ^ 1) - 1) % size) for i in range(size)]
    return near, far


def across(value, path_x, path_y):
    size_y = lax.axis_size("gy")
    pairs = [(x * size_y + y, to_x * size_y + to_y) for x, to_x in path_x for y, to_y in path_y]
    return lax.ppermute(value, ("gx", "gy"), pairs)


def call(kernel, inputs, outputs, sources, targets, slots, chunks):
    half = slots // 2
    heads = sources // 2 * 2
    return pl.pallas_call(
        kernel,
        out_shape=outputs,
        in_specs=[VMEM] * len(inputs),
        out_specs=tuple(VMEM for _ in outputs),
        scratch_shapes=[
            pltpu.VMEM((48, heads * half + chunks * slots), BF16),
            pltpu.VMEM((32, heads * half + chunks * slots), BF16),
            pltpu.VMEM((heads + 4, 8, half), F32),
        ],
        compiler_params=pltpu.CompilerParams(vmem_limit_bytes=24 * 1024 * 1024),
        cost_estimate=pl.CostEstimate(flops=sources * targets * slots * slots * 1000, bytes_accessed=1 << 18, transcendentals=0),
    )(*inputs)


def on_device(positions, velocities, mass, counts):
    slots = positions.shape[-1]
    size_y = lax.axis_size("gy")
    bins = jax.ShapeDtypeStruct((2, 4, slots), F32)
    full = jax.ShapeDtypeStruct(positions.shape, F32)
    running = jax.ShapeDtypeStruct((2, slots, 32), F32)
    present = lax.broadcasted_iota(jnp.int32, mass.shape, 3) < counts[..., None]
    rows = [positions, jnp.where(present, mass, 0.0)[None], jnp.where(present, 1.0, 0.0).astype(F32)[None]]
    packed, keep = pl.pallas_call(
        pack_kernel,
        out_shape=(bins, bins),
        in_specs=[VMEM],
        out_specs=(VMEM, VMEM),
        compiler_params=pltpu.CompilerParams(vmem_limit_bytes=8 * 1024 * 1024),
    )(jnp.concatenate(rows, axis=0).reshape(5, 2, slots))
    speed = velocities
    upper = lax.rem(lax.axis_index("gz"), 2)
    for subcycle in range(SUBCYCLES):
        first, last = subcycle == 0, subcycle == SUBCYCLES - 1
        paths = swaps("gy")[: min(size_y, 3) - 1]
        planes = [packed] + [lax.ppermute(packed, "gy", path) for path in paths]
        near, far = swaps("gx")
        far_planes = [across(packed, far, path) for path in paths] + [lax.ppermute(packed, "gx", far)]
        plane = jnp.stack(planes)
        near_x = lax.ppermute(plane, "gx", near)
        targets, total = call(
            functools.partial(plane_kernel, size_y),
            planes,
            (jax.ShapeDtypeStruct((2, slots, 48), BF16), running),
            6, 2, slots, 2,
        )
        slab = jnp.concatenate([plane, near_x] + [value[None] for value in far_planes], axis=0)
        near, far = swaps("gz")
        far_z = lax.ppermute(lax.dynamic_index_in_dim(slab, upper, 1, False), "gz", far)
        near_z = lax.ppermute(lax.dynamic_index_in_dim(slab, 1 - upper, 1, False), "gz", near)
        (total,) = call(
            functools.partial(slab_kernel, size_y),
            [targets, total, near_x] + far_planes,
            (running,),
            12, 2, slots, 3,
        )
        state = [speed, packed, targets, total]
        (half_done,) = call(
            functools.partial(near_kernel, size_y, first),
            state + [near_z],
            (bins,),
            9, 1, slots, 3,
        )
        packed, speed = call(
            functools.partial(far_kernel, size_y, first, last),
            [keep, half_done] + state + [far_z],
            (full, full) if last else (bins, bins),
            9, 1, slots, 3,
        )
    return packed, speed


def solution(mesh):
    placed = (
        P(None, "gx", "gy", "gz", None),
        P(None, "gx", "gy", "gz", None),
        P("gx", "gy", "gz", None),
        P("gx", "gy", "gz"),
    )
    return jax.shard_map(
        on_device,
        mesh=mesh,
        in_specs=placed,
        out_specs=(P(None, "gx", "gy", "gz", None), P(None, "gx", "gy", "gz", None)),
        check_vma=False,
    )
```

```python
import functools

import jax
import jax.numpy as jnp
from jax import lax
from jax.experimental import pallas as pl
from jax.experimental.pallas import tpu as pltpu
from jax.sharding import PartitionSpec as P

SUBCYCLES = 2

time_step = 0.25

CENTRE = (0.5, 0.5, 1.0)
F32, BF16 = jnp.float32, jnp.bfloat16


def parts(value):
    high = value.astype(BF16).astype(F32)
    rest = value - high
    mid = rest.astype(BF16).astype(F32)
    return high, mid, rest - mid


def row_index(rows, slots):
    return lax.broadcasted_iota(jnp.int32, (rows, slots), 0)


def shifted(packed, offset):
    row = row_index(*packed.shape)
    x, y, z = [jnp.asarray(o, F32) - c for o, c in zip(offset, CENTRE)]
    move = jnp.where(row == 0, x, jnp.where(row == 1, y, jnp.where(row == 2, z, 0.0)))
    return packed + move


def source_rows(moved):
    row = row_index(*moved.shape)
    square = jnp.sum(jnp.where(row < 3, moved * moved, 0.0), axis=0, keepdims=True)
    head = jnp.where(row < 3, moved, square)
    tail = jnp.where(row == 0, 1.0, 0.0).astype(F32)
    high, mid, low = parts(jnp.concatenate([head, tail], axis=0))
    distance = jnp.concatenate([high, high, high, mid, mid, low], axis=0).astype(BF16)
    mass = moved[3:4]
    carried = jnp.where(row < 3, moved * mass, mass)
    high, mid, low = parts(jnp.concatenate([carried, jnp.zeros_like(carried)], axis=0))
    summed = jnp.concatenate([high, mid, low, jnp.zeros_like(low)], axis=0).astype(BF16)
    return distance, summed


def target_rows(moved):
    slots = moved.shape[-1]
    row = row_index(4, slots)
    square = jnp.sum(jnp.where(row < 3, moved * moved, 0.0), axis=0, keepdims=True)
    head = jnp.where(row < 3, 2.0 * moved, -1.0)
    tail = jnp.where(row == 0, 1.0 - square, 0.0)
    high, mid, low = parts(jnp.concatenate([head, tail], axis=0))
    return jnp.concatenate([high, mid, low, high, mid, high], axis=0).T.astype(BF16)


def pair_weight(target, source):
    near = jnp.maximum(jnp.dot(target, source, preferred_element_type=F32), 0.0)
    weight = near * near * near
    high = weight.astype(BF16)
    return high, (weight - high.astype(F32)).astype(BF16)


def contract(weights, rows):
    return lax.dot_general(weights, rows, (((1,), (1,)), ((), ())), preferred_element_type=F32)


def pack_kernel(rows_ref, packed_ref, keep_ref):
    for z in range(2):
        packed_ref[z] = jnp.concatenate([rows_ref[c, z : z + 1, :] for c in range(4)], axis=0)
        keep_ref[z] = jnp.broadcast_to(rows_ref[4, z : z + 1, :], keep_ref.shape[1:])


def ahead(axis):
    return 1 - 2 * lax.rem(lax.axis_index(axis), 2)


def y_shifts(size):
    if size == 2:
        return [[0], [-1, 1]]
    return [[0], [ahead("gy")], [-ahead("gy")]]


def list_chunk(list_ref, chunk):
    return jnp.concatenate([list_ref[2 * chunk], list_ref[2 * chunk + 1]], axis=1)[0:4]


def fill(near_ref, sum_ref, list_ref, entries):
    half = list_ref.shape[-1]
    lane = lax.broadcasted_iota(jnp.int32, (8, half), 1)
    list_ref[...] = jnp.zeros_like(list_ref)
    place = jnp.int32(0)
    held = {}
    for number, (ref, index, offset) in enumerate(entries):
        packed = ref[index]
        head, tail = shifted(packed[:, :half], offset), shifted(packed[:, half:], offset)
        if number == len(entries) - 1 and number % 2 == 0:
            list_ref[0] = jnp.concatenate([head, jnp.zeros_like(head)], axis=0)
        else:
            distance, summed = source_rows(head)
            near_ref[:, number * half : (number + 1) * half] = distance
            sum_ref[:, number * half : (number + 1) * half] = summed
        held[number] = tail
    if len(entries) % 2:
        place = place + half
    known = {}
    tile_rows = jnp.zeros((8, half), F32)
    for number, (ref, index, offset) in enumerate(entries):
        tail = held[number]
        key = (id(ref),) + (index if isinstance(index, tuple) else (index,))
        if key not in known:
            present = jnp.where(tail[3:4] != 0.0, lane[0:1] + 1, 0).astype(F32)
            known[key] = jnp.max(present).astype(jnp.int32)
        length = known[key]
        tile, turn = lax.div(place, half), lax.rem(place, half)
        tail = jnp.where(lane < length, jnp.concatenate([tail, jnp.zeros_like(tail)], axis=0), 0.0)
        tail = pltpu.roll(tail, turn, 1)
        upto = tile_rows + jnp.where(lane >= turn, tail, 0.0)
        list_ref[tile] = upto
        place = place + length
        tile_rows = jnp.where(turn + length >= half, jnp.where(lane < turn, tail, 0.0), upto)
    list_ref[lax.div(place, half)] = tile_rows
    done = (len(entries) // 2) * 2 * half
    for chunk in range((near_ref.shape[1] - done) // (2 * half)):
        distance, summed = source_rows(list_chunk(list_ref, chunk))
        near_ref[:, done + chunk * 2 * half : done + (chunk + 1) * 2 * half] = distance
        sum_ref[:, done + chunk * 2 * half : done + (chunk + 1) * 2 * half] = summed
    return place


def gathered(target, nears, sums):
    highs, lows = [], []
    for near in nears:
        high, low = pair_weight(target, near)
        highs.append(high)
        lows.append(low)
    rows = jnp.concatenate(sums, axis=1)
    return contract(jnp.concatenate(highs + lows, axis=1), jnp.concatenate([rows, rows], axis=1))


def sums_over(targets, totals, near_ref, sum_ref, list_ref, length, sources, tiles):
    wide = 2 * list_ref.shape[-1]
    steps = near_ref.shape[1] // (tiles * wide)

    def step(number, totals):
        nears, sums = [], []
        for tile in range(tiles):
            lanes = pl.ds(pl.multiple_of((number * tiles + tile) * wide, wide), wide)
            nears.append(near_ref[:, lanes])
            sums.append(sum_ref[:, lanes])
        return tuple(total + gathered(target, nears, sums) for target, total in zip(targets, totals))

    totals = step(0, totals) if steps == 1 else lax.fori_loop(0, steps, step, tuple(totals))
    done = steps * tiles - sources // 2

    def rest(number, totals):
        near, summed = source_rows(list_chunk(list_ref, number))
        return tuple(total + gathered(target, [near], [summed]) for target, total in zip(targets, totals))

    return lax.fori_loop(done, jnp.maximum(lax.div(length + (wide - 1), wide), done), rest, tuple(totals))


def plane_kernel(size_y, *refs):
    planes, (target_ref, total_ref, near_ref, sum_ref, list_ref) = refs[:-5], refs[-5:]
    own_ref = planes[0]
    for z in range(2):
        target_ref[z] = target_rows(shifted(own_ref[z], (0, 0, z)))
    entries = []
    for ref, shifts in zip(planes, y_shifts(size_y)):
        for y in shifts:
            entries += [(ref, z, (0, y, z)) for z in range(2)]
    length = fill(near_ref, sum_ref, list_ref, entries)
    zero = jnp.zeros(total_ref.shape[1:], F32)
    targets = [target_ref[z] for z in range(2)]
    totals = sums_over(targets, (zero, zero), near_ref, sum_ref, list_ref, length, len(entries), 5)
    for z in range(2):
        total_ref[z] = totals[z]


def slab_kernel(size_y, target_ref, before_ref, near_x_ref, *refs):
    far_refs, (total_ref, near_ref, sum_ref, list_ref) = refs[:-4], refs[-4:]
    entries = []
    for plane, shifts in enumerate(y_shifts(size_y)):
        for y in shifts:
            entries += [(near_x_ref, (plane, z), (ahead("gx"), y, z)) for z in range(2)]
            entries += [(far_refs[plane - 1], z, (-ahead("gx"), y, z)) for z in range(2)]
    length = fill(near_ref, sum_ref, list_ref, entries)
    targets = [target_ref[z] for z in range(2)]
    totals = sums_over(targets, (before_ref[0], before_ref[1]), near_ref, sum_ref, list_ref, length, len(entries), 9)
    for z in range(2):
        total_ref[z] = totals[z]


def complete(size_y, first, z, speed_ref, own_ref, target_ref, before_ref, source_ref, near_ref, sum_ref, list_ref):
    entries = []
    for column, x in enumerate((0, ahead("gx"), -ahead("gx"))):
        for plane, shifts in enumerate(y_shifts(size_y)):
            planes = len(y_shifts(size_y))
            index = column * planes + (plane if column < 2 else (plane - 1) % planes)
            entries += [(source_ref, index, (x, y, 3 * z - 1)) for y in shifts]
    length = fill(near_ref, sum_ref, list_ref, entries)
    (total,) = sums_over([target_ref[z]], (before_ref[z],), near_ref, sum_ref, list_ref, length, len(entries), 7)
    total = total.T
    total = (total[0:8] + total[8:16] + total[16:24])[0:4]
    own = own_ref[z]
    accel = total - shifted(own, (0, 0, z)) * total[3:4]
    if first:
        rows = [jnp.where(z == 1, speed_ref[c, 0, 0, 1:2, :], speed_ref[c, 0, 0, 0:1, :]) for c in range(3)]
        speed = jnp.concatenate(rows + [jnp.zeros_like(rows[0])], axis=0)
    else:
        speed = speed_ref[z]
    speed = speed + time_step * accel
    place = jnp.clip(own + time_step * speed, 0.0, 1.0)
    return jnp.where(row_index(*own.shape) < 3, place, own), speed


def near_side():
    return (1 + ahead("gz")) // 2


def near_kernel(size_y, first, speed_ref, own_ref, target_ref, before_ref, source_ref, bin_ref, near_ref, sum_ref, list_ref):
    place, speed = complete(
        size_y, first, near_side(), speed_ref, own_ref, target_ref, before_ref, source_ref, near_ref, sum_ref, list_ref
    )
    bin_ref[0] = place
    bin_ref[1] = speed


def far_kernel(size_y, first, last, keep_ref, bin_ref, speed_ref, own_ref, target_ref, before_ref, source_ref, place_out, speed_out, near_ref, sum_ref, list_ref):
    other = near_side()
    z = 1 - other
    place, speed = complete(
        size_y, first, z, speed_ref, own_ref, target_ref, before_ref, source_ref, near_ref, sum_ref, list_ref
    )
    if not last:
        place_out[z] = place
        speed_out[z] = speed
        place_out[other] = bin_ref[0]
        speed_out[other] = bin_ref[1]
        return
    for side in range(2):
        keep = keep_ref[side, 0:1] > 0.0
        moved = jnp.where(z == side, place, bin_ref[0])
        kicked = jnp.where(z == side, speed, bin_ref[1])
        for c in range(3):
            place_out[c, 0, 0, side : side + 1, :] = jnp.where(keep, moved[c : c + 1], 0.0)
            speed_out[c, 0, 0, side : side + 1, :] = jnp.where(keep, kicked[c : c + 1], 0.0)


VMEM = pl.BlockSpec(memory_space=pltpu.VMEM)


def swaps(axis):
    size = lax.axis_size(axis)
    near = [(i, i ^ 1) for i in range(size)]
    far = [(i, (((i + 1) ^ 1) - 1) % size) for i in range(size)]
    return near, far


def across(value, path_x, path_y):
    size_y = lax.axis_size("gy")
    pairs = [(x * size_y + y, to_x * size_y + to_y) for x, to_x in path_x for y, to_y in path_y]
    return lax.ppermute(value, ("gx", "gy"), pairs)


def call(kernel, inputs, outputs, sources, targets, slots, chunks):
    half = slots // 2
    heads = sources // 2 * 2
    return pl.pallas_call(
        kernel,
        out_shape=outputs,
        in_specs=[VMEM] * len(inputs),
        out_specs=tuple(VMEM for _ in outputs),
        scratch_shapes=[
            pltpu.VMEM((48, heads * half + chunks * slots), BF16),
            pltpu.VMEM((32, heads * half + chunks * slots), BF16),
            pltpu.VMEM((heads + 4, 8, half), F32),
        ],
        compiler_params=pltpu.CompilerParams(vmem_limit_bytes=24 * 1024 * 1024),
        cost_estimate=pl.CostEstimate(flops=sources * targets * slots * slots * 1000, bytes_accessed=1 << 18, transcendentals=0),
    )(*inputs)


def on_device(positions, velocities, mass, counts):
    slots = positions.shape[-1]
    size_y = lax.axis_size("gy")
    bins = jax.ShapeDtypeStruct((2, 4, slots), F32)
    full = jax.ShapeDtypeStruct(positions.shape, F32)
    running = jax.ShapeDtypeStruct((2, slots, 32), F32)
    present = lax.broadcasted_iota(jnp.int32, mass.shape, 3) < counts[..., None]
    rows = [positions, jnp.where(present, mass, 0.0)[None], jnp.where(present, 1.0, 0.0).astype(F32)[None]]
    packed, keep = pl.pallas_call(
        pack_kernel,
        out_shape=(bins, bins),
        in_specs=[VMEM],
        out_specs=(VMEM, VMEM),
        compiler_params=pltpu.CompilerParams(vmem_limit_bytes=8 * 1024 * 1024),
    )(jnp.concatenate(rows, axis=0).reshape(5, 2, slots))
    speed = velocities
    upper = lax.rem(lax.axis_index("gz"), 2)
    for subcycle in range(SUBCYCLES):
        first, last = subcycle == 0, subcycle == SUBCYCLES - 1
        paths = swaps("gy")[: min(size_y, 3) - 1]
        planes = [packed] + [lax.ppermute(packed, "gy", path) for path in paths]
        near, far = swaps("gx")
        far_planes = [across(packed, far, path) for path in paths] + [lax.ppermute(packed, "gx", far)]
        plane = jnp.stack(planes)
        near_x = lax.ppermute(plane, "gx", near)
        targets, total = call(
            functools.partial(plane_kernel, size_y),
            planes,
            (jax.ShapeDtypeStruct((2, slots, 48), BF16), running),
            6, 2, slots, 2,
        )
        slab = jnp.concatenate([plane, near_x] + [value[None] for value in far_planes], axis=0)
        near, far = swaps("gz")
        far_z = lax.ppermute(lax.dynamic_index_in_dim(slab, upper, 1, False), "gz", far)
        near_z = lax.ppermute(lax.dynamic_index_in_dim(slab, 1 - upper, 1, False), "gz", near)
        (total,) = call(
            functools.partial(slab_kernel, size_y),
            [targets, total, near_x] + far_planes,
            (running,),
            12, 2, slots, 3,
        )
        state = [speed, packed, targets, total]
        (half_done,) = call(
            functools.partial(near_kernel, size_y, first),
            state + [near_z],
            (bins,),
            9, 1, slots, 3,
        )
        packed, speed = call(
            functools.partial(far_kernel, size_y, first, last),
            [keep, half_done] + state + [far_z],
            (full, full) if last else (bins, bins),
            9, 1, slots, 3,
        )
    return packed, speed


def solution(mesh):
    placed = (
        P(None, "gx", "gy", "gz", None),
        P(None, "gx", "gy", "gz", None),
        P("gx", "gy", "gz", None),
        P("gx", "gy", "gz"),
    )
    return jax.shard_map(
        on_device,
        mesh=mesh,
        in_specs=placed,
        out_specs=(P(None, "gx", "gy", "gz", None), P(None, "gx", "gy", "gz", None)),
        check_vma=False,
    )
```

```python
import functools

import jax
import jax.numpy as jnp
from jax import lax
from jax.experimental import pallas as pl
from jax.experimental.pallas import tpu as pltpu
from jax.sharding import PartitionSpec as P

SUBCYCLES = 2

time_step = 0.25

CENTRE = (0.5, 0.5, 1.0)
F32, BF16 = jnp.float32, jnp.bfloat16


def parts(value):
    high = value.astype(BF16).astype(F32)
    rest = value - high
    mid = rest.astype(BF16).astype(F32)
    return high, mid, rest - mid


def row_index(rows, slots):
    return lax.broadcasted_iota(jnp.int32, (rows, slots), 0)


def shifted(packed, offset):
    row = row_index(*packed.shape)
    x, y, z = [jnp.asarray(o, F32) - c for o, c in zip(offset, CENTRE)]
    move = jnp.where(row == 0, x, jnp.where(row == 1, y, jnp.where(row == 2, z, 0.0)))
    return packed + move


def source_rows(moved):
    row = row_index(*moved.shape)
    square = jnp.sum(jnp.where(row < 3, moved * moved, 0.0), axis=0, keepdims=True)
    head = jnp.where(row < 3, moved, square)
    tail = jnp.where(row == 0, 1.0, 0.0).astype(F32)
    high, mid, low = parts(jnp.concatenate([head, tail], axis=0))
    distance = jnp.concatenate([high, high, high, mid, mid, low], axis=0).astype(BF16)
    mass = moved[3:4]
    carried = jnp.where(row < 3, moved * mass, mass)
    high, mid, low = parts(jnp.concatenate([carried, jnp.zeros_like(carried)], axis=0))
    summed = jnp.concatenate([high, mid, low, jnp.zeros_like(low)], axis=0).astype(BF16)
    return distance, summed


def target_rows(moved):
    slots = moved.shape[-1]
    row = row_index(4, slots)
    square = jnp.sum(jnp.where(row < 3, moved * moved, 0.0), axis=0, keepdims=True)
    head = jnp.where(row < 3, 2.0 * moved, -1.0)
    tail = jnp.where(row == 0, 1.0 - square, 0.0)
    high, mid, low = parts(jnp.concatenate([head, tail], axis=0))
    return jnp.concatenate([high, mid, low, high, mid, high], axis=0).T.astype(BF16)


def pair_weight(target, source):
    near = jnp.maximum(jnp.dot(target, source, preferred_element_type=F32), 0.0)
    weight = near * near * near
    high = weight.astype(BF16)
    return high, (weight - high.astype(F32)).astype(BF16)


def contract(weights, rows):
    return lax.dot_general(weights, rows, (((1,), (1,)), ((), ())), preferred_element_type=F32)


def pack_kernel(rows_ref, packed_ref, keep_ref):
    for z in range(2):
        packed_ref[z] = jnp.concatenate([rows_ref[c, z : z + 1, :] for c in range(4)], axis=0)
        keep_ref[z] = jnp.broadcast_to(rows_ref[4, z : z + 1, :], keep_ref.shape[1:])


def ahead(axis):
    return 1 - 2 * lax.rem(lax.axis_index(axis), 2)


def y_shifts(size):
    if size == 2:
        return [[0], [-1, 1]]
    return [[0], [ahead("gy")], [-ahead("gy")]]


def list_chunk(list_ref, chunk):
    return jnp.concatenate([list_ref[2 * chunk], list_ref[2 * chunk + 1]], axis=1)[0:4]


def fill(near_ref, sum_ref, list_ref, entries):
    half = list_ref.shape[-1]
    lane = lax.broadcasted_iota(jnp.int32, (8, half), 1)
    list_ref[...] = jnp.zeros_like(list_ref)
    place = jnp.int32(0)
    held = {}
    for number, (ref, index, offset) in enumerate(entries):
        packed = ref[index]
        head, tail = shifted(packed[:, :half], offset), shifted(packed[:, half:], offset)
        if number == len(entries) - 1 and number % 2 == 0:
            list_ref[0] = jnp.concatenate([head, jnp.zeros_like(head)], axis=0)
        else:
            distance, summed = source_rows(head)
            near_ref[:, number * half : (number + 1) * half] = distance
            sum_ref[:, number * half : (number + 1) * half] = summed
        held[number] = tail
    if len(entries) % 2:
        place = place + half
    known = {}
    tile_rows = jnp.zeros((8, half), F32)
    for number, (ref, index, offset) in enumerate(entries):
        tail = held[number]
        key = (id(ref),) + (index if isinstance(index, tuple) else (index,))
        if key not in known:
            present = jnp.where(tail[3:4] != 0.0, lane[0:1] + 1, 0).astype(F32)
            known[key] = jnp.max(present).astype(jnp.int32)
        length = known[key]
        tile, turn = lax.div(place, half), lax.rem(place, half)
        tail = jnp.where(lane < length, jnp.concatenate([tail, jnp.zeros_like(tail)], axis=0), 0.0)
        tail = pltpu.roll(tail, turn, 1)
        upto = tile_rows + jnp.where(lane >= turn, tail, 0.0)
        list_ref[tile] = upto
        place = place + length
        tile_rows = jnp.where(turn + length >= half, jnp.where(lane < turn, tail, 0.0), upto)
    list_ref[lax.div(place, half)] = tile_rows
    done = (len(entries) // 2) * 2 * half
    for chunk in range((near_ref.shape[1] - done) // (2 * half)):
        distance, summed = source_rows(list_chunk(list_ref, chunk))
        near_ref[:, done + chunk * 2 * half : done + (chunk + 1) * 2 * half] = distance
        sum_ref[:, done + chunk * 2 * half : done + (chunk + 1) * 2 * half] = summed
    return place


def gathered(target, nears, sums):
    highs, lows = [], []
    for near in nears:
        high, low = pair_weight(target, near)
        highs.append(high)
        lows.append(low)
    rows = jnp.concatenate(sums, axis=1)
    return contract(jnp.concatenate(highs + lows, axis=1), jnp.concatenate([rows, rows], axis=1))


def sums_over(targets, totals, near_ref, sum_ref, list_ref, length, sources, tiles):
    wide = 2 * list_ref.shape[-1]
    steps = near_ref.shape[1] // (tiles * wide)

    def step(number, totals):
        nears, sums = [], []
        for tile in range(tiles):
            lanes = pl.ds(pl.multiple_of((number * tiles + tile) * wide, wide), wide)
            nears.append(near_ref[:, lanes])
            sums.append(sum_ref[:, lanes])
        return tuple(total + gathered(target, nears, sums) for target, total in zip(targets, totals))

    totals = step(0, totals) if steps == 1 else lax.fori_loop(0, steps, step, tuple(totals))
    done = steps * tiles - sources // 2

    def rest(number, totals):
        near, summed = source_rows(list_chunk(list_ref, number))
        return tuple(total + gathered(target, [near], [summed]) for target, total in zip(targets, totals))

    return lax.fori_loop(done, jnp.maximum(lax.div(length + (wide - 1), wide), done), rest, tuple(totals))


def pair_kernel(own_ref, near_x_ref, target_ref, total_ref, near_ref, sum_ref, list_ref):
    for z in range(2):
        target_ref[z] = target_rows(shifted(own_ref[z], (0, 0, z)))
    entries = [(own_ref, z, (0, 0, z)) for z in range(2)] + [(near_x_ref, z, (ahead("gx"), 0, z)) for z in range(2)]
    length = fill(near_ref, sum_ref, list_ref, entries)
    zero = jnp.zeros(total_ref.shape[1:], F32)
    targets = [target_ref[z] for z in range(2)]
    totals = sums_over(targets, (zero, zero), near_ref, sum_ref, list_ref, length, len(entries), 3)
    for z in range(2):
        total_ref[z] = totals[z]


def slab_kernel(size_y, target_ref, before_ref, *refs):
    others, (total_ref, near_ref, sum_ref, list_ref) = refs[:-4], refs[-4:]
    planes = len(others) // 2
    far_ref = others[planes]
    entries = [(far_ref, (0, z), (-ahead("gx"), 0, z)) for z in range(2)]
    for plane, shifts in enumerate(y_shifts(size_y)[1:]):
        for y in shifts:
            for z in range(2):
                entries.append((others[plane], (0, z), (0, y, z)))
                entries.append((others[plane], (1, z), (ahead("gx"), y, z)))
                entries.append((others[planes + 1 + plane], z, (-ahead("gx"), y, z)))
    length = fill(near_ref, sum_ref, list_ref, entries)
    targets = [target_ref[z] for z in range(2)]
    totals = sums_over(targets, (before_ref[0], before_ref[1]), near_ref, sum_ref, list_ref, length, len(entries), 10)
    for z in range(2):
        total_ref[z] = totals[z]


def complete(size_y, first, z, speed_ref, own_ref, target_ref, before_ref, source_ref, near_ref, sum_ref, list_ref):
    entries = []
    for column, x in enumerate((0, ahead("gx"), -ahead("gx"))):
        for plane, shifts in enumerate(y_shifts(size_y)):
            planes = len(y_shifts(size_y))
            index = 2 * plane + column if column < 2 else 2 * planes + plane
            entries += [(source_ref, index, (x, y, 3 * z - 1)) for y in shifts]
    length = fill(near_ref, sum_ref, list_ref, entries)
    (total,) = sums_over([target_ref[z]], (before_ref[z],), near_ref, sum_ref, list_ref, length, len(entries), 7)
    total = total.T
    total = (total[0:8] + total[8:16] + total[16:24])[0:4]
    own = own_ref[z]
    accel = total - shifted(own, (0, 0, z)) * total[3:4]
    if first:
        rows = [jnp.where(z == 1, speed_ref[c, 0, 0, 1:2, :], speed_ref[c, 0, 0, 0:1, :]) for c in range(3)]
        speed = jnp.concatenate(rows + [jnp.zeros_like(rows[0])], axis=0)
    else:
        speed = speed_ref[z]
    speed = speed + time_step * accel
    place = jnp.clip(own + time_step * speed, 0.0, 1.0)
    return jnp.where(row_index(*own.shape) < 3, place, own), speed


def near_side():
    return (1 + ahead("gz")) // 2


def near_kernel(size_y, first, speed_ref, own_ref, target_ref, before_ref, source_ref, bin_ref, near_ref, sum_ref, list_ref):
    place, speed = complete(
        size_y, first, near_side(), speed_ref, own_ref, target_ref, before_ref, source_ref, near_ref, sum_ref, list_ref
    )
    bin_ref[0] = place
    bin_ref[1] = speed


def far_kernel(size_y, first, last, keep_ref, bin_ref, speed_ref, own_ref, target_ref, before_ref, source_ref, place_out, speed_out, near_ref, sum_ref, list_ref):
    other = near_side()
    z = 1 - other
    place, speed = complete(
        size_y, first, z, speed_ref, own_ref, target_ref, before_ref, source_ref, near_ref, sum_ref, list_ref
    )
    if not last:
        place_out[z] = place
        speed_out[z] = speed
        place_out[other] = bin_ref[0]
        speed_out[other] = bin_ref[1]
        return
    for side in range(2):
        keep = keep_ref[side, 0:1] > 0.0
        moved = jnp.where(z == side, place, bin_ref[0])
        kicked = jnp.where(z == side, speed, bin_ref[1])
        for c in range(3):
            place_out[c, 0, 0, side : side + 1, :] = jnp.where(keep, moved[c : c + 1], 0.0)
            speed_out[c, 0, 0, side : side + 1, :] = jnp.where(keep, kicked[c : c + 1], 0.0)


VMEM = pl.BlockSpec(memory_space=pltpu.VMEM)


def swaps(axis):
    size = lax.axis_size(axis)
    near = [(i, i ^ 1) for i in range(size)]
    far = [(i, (((i + 1) ^ 1) - 1) % size) for i in range(size)]
    return near, far


def across(value, path_x, path_y):
    size_y = lax.axis_size("gy")
    pairs = [(x * size_y + y, to_x * size_y + to_y) for x, to_x in path_x for y, to_y in path_y]
    return lax.ppermute(value, ("gx", "gy"), pairs)


def call(kernel, inputs, outputs, sources, targets, slots, chunks):
    half = slots // 2
    heads = sources // 2 * 2
    return pl.pallas_call(
        kernel,
        out_shape=outputs,
        in_specs=[VMEM] * len(inputs),
        out_specs=tuple(VMEM for _ in outputs),
        scratch_shapes=[
            pltpu.VMEM((48, heads * half + chunks * slots), BF16),
            pltpu.VMEM((32, heads * half + chunks * slots), BF16),
            pltpu.VMEM((heads + 4, 8, half), F32),
        ],
        compiler_params=pltpu.CompilerParams(vmem_limit_bytes=24 * 1024 * 1024),
        cost_estimate=pl.CostEstimate(flops=sources * targets * slots * slots * 1000, bytes_accessed=1 << 18, transcendentals=0),
    )(*inputs)


def on_device(positions, velocities, mass, counts):
    slots = positions.shape[-1]
    size_y = lax.axis_size("gy")
    bins = jax.ShapeDtypeStruct((2, 4, slots), F32)
    full = jax.ShapeDtypeStruct(positions.shape, F32)
    running = jax.ShapeDtypeStruct((2, slots, 32), F32)
    present = lax.broadcasted_iota(jnp.int32, mass.shape, 3) < counts[..., None]
    rows = [positions, jnp.where(present, mass, 0.0)[None], jnp.where(present, 1.0, 0.0).astype(F32)[None]]
    packed, keep = pl.pallas_call(
        pack_kernel,
        out_shape=(bins, bins),
        in_specs=[VMEM],
        out_specs=(VMEM, VMEM),
        compiler_params=pltpu.CompilerParams(vmem_limit_bytes=8 * 1024 * 1024),
    )(jnp.concatenate(rows, axis=0).reshape(5, 2, slots))
    speed = velocities
    upper = lax.rem(lax.axis_index("gz"), 2)
    for subcycle in range(SUBCYCLES):
        first, last = subcycle == 0, subcycle == SUBCYCLES - 1
        paths = swaps("gy")[: min(size_y, 3) - 1]
        near, far = swaps("gx")
        near_x = lax.ppermute(packed, "gx", near)
        corners = [across(packed, far, path) for path in paths]
        pair = jnp.stack([packed, near_x])
        along_y = [lax.ppermute(pair, "gy", path) for path in paths]
        far_x = lax.ppermute(pair, "gx", far)
        targets, total = call(
            pair_kernel,
            [packed, near_x],
            (jax.ShapeDtypeStruct((2, slots, 48), BF16), running),
            4, 2, slots, 1,
        )
        slab = jnp.concatenate([pair] + along_y + [far_x[:1]] + [value[None] for value in corners], axis=0)
        near, far = swaps("gz")
        far_z = lax.ppermute(lax.dynamic_index_in_dim(slab, upper, 1, False), "gz", far)
        near_z = lax.ppermute(lax.dynamic_index_in_dim(slab, 1 - upper, 1, False), "gz", near)
        (total,) = call(
            functools.partial(slab_kernel, size_y),
            [targets, total] + along_y + [far_x] + corners,
            (running,),
            14, 2, slots, 3,
        )
        state = [speed, packed, targets, total]
        (half_done,) = call(
            functools.partial(near_kernel, size_y, first),
            state + [near_z],
            (bins,),
            9, 1, slots, 3,
        )
        packed, speed = call(
            functools.partial(far_kernel, size_y, first, last),
            [keep, half_done] + state + [far_z],
            (full, full) if last else (bins, bins),
            9, 1, slots, 3,
        )
    return packed, speed


def solution(mesh):
    placed = (
        P(None, "gx", "gy", "gz", None),
        P(None, "gx", "gy", "gz", None),
        P("gx", "gy", "gz", None),
        P("gx", "gy", "gz"),
    )
    return jax.shard_map(
        on_device,
        mesh=mesh,
        in_specs=placed,
        out_specs=(P(None, "gx", "gy", "gz", None), P(None, "gx", "gy", "gz", None)),
        check_vma=False,
    )
```

```python
import functools

import jax
import jax.numpy as jnp
from jax import lax
from jax.experimental import pallas as pl
from jax.experimental.pallas import tpu as pltpu
from jax.sharding import PartitionSpec as P

SUBCYCLES = 2

time_step = 0.25

CENTRE = (0.5, 0.5, 1.0)
F32, BF16 = jnp.float32, jnp.bfloat16


def parts(value):
    high = value.astype(BF16).astype(F32)
    rest = value - high
    mid = rest.astype(BF16).astype(F32)
    return high, mid, rest - mid


def row_index(rows, slots):
    return lax.broadcasted_iota(jnp.int32, (rows, slots), 0)


def shifted(packed, offset):
    row = row_index(*packed.shape)
    x, y, z = [jnp.asarray(o, F32) - c for o, c in zip(offset, CENTRE)]
    move = jnp.where(row == 0, x, jnp.where(row == 1, y, jnp.where(row == 2, z, 0.0)))
    return packed + move


def source_rows(moved):
    row = row_index(*moved.shape)
    square = jnp.sum(jnp.where(row < 3, moved * moved, 0.0), axis=0, keepdims=True)
    head = jnp.where(row < 3, moved, square)
    tail = jnp.where(row == 0, 1.0, 0.0).astype(F32)
    high, mid, low = parts(jnp.concatenate([head, tail], axis=0))
    distance = jnp.concatenate([high, high, high, mid, mid, low], axis=0).astype(BF16)
    mass = moved[3:4]
    carried = jnp.where(row < 3, moved * mass, mass)
    high, mid, low = parts(jnp.concatenate([carried, jnp.zeros_like(carried)], axis=0))
    summed = jnp.concatenate([high, mid, low, jnp.zeros_like(low)], axis=0).astype(BF16)
    return distance, summed


def target_rows(moved):
    slots = moved.shape[-1]
    row = row_index(4, slots)
    square = jnp.sum(jnp.where(row < 3, moved * moved, 0.0), axis=0, keepdims=True)
    head = jnp.where(row < 3, 2.0 * moved, -1.0)
    tail = jnp.where(row == 0, 1.0 - square, 0.0)
    high, mid, low = parts(jnp.concatenate([head, tail], axis=0))
    return jnp.concatenate([high, mid, low, high, mid, high], axis=0).T.astype(BF16)


def pair_weight(target, source):
    near = jnp.maximum(jnp.dot(target, source, preferred_element_type=F32), 0.0)
    weight = near * near * near
    high = weight.astype(BF16)
    return high, (weight - high.astype(F32)).astype(BF16)


def contract(weights, rows):
    return lax.dot_general(weights, rows, (((1,), (1,)), ((), ())), preferred_element_type=F32)


def pack_kernel(rows_ref, packed_ref, keep_ref):
    for z in range(2):
        packed_ref[z] = jnp.concatenate([rows_ref[c, z : z + 1, :] for c in range(4)], axis=0)
        keep_ref[z] = jnp.broadcast_to(rows_ref[4, z : z + 1, :], keep_ref.shape[1:])


def ahead(axis):
    return 1 - 2 * lax.rem(lax.axis_index(axis), 2)


def y_shifts(size):
    if size == 2:
        return [[0], [-1, 1]]
    return [[0], [ahead("gy")], [-ahead("gy")]]


def list_chunk(list_ref, chunk):
    return jnp.concatenate([list_ref[2 * chunk], list_ref[2 * chunk + 1]], axis=1)[0:4]


def fill(list_ref, entries, chunks):
    half = list_ref.shape[-1]
    lane = lax.broadcasted_iota(jnp.int32, (8, half), 1)
    list_ref[...] = jnp.zeros_like(list_ref)
    place = jnp.int32(0)
    held = {}
    heads = []
    for number, (ref, index, offset) in enumerate(entries):
        packed = ref[index]
        head, tail = shifted(packed[:, :half], offset), shifted(packed[:, half:], offset)
        if number == len(entries) - 1 and number % 2 == 0:
            list_ref[0] = jnp.concatenate([head, jnp.zeros_like(head)], axis=0)
        else:
            heads.append(head)
        held[number] = tail
    if len(entries) % 2:
        place = place + half
    known = {}
    tile_rows = jnp.zeros((8, half), F32)
    for number, (ref, index, offset) in enumerate(entries):
        tail = held[number]
        key = (id(ref),) + (index if isinstance(index, tuple) else (index,))
        if key not in known:
            present = jnp.where(tail[3:4] != 0.0, lane[0:1] + 1, 0).astype(F32)
            known[key] = jnp.max(present).astype(jnp.int32)
        length = known[key]
        tile, turn = lax.div(place, half), lax.rem(place, half)
        tail = jnp.where(lane < length, jnp.concatenate([tail, jnp.zeros_like(tail)], axis=0), 0.0)
        tail = pltpu.roll(tail, turn, 1)
        upto = tile_rows + jnp.where(lane >= turn, tail, 0.0)
        list_ref[tile] = upto
        place = place + length
        tile_rows = jnp.where(turn + length >= half, jnp.where(lane < turn, tail, 0.0), upto)
    list_ref[lax.div(place, half)] = tile_rows
    first = [source_rows(jnp.concatenate(heads[at : at + 2], axis=1)) for at in range(0, len(heads), 2)]
    packed = [source_rows(list_chunk(list_ref, chunk)) for chunk in range(chunks)]
    return first, packed, place


def gathered(target, sources):
    weights, rows = [], []
    for near, summed in sources:
        weights += pair_weight(target, near)
        rows += [summed, summed]
    return contract(jnp.concatenate(weights, axis=1), jnp.concatenate(rows, axis=1))


def sums_over(targets, totals, list_ref, entries, chunks):
    wide = 2 * list_ref.shape[-1]
    first, packed, length = fill(list_ref, entries, chunks)
    totals = [total + gathered(target, first) for target, total in zip(targets, totals)]
    totals = tuple(total + gathered(target, packed) for target, total in zip(targets, totals))

    def rest(number, totals):
        sources = [source_rows(list_chunk(list_ref, number))]
        return tuple(total + gathered(target, sources) for target, total in zip(targets, totals))

    return lax.fori_loop(chunks, jnp.maximum(lax.div(length + (wide - 1), wide), chunks), rest, totals)


def plane_kernel(size_y, *refs):
    planes, (target_ref, total_ref, list_ref) = refs[:-3], refs[-3:]
    own_ref = planes[0]
    for z in range(2):
        target_ref[z] = target_rows(shifted(own_ref[z], (0, 0, z)))
    entries = []
    for ref, shifts in zip(planes, y_shifts(size_y)):
        for y in shifts:
            entries += [(ref, z, (0, y, z)) for z in range(2)]
    zero = jnp.zeros(total_ref.shape[1:], F32)
    targets = [target_ref[z] for z in range(2)]
    totals = sums_over(targets, (zero, zero), list_ref, entries, 2)
    for z in range(2):
        total_ref[z] = totals[z]


def slab_kernel(size_y, target_ref, before_ref, near_x_ref, *refs):
    far_refs, (total_ref, list_ref) = refs[:-2], refs[-2:]
    entries = []
    for plane, shifts in enumerate(y_shifts(size_y)):
        for y in shifts:
            entries += [(near_x_ref, (plane, z), (ahead("gx"), y, z)) for z in range(2)]
            entries += [(far_refs[plane - 1], z, (-ahead("gx"), y, z)) for z in range(2)]
    targets = [target_ref[z] for z in range(2)]
    totals = sums_over(targets, (before_ref[0], before_ref[1]), list_ref, entries, 3)
    for z in range(2):
        total_ref[z] = totals[z]


def complete(size_y, first, z, speed_ref, own_ref, target_ref, before_ref, source_ref, list_ref):
    entries = []
    for column, x in enumerate((0, ahead("gx"), -ahead("gx"))):
        for plane, shifts in enumerate(y_shifts(size_y)):
            planes = len(y_shifts(size_y))
            index = column * planes + (plane if column < 2 else (plane - 1) % planes)
            entries += [(source_ref, index, (x, y, 3 * z - 1)) for y in shifts]
    (total,) = sums_over([target_ref[z]], (before_ref[z],), list_ref, entries, 3)
    total = total.T
    total = (total[0:8] + total[8:16] + total[16:24])[0:4]
    own = own_ref[z]
    accel = total - shifted(own, (0, 0, z)) * total[3:4]
    if first:
        rows = [jnp.where(z == 1, speed_ref[c, 0, 0, 1:2, :], speed_ref[c, 0, 0, 0:1, :]) for c in range(3)]
        speed = jnp.concatenate(rows + [jnp.zeros_like(rows[0])], axis=0)
    else:
        speed = speed_ref[z]
    speed = speed + time_step * accel
    place = jnp.clip(own + time_step * speed, 0.0, 1.0)
    return jnp.where(row_index(*own.shape) < 3, place, own), speed


def near_side():
    return (1 + ahead("gz")) // 2


def near_kernel(size_y, first, speed_ref, own_ref, target_ref, before_ref, source_ref, bin_ref, list_ref):
    place, speed = complete(
        size_y, first, near_side(), speed_ref, own_ref, target_ref, before_ref, source_ref, list_ref
    )
    bin_ref[0] = place
    bin_ref[1] = speed


def far_kernel(size_y, first, last, keep_ref, bin_ref, speed_ref, own_ref, target_ref, before_ref, source_ref, place_out, speed_out, list_ref):
    other = near_side()
    z = 1 - other
    place, speed = complete(
        size_y, first, z, speed_ref, own_ref, target_ref, before_ref, source_ref, list_ref
    )
    if not last:
        place_out[z] = place
        speed_out[z] = speed
        place_out[other] = bin_ref[0]
        speed_out[other] = bin_ref[1]
        return
    for side in range(2):
        keep = keep_ref[side, 0:1] > 0.0
        moved = jnp.where(z == side, place, bin_ref[0])
        kicked = jnp.where(z == side, speed, bin_ref[1])
        for c in range(3):
            place_out[c, 0, 0, side : side + 1, :] = jnp.where(keep, moved[c : c + 1], 0.0)
            speed_out[c, 0, 0, side : side + 1, :] = jnp.where(keep, kicked[c : c + 1], 0.0)


VMEM = pl.BlockSpec(memory_space=pltpu.VMEM)


def swaps(axis):
    size = lax.axis_size(axis)
    near = [(i, i ^ 1) for i in range(size)]
    far = [(i, (((i + 1) ^ 1) - 1) % size) for i in range(size)]
    return near, far


def across(value, path_x, path_y):
    size_y = lax.axis_size("gy")
    pairs = [(x * size_y + y, to_x * size_y + to_y) for x, to_x in path_x for y, to_y in path_y]
    return lax.ppermute(value, ("gx", "gy"), pairs)


def call(kernel, inputs, outputs, sources, targets, slots):
    half = slots // 2
    heads = sources // 2 * 2
    return pl.pallas_call(
        kernel,
        out_shape=outputs,
        in_specs=[VMEM] * len(inputs),
        out_specs=tuple(VMEM for _ in outputs),
        scratch_shapes=[
            pltpu.VMEM((heads + 4, 8, half), F32),
        ],
        compiler_params=pltpu.CompilerParams(vmem_limit_bytes=24 * 1024 * 1024),
        cost_estimate=pl.CostEstimate(flops=sources * targets * slots * slots * 1000, bytes_accessed=1 << 18, transcendentals=0),
    )(*inputs)


def on_device(positions, velocities, mass, counts):
    slots = positions.shape[-1]
    size_y = lax.axis_size("gy")
    bins = jax.ShapeDtypeStruct((2, 4, slots), F32)
    full = jax.ShapeDtypeStruct(positions.shape, F32)
    running = jax.ShapeDtypeStruct((2, slots, 32), F32)
    present = lax.broadcasted_iota(jnp.int32, mass.shape, 3) < counts[..., None]
    rows = [positions, jnp.where(present, mass, 0.0)[None], jnp.where(present, 1.0, 0.0).astype(F32)[None]]
    packed, keep = pl.pallas_call(
        pack_kernel,
        out_shape=(bins, bins),
        in_specs=[VMEM],
        out_specs=(VMEM, VMEM),
        compiler_params=pltpu.CompilerParams(vmem_limit_bytes=8 * 1024 * 1024),
    )(jnp.concatenate(rows, axis=0).reshape(5, 2, slots))
    speed = velocities
    upper = lax.rem(lax.axis_index("gz"), 2)
    for subcycle in range(SUBCYCLES):
        first, last = subcycle == 0, subcycle == SUBCYCLES - 1
        paths = swaps("gy")[: min(size_y, 3) - 1]
        planes = [packed] + [lax.ppermute(packed, "gy", path) for path in paths]
        near, far = swaps("gx")
        far_planes = [across(packed, far, path) for path in paths] + [lax.ppermute(packed, "gx", far)]
        plane = jnp.stack(planes)
        near_x = lax.ppermute(plane, "gx", near)
        targets, total = call(
            functools.partial(plane_kernel, size_y),
            planes,
            (jax.ShapeDtypeStruct((2, slots, 48), BF16), running),
            6, 2, slots,
        )
        slab = jnp.concatenate([plane, near_x] + [value[None] for value in far_planes], axis=0)
        near, far = swaps("gz")
        far_z = lax.ppermute(lax.dynamic_index_in_dim(slab, upper, 1, False), "gz", far)
        near_z = lax.ppermute(lax.dynamic_index_in_dim(slab, 1 - upper, 1, False), "gz", near)
        (total,) = call(
            functools.partial(slab_kernel, size_y),
            [targets, total, near_x] + far_planes,
            (running,),
            12, 2, slots,
        )
        state = [speed, packed, targets, total]
        (half_done,) = call(
            functools.partial(near_kernel, size_y, first),
            state + [near_z],
            (bins,),
            9, 1, slots,
        )
        packed, speed = call(
            functools.partial(far_kernel, size_y, first, last),
            [keep, half_done] + state + [far_z],
            (full, full) if last else (bins, bins),
            9, 1, slots,
        )
    return packed, speed


def solution(mesh):
    placed = (
        P(None, "gx", "gy", "gz", None),
        P(None, "gx", "gy", "gz", None),
        P("gx", "gy", "gz", None),
        P("gx", "gy", "gz"),
    )
    return jax.shard_map(
        on_device,
        mesh=mesh,
        in_specs=placed,
        out_specs=(P(None, "gx", "gy", "gz", None), P(None, "gx", "gy", "gz", None)),
        check_vma=False,
    )
```

```python
import functools

import jax
import jax.numpy as jnp
from jax import lax
from jax.experimental import pallas as pl
from jax.experimental.pallas import tpu as pltpu
from jax.sharding import PartitionSpec as P

SUBCYCLES = 2

time_step = 0.25

CENTRE = (0.5, 0.5, 1.0)
F32, BF16 = jnp.float32, jnp.bfloat16


def parts(value):
    high = value.astype(BF16).astype(F32)
    rest = value - high
    mid = rest.astype(BF16).astype(F32)
    return high, mid, rest - mid


def row_index(rows, slots):
    return lax.broadcasted_iota(jnp.int32, (rows, slots), 0)


def shifted(packed, offset):
    row = row_index(*packed.shape)
    x, y, z = [jnp.asarray(o, F32) - c for o, c in zip(offset, CENTRE)]
    move = jnp.where(row == 0, x, jnp.where(row == 1, y, jnp.where(row == 2, z, 0.0)))
    return packed + move


def source_rows(moved):
    row = row_index(*moved.shape)
    square = jnp.sum(jnp.where(row < 3, moved * moved, 0.0), axis=0, keepdims=True)
    head = jnp.where(row < 3, moved, square)
    tail = jnp.where(row == 0, 1.0, 0.0).astype(F32)
    high, mid, low = parts(jnp.concatenate([head, tail], axis=0))
    distance = jnp.concatenate([high, high, high, mid, mid, low], axis=0).astype(BF16)
    mass = moved[3:4]
    carried = jnp.where(row < 3, moved * mass, mass)
    high, mid, low = parts(jnp.concatenate([carried, jnp.zeros_like(carried)], axis=0))
    summed = jnp.concatenate([high, mid, low, jnp.zeros_like(low)], axis=0).astype(BF16)
    return distance, summed


def target_rows(moved):
    slots = moved.shape[-1]
    row = row_index(4, slots)
    square = jnp.sum(jnp.where(row < 3, moved * moved, 0.0), axis=0, keepdims=True)
    head = jnp.where(row < 3, 2.0 * moved, -1.0)
    tail = jnp.where(row == 0, 1.0 - square, 0.0)
    high, mid, low = parts(jnp.concatenate([head, tail], axis=0))
    return jnp.concatenate([high, mid, low, high, mid, high], axis=0).T.astype(BF16)


def pair_weight(target, source):
    near = jnp.maximum(jnp.dot(target, source, preferred_element_type=F32), 0.0)
    weight = near * near * near
    high = weight.astype(BF16)
    return high, (weight - high.astype(F32)).astype(BF16)


def contract(weights, rows):
    return lax.dot_general(weights, rows, (((1,), (1,)), ((), ())), preferred_element_type=F32)


def pack_kernel(rows_ref, packed_ref, keep_ref):
    for z in range(2):
        packed_ref[z] = jnp.concatenate([rows_ref[c, z : z + 1, :] for c in range(4)], axis=0)
        keep_ref[z] = jnp.broadcast_to(rows_ref[4, z : z + 1, :], keep_ref.shape[1:])


def ahead(axis):
    return 1 - 2 * lax.rem(lax.axis_index(axis), 2)


def y_shifts(size):
    if size == 2:
        return [[0], [-1, 1]]
    return [[0], [ahead("gy")], [-ahead("gy")]]


def list_chunk(list_ref, chunk):
    return jnp.concatenate([list_ref[2 * chunk], list_ref[2 * chunk + 1]], axis=1)[0:4]


def fill(list_ref, entries, chunks):
    half = list_ref.shape[-1]
    lane = lax.broadcasted_iota(jnp.int32, (8, half), 1)
    list_ref[...] = jnp.zeros_like(list_ref)
    place = jnp.int32(0)
    held = {}
    heads = []
    for number, (ref, index, offset) in enumerate(entries):
        packed = ref[index]
        head, tail = shifted(packed[:, :half], offset), shifted(packed[:, half:], offset)
        if number == len(entries) - 1 and number % 2 == 0:
            list_ref[0] = jnp.concatenate([head, jnp.zeros_like(head)], axis=0)
        else:
            heads.append(head)
        held[number] = tail
    if len(entries) % 2:
        place = place + half
    known = {}
    tile_rows = jnp.zeros((8, half), F32)
    for number, (ref, index, offset) in enumerate(entries):
        tail = held[number]
        key = (id(ref),) + (index if isinstance(index, tuple) else (index,))
        if key not in known:
            present = jnp.where(tail[3:4] != 0.0, lane[0:1] + 1, 0).astype(F32)
            known[key] = jnp.max(present).astype(jnp.int32)
        length = known[key]
        tile, turn = lax.div(place, half), lax.rem(place, half)
        tail = jnp.where(lane < length, jnp.concatenate([tail, jnp.zeros_like(tail)], axis=0), 0.0)
        tail = pltpu.roll(tail, turn, 1)
        upto = tile_rows + jnp.where(lane >= turn, tail, 0.0)
        list_ref[tile] = upto
        place = place + length
        tile_rows = jnp.where(turn + length >= half, jnp.where(lane < turn, tail, 0.0), upto)
    list_ref[lax.div(place, half)] = tile_rows
    first = [source_rows(jnp.concatenate(heads[at : at + 2], axis=1)) for at in range(0, len(heads), 2)]
    packed = [source_rows(list_chunk(list_ref, chunk)) for chunk in range(chunks)]
    return first, packed, place


def gathered(target, sources):
    weights, rows = [], []
    for near, summed in sources:
        weights += pair_weight(target, near)
        rows += [summed, summed]
    return contract(jnp.concatenate(weights, axis=1), jnp.concatenate(rows, axis=1))


def sums_over(targets, totals, list_ref, entries, chunks):
    wide = 2 * list_ref.shape[-1]
    first, packed, length = fill(list_ref, entries, chunks)
    totals = tuple(total + gathered(target, first + packed) for target, total in zip(targets, totals))

    def rest(number, totals):
        sources = [source_rows(list_chunk(list_ref, number))]
        return tuple(total + gathered(target, sources) for target, total in zip(targets, totals))

    return lax.fori_loop(chunks, jnp.maximum(lax.div(length + (wide - 1), wide), chunks), rest, totals)


def plane_kernel(size_y, *refs):
    planes, (target_ref, total_ref, list_ref) = refs[:-3], refs[-3:]
    own_ref = planes[0]
    for z in range(2):
        target_ref[z] = target_rows(shifted(own_ref[z], (0, 0, z)))
    entries = []
    for ref, shifts in zip(planes, y_shifts(size_y)):
        for y in shifts:
            entries += [(ref, z, (0, y, z)) for z in range(2)]
    zero = jnp.zeros(total_ref.shape[1:], F32)
    targets = [target_ref[z] for z in range(2)]
    totals = sums_over(targets, (zero, zero), list_ref, entries, 2)
    for z in range(2):
        total_ref[z] = totals[z]


def slab_kernel(size_y, target_ref, before_ref, near_x_ref, *refs):
    far_refs, (total_ref, list_ref) = refs[:-2], refs[-2:]
    entries = []
    for plane, shifts in enumerate(y_shifts(size_y)):
        for y in shifts:
            entries += [(near_x_ref, (plane, z), (ahead("gx"), y, z)) for z in range(2)]
            entries += [(far_refs[plane - 1], z, (-ahead("gx"), y, z)) for z in range(2)]
    targets = [target_ref[z] for z in range(2)]
    totals = sums_over(targets, (before_ref[0], before_ref[1]), list_ref, entries, 3)
    for z in range(2):
        total_ref[z] = totals[z]


def complete(size_y, first, z, speed_ref, own_ref, target_ref, before_ref, source_ref, list_ref):
    entries = []
    for column, x in enumerate((0, ahead("gx"), -ahead("gx"))):
        for plane, shifts in enumerate(y_shifts(size_y)):
            planes = len(y_shifts(size_y))
            index = column * planes + (plane if column < 2 else (plane - 1) % planes)
            entries += [(source_ref, index, (x, y, 3 * z - 1)) for y in shifts]
    (total,) = sums_over([target_ref[z]], (before_ref[z],), list_ref, entries, 3)
    total = total.T
    total = (total[0:8] + total[8:16] + total[16:24])[0:4]
    own = own_ref[z]
    accel = total - shifted(own, (0, 0, z)) * total[3:4]
    if first:
        rows = [jnp.where(z == 1, speed_ref[c, 0, 0, 1:2, :], speed_ref[c, 0, 0, 0:1, :]) for c in range(3)]
        speed = jnp.concatenate(rows + [jnp.zeros_like(rows[0])], axis=0)
    else:
        speed = speed_ref[z]
    speed = speed + time_step * accel
    place = jnp.clip(own + time_step * speed, 0.0, 1.0)
    return jnp.where(row_index(*own.shape) < 3, place, own), speed


def near_side():
    return (1 + ahead("gz")) // 2


def near_kernel(size_y, first, speed_ref, own_ref, target_ref, before_ref, source_ref, bin_ref, list_ref):
    place, speed = complete(
        size_y, first, near_side(), speed_ref, own_ref, target_ref, before_ref, source_ref, list_ref
    )
    bin_ref[0] = place
    bin_ref[1] = speed


def far_kernel(size_y, first, last, keep_ref, bin_ref, speed_ref, own_ref, target_ref, before_ref, source_ref, place_out, speed_out, list_ref):
    other = near_side()
    z = 1 - other
    place, speed = complete(
        size_y, first, z, speed_ref, own_ref, target_ref, before_ref, source_ref, list_ref
    )
    if not last:
        place_out[z] = place
        speed_out[z] = speed
        place_out[other] = bin_ref[0]
        speed_out[other] = bin_ref[1]
        return
    for side in range(2):
        keep = keep_ref[side, 0:1] > 0.0
        moved = jnp.where(z == side, place, bin_ref[0])
        kicked = jnp.where(z == side, speed, bin_ref[1])
        for c in range(3):
            place_out[c, 0, 0, side : side + 1, :] = jnp.where(keep, moved[c : c + 1], 0.0)
            speed_out[c, 0, 0, side : side + 1, :] = jnp.where(keep, kicked[c : c + 1], 0.0)


VMEM = pl.BlockSpec(memory_space=pltpu.VMEM)


def swaps(axis):
    size = lax.axis_size(axis)
    near = [(i, i ^ 1) for i in range(size)]
    far = [(i, (((i + 1) ^ 1) - 1) % size) for i in range(size)]
    return near, far


def across(value, path_x, path_y):
    size_y = lax.axis_size("gy")
    pairs = [(x * size_y + y, to_x * size_y + to_y) for x, to_x in path_x for y, to_y in path_y]
    return lax.ppermute(value, ("gx", "gy"), pairs)


def call(kernel, inputs, outputs, sources, targets, slots):
    half = slots // 2
    heads = sources // 2 * 2
    return pl.pallas_call(
        kernel,
        out_shape=outputs,
        in_specs=[VMEM] * len(inputs),
        out_specs=tuple(VMEM for _ in outputs),
        scratch_shapes=[
            pltpu.VMEM((heads + 4, 8, half), F32),
        ],
        compiler_params=pltpu.CompilerParams(vmem_limit_bytes=24 * 1024 * 1024),
        cost_estimate=pl.CostEstimate(flops=sources * targets * slots * slots * 1000, bytes_accessed=1 << 18, transcendentals=0),
    )(*inputs)


def on_device(positions, velocities, mass, counts):
    slots = positions.shape[-1]
    size_y = lax.axis_size("gy")
    bins = jax.ShapeDtypeStruct((2, 4, slots), F32)
    full = jax.ShapeDtypeStruct(positions.shape, F32)
    running = jax.ShapeDtypeStruct((2, slots, 32), F32)
    present = lax.broadcasted_iota(jnp.int32, mass.shape, 3) < counts[..., None]
    rows = [positions, jnp.where(present, mass, 0.0)[None], jnp.where(present, 1.0, 0.0).astype(F32)[None]]
    packed, keep = pl.pallas_call(
        pack_kernel,
        out_shape=(bins, bins),
        in_specs=[VMEM],
        out_specs=(VMEM, VMEM),
        compiler_params=pltpu.CompilerParams(vmem_limit_bytes=8 * 1024 * 1024),
    )(jnp.concatenate(rows, axis=0).reshape(5, 2, slots))
    speed = velocities
    upper = lax.rem(lax.axis_index("gz"), 2)
    for subcycle in range(SUBCYCLES):
        first, last = subcycle == 0, subcycle == SUBCYCLES - 1
        paths = swaps("gy")[: min(size_y, 3) - 1]
        planes = [packed] + [lax.ppermute(packed, "gy", path) for path in paths]
        near, far = swaps("gx")
        far_planes = [across(packed, far, path) for path in paths] + [lax.ppermute(packed, "gx", far)]
        plane = jnp.stack(planes)
        near_x = lax.ppermute(plane, "gx", near)
        targets, total = call(
            functools.partial(plane_kernel, size_y),
            planes,
            (jax.ShapeDtypeStruct((2, slots, 48), BF16), running),
            6, 2, slots,
        )
        slab = jnp.concatenate([plane, near_x] + [value[None] for value in far_planes], axis=0)
        near, far = swaps("gz")
        far_z = lax.ppermute(lax.dynamic_index_in_dim(slab, upper, 1, False), "gz", far)
        near_z = lax.ppermute(lax.dynamic_index_in_dim(slab, 1 - upper, 1, False), "gz", near)
        (total,) = call(
            functools.partial(slab_kernel, size_y),
            [targets, total, near_x] + far_planes,
            (running,),
            12, 2, slots,
        )
        state = [speed, packed, targets, total]
        (half_done,) = call(
            functools.partial(near_kernel, size_y, first),
            state + [near_z],
            (bins,),
            9, 1, slots,
        )
        packed, speed = call(
            functools.partial(far_kernel, size_y, first, last),
            [keep, half_done] + state + [far_z],
            (full, full) if last else (bins, bins),
            9, 1, slots,
        )
    return packed, speed


def solution(mesh):
    placed = (
        P(None, "gx", "gy", "gz", None),
        P(None, "gx", "gy", "gz", None),
        P("gx", "gy", "gz", None),
        P("gx", "gy", "gz"),
    )
    return jax.shard_map(
        on_device,
        mesh=mesh,
        in_specs=placed,
        out_specs=(P(None, "gx", "gy", "gz", None), P(None, "gx", "gy", "gz", None)),
        check_vma=False,
    )
```
